256 devices in a mesh: rep: 2 (over z_hi), shard: 128 (over y, z_lo, x, core).
Axes of the slice: x: 4, y: 4, z: 8 (z_hi: 2, z_lo: 4; z = z_hi * 4 + z_lo), core: 2. Of those that a mesh axis runs over, the one named last changes fastest.
Arguments:
- old_master: float32 [655360, 128], P('shard'), may hold values from -100 to 100
- old_first: float32 [655360, 128], P('shard'), may hold values from -6 to 6
- old_second: float32 [655360, 128], P('shard'), may hold values from 0 to 1, as said below
- grad_parts: float32 [2, 393216, 128], P('rep', 'shard'), may hold values from -6 to 6
- old_offsets: int32 [65], replicated, may hold values from 0 to 262144, as said below
- new_offsets: int32 [129], replicated, may hold values from 0 to 262144, as said below
Outputs:
- new_master: float32 [128, 2, 1536, 128], P('shard', 'rep')
- new_first: float32 [128, 2, 1536, 128], P('shard', 'rep')
- new_second: float32 [128, 2, 1536, 128], P('shard', 'rep')
- new_weights: bfloat16 [393216, 128], P('shard')
The draws below stay inside these ranges and needn't reach their ends.
Inputs may be any that keep to these rules, and one draw needn't show every extreme that they name: `old_offsets`: Rising; starts at 0 and ends at 262144; entry o lies within 512 of 2 * 2048 * o, and at least one old owner holds 5120 rows, the most that any can hold. Old owner o's rows are on shard index 2 * o; odd shard indices hold no old rows. `new_offsets`: Rising; starts at 0 and ends at 262144; entry i lies within 512 of 2048 * i, and at least one new owner holds 3072 rows, the most that any can hold. `old_second`: every entry is positive.
All inputs are finite; a program needn't handle non-finite values.
Results may differ from the reference program's by a relative error of at most 0.001.
Values may be sent and summed in bfloat16 or wider, within the bound.
A program may use at most 128 MiB of HBM per device.

```python
import math
import jax
import jax.numpy as jnp
from jax import lax

BLK = 2048
LANES = 128
STEP = 10
OWNERS = 64
OLD_CAP = 5120
NEW_CAP = 3072
ROWS = 262144
N_REP = 2
N_SHARD = 128


def draw_old_offsets(key, part):
    key = jax.random.fold_in(key, 3)
    quarter = BLK // 4
    index = jnp.arange(OWNERS + 1, dtype=jnp.int32)
    jitter = jax.random.randint(key, (OWNERS + 1,), -quarter, quarter + 1)
    jitter = jnp.where(index == 1, -quarter, jnp.where(index == 2, quarter, jitter))
    jitter = jnp.where((index == 0) | (index == OWNERS), 0, jitter)
    return (2 * BLK * index + jitter).astype(jnp.int32)


def draw_new_offsets(key, part):
    key = jax.random.fold_in(key, 5)
    quarter = BLK // 4
    index = jnp.arange(N_SHARD + 1, dtype=jnp.int32)
    jitter = jax.random.randint(key, (N_SHARD + 1,), -quarter, quarter + 1)
    jitter = jnp.where(index == 1, quarter, jnp.where(index == 2, -quarter, jnp.where(index == 3, quarter, jitter)))
    jitter = jnp.where((index == 0) | (index == N_SHARD), 0, jitter)
    return (BLK * index + jitter).astype(jnp.int32)


def old_rows(key, part):
    offsets = draw_old_offsets(key, part)
    slots = jnp.arange(N_SHARD * OLD_CAP, dtype=jnp.int32)
    device = slots // OLD_CAP
    owner = device // 2
    flat = (offsets[owner] + slots % OLD_CAP).astype(jnp.int32)
    live = (device % 2 == 0) & (flat < offsets[owner + 1])
    return jnp.where(live, flat, -1).astype(jnp.int32)


def new_rows(key, part):
    offsets = draw_new_offsets(key, part)
    slots = jnp.arange(N_SHARD * NEW_CAP, dtype=jnp.int32)
    holder = slots // NEW_CAP
    flat = (offsets[holder] + slots % NEW_CAP).astype(jnp.int32)
    live = flat < offsets[holder + 1]
    return jnp.where(live, flat, -1).astype(jnp.int32)


def flat_normal(key, salt, bound):
    return jax.random.truncated_normal(jax.random.fold_in(key, salt), -bound, bound, (ROWS, LANES), jnp.float32)


def flat_spread(key, salt, lowest, highest):
    unit = jax.random.uniform(jax.random.fold_in(key, salt), (ROWS, LANES), jnp.float32)
    return lowest * jnp.exp(unit * math.log(highest / lowest))


def arrange(rows, field, filler):
    return jnp.where((rows >= 0)[:, None], field[jnp.maximum(rows, 0)], filler)


def draw_old_master(key, part):
    private = jax.random.fold_in(key, 7)
    rows = old_rows(key, part)
    filler = jax.random.truncated_normal(private, -6.0, 6.0, (N_SHARD * OLD_CAP, LANES), jnp.float32)
    field = flat_normal(key, 40, 6.0)
    return arrange(rows, field, filler)


def draw_old_first(key, part):
    private = jax.random.fold_in(key, 9)
    rows = old_rows(key, part)
    filler = jax.random.truncated_normal(private, -6.0, 6.0, (N_SHARD * OLD_CAP, LANES), jnp.float32)
    field = flat_normal(key, 41, 6.0)
    return arrange(rows, field, filler)


def draw_old_second(key, part):
    private = jax.random.fold_in(key, 11)
    rows = old_rows(key, part)
    unit = jax.random.uniform(private, (N_SHARD * OLD_CAP, LANES), jnp.float32)
    filler = 0.01 * jnp.exp(unit * math.log(100.0))
    field = flat_spread(key, 42, 0.01, 1.0)
    return arrange(rows, field, filler)


def draw_grad_parts(key, part):
    private = jax.random.fold_in(key, 13)
    rows = new_rows(key, part)
    pieces = []
    for replica in range(N_REP):
        filler = jax.random.truncated_normal(jax.random.fold_in(private, replica), -6.0, 6.0, (N_SHARD * NEW_CAP, LANES), jnp.float32)
        field = flat_normal(key, 50 + replica, 6.0)
        pieces.append(arrange(rows, field, filler))
    return jnp.stack(pieces, 0)


def setup_inputs(seed: int = 0) -> dict:
    keys = jax.random.split(jax.random.key(seed), 7)
    old_master = draw_old_master(jax.random.fold_in(keys[6], 71), 0)
    old_first = draw_old_first(jax.random.fold_in(keys[6], 71), 0)
    old_second = draw_old_second(jax.random.fold_in(keys[6], 71), 0)
    grad_parts = draw_grad_parts(jax.random.fold_in(keys[6], 71), 0)
    old_offsets = draw_old_offsets(jax.random.fold_in(keys[6], 71), 0)
    new_offsets = draw_new_offsets(jax.random.fold_in(keys[6], 71), 0)
    return {"old_master": old_master, "old_first": old_first, "old_second": old_second, "grad_parts": grad_parts, "old_offsets": old_offsets, "new_offsets": new_offsets}


def adam_update(master, first, second, grads, valid):
    first_n = 0.9 * first + 0.1 * grads
    second_n = 0.95 * second + 0.05 * grads * grads
    first_hat = first_n / (1.0 - 0.9 ** STEP)
    second_hat = second_n / (1.0 - 0.95 ** STEP)
    master_n = master - 0.02 * (first_hat / (jnp.sqrt(second_hat) + 1e-08) + 0.1 * master)
    keep = valid[:, None]
    return (jnp.where(keep, master_n, 0.0), jnp.where(keep, first_n, 0.0), jnp.where(keep, second_n, 0.0))

def reference(old_master, old_first, old_second, grad_parts, old_offsets, new_offsets):
    rows = N_SHARD * BLK
    old_cap = old_master.shape[0] // N_SHARD
    new_cap = grad_parts.shape[1] // N_SHARD
    flat_rows = jnp.arange(rows, dtype=jnp.int32)
    inner = old_offsets[1:-1]
    owner = lax.optimization_barrier(jnp.sum((flat_rows[:, None] >= inner[None, :]).astype(jnp.int32), axis=1)).astype(jnp.int32)
    source = (2 * owner * old_cap + flat_rows - old_offsets[owner]).astype(jnp.int32)
    place = jnp.arange(N_SHARD * new_cap, dtype=jnp.int32)
    holder = place // new_cap
    wanted = (new_offsets[holder] + place % new_cap).astype(jnp.int32)
    valid = wanted < new_offsets[holder + 1]
    pick = source[jnp.minimum(wanted, rows - 1)]
    master, first, second = [jnp.where(valid[:, None], s[pick], 0.0) for s in (old_master, old_first, old_second)]
    grads = lax.optimization_barrier(jnp.sum(grad_parts.astype(jnp.float32), axis=0))
    master_n, first_n, second_n = adam_update(master, first, second, grads, valid)
    shape = (N_SHARD, N_REP, new_cap // N_REP, master.shape[1])
    weights = master_n.astype(jnp.bfloat16)
    return (master_n.reshape(shape), first_n.reshape(shape), second_n.reshape(shape), weights)
```

```python
import functools

import jax
import jax.numpy as jnp
from jax import lax
from jax.experimental import pallas as pl
from jax.experimental.pallas import tpu as pltpu
from jax.sharding import PartitionSpec as P

STEP = 10
MESH = pl.DeviceIdType.MESH
JITTER = 512
EDGE = 2 * JITTER
WINDOW = 3584
CHUNKS = 8
SUB = 64


def within(start):
    return jnp.clip(start, 0, 2 * EDGE)


def kernel(
    old_off,
    new_off,
    old_m,
    old_f,
    old_s,
    grads,
    out_m,
    out_f,
    out_s,
    out_w,
    main,
    alt,
    stage,
    edge,
    mine,
    theirs,
    res,
    wts,
    in_sem,
    mine_sem,
    stage_sem,
    die_sem,
    head_sem,
    tail_sem,
    grad_send,
    grad_recv,
    wts_send,
    wts_recv,
    res_sem,
    own_sem,
):
    olds = (old_m, old_f, old_s)
    outs = (out_m, out_f, out_s)
    old_cap = old_m.shape[0]
    half = mine.shape[0]
    size = half // CHUNKS
    r = lax.axis_index("rep")
    s = lax.axis_index("shard")
    owners = lax.axis_size("shard") // 2
    o = s // 2
    core = s % 2
    even = core == 0
    odd = core == 1
    other = (1 - r, s)

    up_rep = jnp.where(o % 16 == 15, 1 - r, r)
    down_rep = jnp.where(o % 16 == 0, 1 - r, r)
    sends_head = even & (up_rep == 0) & (o < owners - 1)
    gets_head = even & (r == 0) & (o > 0)
    sends_tail = even & (o > 0)
    sends_short = sends_tail & (down_rep == 0)
    sends_long = sends_tail & (down_rep == 1)
    gets_tail = odd & (o < owners - 1)
    gets_short = gets_tail & (r == 0)
    gets_long = gets_tail & (r == 1)
    head_to = (up_rep, lax.rem(s + 2, 2 * owners))
    head_from = (down_rep, lax.rem(s + 2 * owners - 2, 2 * owners))
    tail_to = (down_rep, lax.rem(s + 2 * owners - 1, 2 * owners))
    tail_from = (up_rep, lax.rem(s + 1, 2 * owners))
    die_to = (r, s + 1 - 2 * core)

    my_grads = pltpu.make_async_copy(grads.at[0, pl.ds(r * half, half)], mine, mine_sem)
    my_grads.start()

    def load_own(k, rep):
        if rep == 0:
            return pltpu.make_async_copy(
                olds[k].at[pl.ds(0, WINDOW - EDGE)], main.at[k, pl.ds(EDGE, WINDOW - EDGE)], in_sem.at[k]
            )
        return pltpu.make_async_copy(olds[k].at[pl.ds(JITTER, WINDOW)], main.at[k], in_sem.at[k])

    def load_stage(k):
        rows = stage.shape[1]
        return pltpu.make_async_copy(olds[k].at[pl.ds(old_cap - rows, rows)], stage.at[k], stage_sem.at[k])

    def die_copy(k, rep):
        first = 1024 if rep == 0 else 2560
        rows = min(WINDOW, old_cap - first)
        return pltpu.make_async_remote_copy(
            olds[k].at[pl.ds(first, rows)],
            main.at[k, pl.ds(0, rows)],
            die_sem.at[0, k],
            die_sem.at[1, k],
            device_id=die_to,
            device_id_type=MESH,
        )

    def head_copy(k):
        return pltpu.make_async_remote_copy(
            edge.at[k],
            main.at[k, pl.ds(0, EDGE)],
            head_sem.at[0, k],
            head_sem.at[1, k],
            device_id=head_to,
            device_id_type=MESH,
        )

    def tail_copy(k, rep):
        first, rows = (3072, JITTER) if rep == 0 else (1536, EDGE)
        return pltpu.make_async_remote_copy(
            olds[k].at[pl.ds(0, rows)],
            alt.at[k, pl.ds(first, rows)],
            tail_sem.at[0, k],
            tail_sem.at[1, k],
            device_id=tail_to,
            device_id_type=MESH,
        )

    def grad_copy(c):
        first = pl.multiple_of(c * size, 16)
        return pltpu.make_async_remote_copy(
            grads.at[0, pl.ds(pl.multiple_of((1 - r) * half + first, 16), size)],
            theirs.at[pl.ds(first, size)],
            grad_send.at[c],
            grad_recv.at[c],
            device_id=other,
            device_id_type=MESH,
        )

    def wts_copy(c):
        first = pl.multiple_of(c * size, 16)
        return pltpu.make_async_remote_copy(
            wts.at[pl.ds(first, size)],
            out_w.at[pl.ds(pl.multiple_of(r * half + first, 16), size)],
            wts_send.at[c],
            wts_recv.at[c],
            device_id=other,
            device_id_type=MESH,
        )

    def wts_arrival(c):
        first = pl.multiple_of(c * size, 16)
        return pltpu.make_async_remote_copy(
            wts.at[pl.ds(first, size)],
            out_w.at[pl.ds(pl.multiple_of((1 - r) * half + first, 16), size)],
            wts_send.at[c],
            wts_recv.at[c],
            device_id=other,
            device_id_type=MESH,
        )

    def own_copy(c):
        first = pl.multiple_of(c * size, 16)
        return pltpu.make_async_copy(
            wts.at[pl.ds(first, size)],
            out_w.at[pl.ds(pl.multiple_of(r * half + first, 16), size)],
            own_sem.at[c],
        )

    def res_copy(k, c):
        first = pl.multiple_of(c * size, 16)
        return pltpu.make_async_copy(
            res.at[k, pl.ds(first, size)], outs[k].at[pl.ds(first, size)], res_sem.at[k, c]
        )

    for rep in (0, 1):

        @pl.when(even & (r == rep))
        def _():
            for k in range(3):
                load_own(k, rep).start()

    @pl.when(sends_head)
    def _():
        for k in range(3):
            load_stage(k).start()

    barrier = pltpu.get_barrier_semaphore()
    pl.semaphore_signal(barrier, inc=1, device_id=other, device_id_type=MESH)

    @pl.when(odd)
    def _():
        pl.semaphore_signal(barrier, inc=1, device_id=die_to, device_id_type=MESH)

    @pl.when(gets_head)
    def _():
        pl.semaphore_signal(barrier, inc=1, device_id=head_from, device_id_type=MESH)

    @pl.when(gets_tail)
    def _():
        pl.semaphore_signal(barrier, inc=1, device_id=tail_from, device_id_type=MESH)

    targets = 1 + even.astype(jnp.int32) + sends_head.astype(jnp.int32) + sends_tail.astype(jnp.int32)
    pl.semaphore_wait(barrier, targets)

    for rep, cond in ((0, sends_short), (1, sends_long)):

        @pl.when(cond)
        def _():
            for k in range(3):
                tail_copy(k, rep).start()

    @pl.loop(0, CHUNKS)
    def _(c):
        grad_copy(c).start()

    for rep in (0, 1):

        @pl.when(even & (r == rep))
        def _():
            for k in range(3):
                die_copy(k, rep).start()

    @pl.when(sends_head)
    def _():
        begin = within(old_off[o + 1] - old_off[o] - (old_cap - stage.shape[1]) - EDGE)
        for k in range(3):
            load_stage(k).wait()
        for k in range(3):

            @pl.loop(0, EDGE // SUB)
            def _(j):
                edge[k, pl.ds(pl.multiple_of(j * SUB, SUB), SUB), :] = stage[k, pl.ds(begin + j * SUB, SUB), :]

            head_copy(k).start()

    for rep in (0, 1):

        @pl.when(even & (r == rep))
        def _():
            for k in range(3):
                load_own(k, rep).wait()

        @pl.when(odd & (r == rep))
        def _():
            for k in range(3):
                die_copy(k, rep).wait_recv()

    @pl.when(gets_head)
    def _():
        for k in range(3):
            head_copy(k).wait_recv()

    for rep, cond in ((0, gets_short), (1, gets_long)):

        @pl.when(cond)
        def _():
            for k in range(3):
                tail_copy(k, rep).wait_recv()

    my_grads.wait()

    start = within(new_off[s] - old_off[o] + EDGE - 2 * EDGE * core)
    edge_start = within(new_off[s] - old_off[o + 1] + 2 * half)
    split = jnp.where(even, new_off[s + 1], old_off[o + 1])
    flat = new_off[s] + r * half
    stop = new_off[s + 1]

    @pl.loop(0, CHUNKS)
    def _(c):
        grad_copy(c).wait_recv()

        @pl.loop(0, size // SUB)
        def _(j):
            at = c * size + j * SUB
            rows = pl.ds(pl.multiple_of(at, SUB), SUB)
            row = flat + at + lax.broadcasted_iota(jnp.int32, (SUB, 128), 0)
            near = row < split
            keep = row < stop
            master, first, second = [
                jnp.where(near, main[k, pl.ds(start + at, SUB), :], alt[k, pl.ds(edge_start + at, SUB), :])
                for k in range(3)
            ]
            total = mine[rows, :] + theirs[rows, :]
            first_n = 0.9 * first + 0.1 * total
            second_n = 0.95 * second + 0.05 * total * total
            first_hat = first_n / (1.0 - 0.9**STEP)
            second_hat = second_n / (1.0 - 0.95**STEP)
            master_n = master - 0.02 * (first_hat / (jnp.sqrt(second_hat) + 1e-08) + 0.1 * master)
            master_n = jnp.where(keep, master_n, 0.0)
            res[0, rows, :] = master_n
            res[1, rows, :] = jnp.where(keep, first_n, 0.0)
            res[2, rows, :] = jnp.where(keep, second_n, 0.0)
            wts[rows, :] = master_n.astype(jnp.bfloat16)

        wts_copy(c).start()
        own_copy(c).start()
        for k in range(3):
            res_copy(k, c).start()

    for rep in (0, 1):

        @pl.when(even & (r == rep))
        def _():
            for k in range(3):
                die_copy(k, rep).wait_send()

    @pl.when(sends_head)
    def _():
        for k in range(3):
            head_copy(k).wait_send()

    for rep, cond in ((0, sends_short), (1, sends_long)):

        @pl.when(cond)
        def _():
            for k in range(3):
                tail_copy(k, rep).wait_send()

    @pl.loop(0, CHUNKS)
    def _(c):
        grad_copy(c).wait_send()
        for k in range(3):
            res_copy(k, c).wait()
        own_copy(c).wait()
        wts_copy(c).wait_send()
        wts_arrival(c).wait_recv()


def local(old_master, old_first, old_second, grad_parts, old_offsets, new_offsets):
    new_cap, lanes = grad_parts.shape[1:]
    half = new_cap // 2
    smem = pl.BlockSpec(memory_space=pltpu.SMEM)
    hbm = pl.BlockSpec(memory_space=pl.ANY)
    state = jax.ShapeDtypeStruct((half, lanes), jnp.float32)
    dma = pltpu.SemaphoreType.DMA
    master, first, second, weights = pl.pallas_call(
        kernel,
        out_shape=(state, state, state, jax.ShapeDtypeStruct((new_cap, lanes), jnp.bfloat16)),
        in_specs=[smem, smem, hbm, hbm, hbm, hbm],
        out_specs=(hbm, hbm, hbm, hbm),
        scratch_shapes=[
            pltpu.VMEM((3, WINDOW, lanes), jnp.float32),
            pltpu.VMEM((3, WINDOW, lanes), jnp.float32),
            pltpu.VMEM((3, 3 * EDGE, lanes), jnp.float32),
            pltpu.VMEM((3, EDGE, lanes), jnp.float32),
            pltpu.VMEM((half, lanes), jnp.float32),
            pltpu.VMEM((half, lanes), jnp.float32),
            pltpu.VMEM((3, half, lanes), jnp.float32),
            pltpu.VMEM((half, lanes), jnp.bfloat16),
            dma((3,)),
            dma,
            dma((3,)),
            dma((2, 3)),
            dma((2, 3)),
            dma((2, 3)),
            dma((CHUNKS,)),
            dma((CHUNKS,)),
            dma((CHUNKS,)),
            dma((CHUNKS,)),
            dma((3, CHUNKS)),
            dma((CHUNKS,)),
        ],
        compiler_params=pltpu.CompilerParams(
            collective_id=0, has_side_effects=True, vmem_limit_bytes=48 * 1024 * 1024
        ),
        name="move_and_update",
    )(old_offsets, new_offsets, old_master, old_first, old_second, grad_parts)
    return (master[None, None], first[None, None], second[None, None], weights)


def solution(mesh):
    in_specs = (
        P("shard", None),
        P("shard", None),
        P("shard", None),
        P("rep", "shard", None),
        P(),
        P(),
    )
    out_specs = (
        P("shard", "rep", None, None),
        P("shard", "rep", None, None),
        P("shard", "rep", None, None),
        P("shard", None),
    )
    return jax.shard_map(local, mesh=mesh, in_specs=in_specs, out_specs=out_specs, check_vma=False)
```

```python
import functools

import jax
import jax.numpy as jnp
from jax import lax
from jax.experimental import pallas as pl
from jax.experimental.pallas import tpu as pltpu
from jax.sharding import PartitionSpec as P

STEP = 10
MESH = pl.DeviceIdType.MESH
JITTER = 512
EDGE = 2 * JITTER
WINDOW = 3584
CHUNKS = 8
SUB = 64


def within(start):
    return jnp.clip(start, 0, 2 * EDGE)


def kernel(
    old_off_in,
    new_off_in,
    old_m,
    old_f,
    old_s,
    grads,
    out_m,
    out_f,
    out_s,
    out_w,
    old_off,
    new_off,
    main,
    alt,
    relay,
    stage,
    edge,
    mine,
    theirs,
    res,
    wts,
    off_sem,
    in_sem,
    mine_sem,
    stage_sem,
    die_sem,
    head_sem,
    tail_sem,
    head_relay_sem,
    tail_relay_sem,
    grad_send,
    grad_recv,
    wts_send,
    wts_recv,
    res_sem,
    own_sem,
):
    olds = (old_m, old_f, old_s)
    outs = (out_m, out_f, out_s)
    old_cap = old_m.shape[0]
    half = mine.shape[0]
    size = half // CHUNKS
    r = lax.axis_index("rep")
    s = lax.axis_index("shard")
    owners = lax.axis_size("shard") // 2
    o = s // 2
    core = s % 2
    even = core == 0
    odd = core == 1
    other = (1 - r, s)

    x = o % 4

    up_rep = jnp.where(o % 16 == 15, 1 - r, r)
    down_rep = jnp.where(o % 16 == 0, 1 - r, r)
    sends_head = even & (up_rep == 0) & (o < owners - 1)
    gets_head = even & (r == 0) & (o > 0)
    sends_tail = even & (o > 0)
    gets_tail = odd & (o < owners - 1)
    count = 2 * owners
    head_to = (up_rep, lax.rem(s + 2, count))
    head_from = (down_rep, lax.rem(s + count - 2, count))
    tail_to = (down_rep, lax.rem(s + count - 1, count))
    tail_from = (up_rep, lax.rem(s + 1, count))
    die_to = (r, s + 1 - 2 * core)

    z_lo = (o // 4) % 4
    head_wraps = sends_head & (x == 3)
    head_unwraps = gets_head & (x == 0)
    tail_wraps = sends_tail & (x == 0)
    tail_unwraps = gets_tail & (x == 3)
    head_source = s - 1 + 2 * (3 - x)
    head_rep = jnp.where(z_lo == 3, 1 - r, r)
    relays_head = odd & (x < 3) & (head_rep == 0) & (head_source < count - 2)
    tail_source = s - 1 - 2 * x
    tail_rep = jnp.where(z_lo == 0, 1 - r, r)
    relays_tail = odd & (x > 0) & (tail_source > 0)

    offsets = (
        pltpu.make_async_copy(old_off_in, old_off, off_sem.at[0]),
        pltpu.make_async_copy(new_off_in, new_off, off_sem.at[1]),
    )
    for copy in offsets:
        copy.start()
    my_grads = pltpu.make_async_copy(grads.at[0, pl.ds(r * half, half)], mine, mine_sem)
    my_grads.start()

    def load_own(k, rep):
        if rep == 0:
            return pltpu.make_async_copy(
                olds[k].at[pl.ds(0, WINDOW - EDGE)], main.at[k, pl.ds(EDGE, WINDOW - EDGE)], in_sem.at[k]
            )
        return pltpu.make_async_copy(olds[k].at[pl.ds(JITTER, WINDOW)], main.at[k], in_sem.at[k])

    def load_stage(k):
        rows = stage.shape[1]
        return pltpu.make_async_copy(olds[k].at[pl.ds(old_cap - rows, rows)], stage.at[k], stage_sem.at[k])

    def die_copy(k, rep):
        first = 1024 if rep == 0 else 2560
        rows = min(WINDOW, old_cap - first)
        return pltpu.make_async_remote_copy(
            olds[k].at[pl.ds(first, rows)],
            main.at[k, pl.ds(0, rows)],
            die_sem.at[0, k],
            die_sem.at[1, k],
            device_id=die_to,
            device_id_type=MESH,
        )

    def send(src, dst, sems, to):
        return pltpu.make_async_remote_copy(src, dst, sems[0], sems[1], device_id=to, device_id_type=MESH)

    quarter = EDGE // 4

    def head_copy(k, part=None):
        rows = pl.ds(0, EDGE) if part is None else pl.ds(part * quarter, quarter)
        at = 0 if part is None else part
        sems = (head_sem.at[0, at, k], head_sem.at[1, at, k])
        return send(edge.at[k, rows], main.at[k, rows], sems, head_to)

    def head_relay_in(k, part):
        rows = pl.ds(part * quarter, quarter)
        sems = (head_sem.at[0, part, k], head_relay_sem.at[0, k])
        return send(edge.at[k, rows], relay.at[0, k], sems, (r, s - 2 * (3 - part) + 1))

    def head_relay_out(k, part):
        rows = pl.ds(part * quarter, quarter)
        sems = (head_relay_sem.at[1, k], head_sem.at[1, part, k])
        return send(relay.at[0, k], main.at[k, rows], sems, (head_rep, lax.rem(head_source + 2, count)))

    def tail_place(rep):
        return (3072, JITTER) if rep == 0 else (1536, EDGE)

    def tail_copy(k, rep, part=None):
        first, rows = tail_place(rep)
        begin = 0
        if part is not None:
            rows //= 4
            begin = part * rows
        at = 0 if part is None else part
        sems = (tail_sem.at[0, at, k], tail_sem.at[1, at, k])
        return send(olds[k].at[pl.ds(begin, rows)], alt.at[k, pl.ds(first + begin, rows)], sems, tail_to)

    def tail_relay_in(k, rep, part):
        rows = tail_place(rep)[1] // 4
        sems = (tail_sem.at[0, part, k], tail_relay_sem.at[0, k])
        to = (r, lax.rem(s + 2 * part + 1, count))
        return send(olds[k].at[pl.ds(part * rows, rows)], relay.at[1, k, pl.ds(0, rows)], sems, to)

    def tail_relay_out(k, rep, part):
        first, rows = tail_place(rep)
        rows //= 4
        sems = (tail_relay_sem.at[1, k], tail_sem.at[1, part, k])
        to = (tail_rep, lax.rem(tail_source + count - 1, count))
        return send(relay.at[1, k, pl.ds(0, rows)], alt.at[k, pl.ds(first + part * rows, rows)], sems, to)

    def grad_copy(c):
        first = pl.multiple_of(c * size, 16)
        return pltpu.make_async_remote_copy(
            grads.at[0, pl.ds(pl.multiple_of((1 - r) * half + first, 16), size)],
            theirs.at[pl.ds(first, size)],
            grad_send.at[c],
            grad_recv.at[c],
            device_id=other,
            device_id_type=MESH,
        )

    def wts_copy(c):
        first = pl.multiple_of(c * size, 16)
        return pltpu.make_async_remote_copy(
            wts.at[pl.ds(first, size)],
            out_w.at[pl.ds(pl.multiple_of(r * half + first, 16), size)],
            wts_send.at[c],
            wts_recv.at[c],
            device_id=other,
            device_id_type=MESH,
        )

    def wts_arrival(c):
        first = pl.multiple_of(c * size, 16)
        return pltpu.make_async_remote_copy(
            wts.at[pl.ds(first, size)],
            out_w.at[pl.ds(pl.multiple_of((1 - r) * half + first, 16), size)],
            wts_send.at[c],
            wts_recv.at[c],
            device_id=other,
            device_id_type=MESH,
        )

    def own_copy(c):
        first = pl.multiple_of(c * size, 16)
        return pltpu.make_async_copy(
            wts.at[pl.ds(first, size)],
            out_w.at[pl.ds(pl.multiple_of(r * half + first, 16), size)],
            own_sem.at[c],
        )

    def res_copy(k, c):
        first = pl.multiple_of(c * size, 16)
        return pltpu.make_async_copy(
            res.at[k, pl.ds(first, size)], outs[k].at[pl.ds(first, size)], res_sem.at[k, c]
        )

    for rep in (0, 1):

        @pl.when(even & (r == rep))
        def _():
            for k in range(3):
                load_own(k, rep).start()

    @pl.when(sends_head)
    def _():
        for k in range(3):
            load_stage(k).start()

    barrier = pltpu.get_barrier_semaphore()
    pl.semaphore_signal(barrier, inc=1, device_id=other, device_id_type=MESH)

    @pl.when(odd)
    def _():
        pl.semaphore_signal(barrier, inc=1, device_id=die_to, device_id_type=MESH)

    @pl.when(gets_head)
    def _():
        pl.semaphore_signal(barrier, inc=1, device_id=head_from, device_id_type=MESH)

    @pl.when(head_unwraps)
    def _():
        for part in (0, 1, 2):
            at = lax.rem(s + count - 2 - 2 * (3 - part) + 1, count)
            pl.semaphore_signal(barrier, inc=1, device_id=(down_rep, at), device_id_type=MESH)

    @pl.when(gets_tail)
    def _():
        pl.semaphore_signal(barrier, inc=1, device_id=tail_from, device_id_type=MESH)

    @pl.when(tail_unwraps)
    def _():
        for part in (1, 2, 3):
            at = lax.rem(s + 2 * part + 2, count)
            pl.semaphore_signal(barrier, inc=1, device_id=(up_rep, at), device_id_type=MESH)

    @pl.when(relays_head)
    def _():
        pl.semaphore_signal(barrier, inc=1, device_id=(r, lax.rem(head_source, count)), device_id_type=MESH)

    @pl.when(relays_tail)
    def _():
        pl.semaphore_signal(barrier, inc=1, device_id=(r, lax.rem(tail_source + count, count)), device_id_type=MESH)

    targets = 1
    for cond, more in (
        (even, 1),
        (sends_head, 1),
        (head_wraps, 3),
        (sends_tail, 1),
        (tail_wraps, 3),
        (relays_head, 1),
        (relays_tail, 1),
    ):
        targets = targets + more * cond.astype(jnp.int32)
    pl.semaphore_wait(barrier, targets)

    for rep in (0, 1):

        @pl.when(sends_tail & (down_rep == rep) & (x > 0))
        def _():
            for k in range(3):
                tail_copy(k, rep).start()

        @pl.when(tail_wraps & (down_rep == rep))
        def _():
            for part in (1, 2, 3):
                for k in range(3):
                    tail_relay_in(k, rep, part).start()
            for k in range(3):
                tail_copy(k, rep, 0).start()

    @pl.loop(0, CHUNKS)
    def _(c):
        grad_copy(c).start()

    for rep in (0, 1):

        @pl.when(even & (r == rep))
        def _():
            for k in range(3):
                die_copy(k, rep).start()

    for copy in offsets:
        copy.wait()

    @pl.when(sends_head)
    def _():
        begin = within(old_off[o + 1] - old_off[o] - (old_cap - stage.shape[1]) - EDGE)
        for k in range(3):
            load_stage(k).wait()
        for k in range(3):

            @pl.loop(0, EDGE // SUB)
            def _(j):
                edge[k, pl.ds(pl.multiple_of(j * SUB, SUB), SUB), :] = stage[k, pl.ds(begin + j * SUB, SUB), :]

            @pl.when(x < 3)
            def _():
                head_copy(k).start()

            @pl.when(x == 3)
            def _():
                for part in (0, 1, 2):
                    head_relay_in(k, part).start()
                head_copy(k, 3).start()

    for rep in (0, 1):
        for part in (1, 2, 3):

            @pl.when(relays_tail & (tail_rep == rep) & (x == part))
            def _():
                for k in range(3):
                    tail_relay_in(k, rep, part).wait_recv()
                    tail_relay_out(k, rep, part).start()

    for part in (0, 1, 2):

        @pl.when(relays_head & (x == part))
        def _():
            for k in range(3):
                head_relay_in(k, part).wait_recv()
                head_relay_out(k, part).start()

    for rep in (0, 1):

        @pl.when(even & (r == rep))
        def _():
            for k in range(3):
                load_own(k, rep).wait()

        @pl.when(odd & (r == rep))
        def _():
            for k in range(3):
                die_copy(k, rep).wait_recv()

    @pl.when(gets_head & (x > 0))
    def _():
        for k in range(3):
            head_copy(k).wait_recv()

    @pl.when(head_unwraps)
    def _():
        for part in range(4):
            for k in range(3):
                head_copy(k, part).wait_recv()

    for rep in (0, 1):

        @pl.when(gets_tail & (r == rep) & (x < 3))
        def _():
            for k in range(3):
                tail_copy(k, rep).wait_recv()

        @pl.when(tail_unwraps & (r == rep))
        def _():
            for part in range(4):
                for k in range(3):
                    tail_copy(k, rep, part).wait_recv()

    my_grads.wait()

    start = within(new_off[s] - old_off[o] + EDGE - 2 * EDGE * core)
    edge_start = within(new_off[s] - old_off[o + 1] + 2 * half)
    split = jnp.where(even, new_off[s + 1], old_off[o + 1])
    flat = new_off[s] + r * half
    stop = new_off[s + 1]

    @pl.loop(0, CHUNKS)
    def _(c):
        grad_copy(c).wait_recv()

        @pl.loop(0, size // SUB)
        def _(j):
            at = c * size + j * SUB
            rows = pl.ds(pl.multiple_of(at, SUB), SUB)
            row = flat + at + lax.broadcasted_iota(jnp.int32, (SUB, 128), 0)
            near = row < split
            keep = row < stop
            master, first, second = [
                jnp.where(near, main[k, pl.ds(start + at, SUB), :], alt[k, pl.ds(edge_start + at, SUB), :])
                for k in range(3)
            ]
            total = mine[rows, :] + theirs[rows, :]
            first_n = 0.9 * first + 0.1 * total
            second_n = 0.95 * second + 0.05 * total * total
            first_hat = first_n / (1.0 - 0.9**STEP)
            second_hat = second_n / (1.0 - 0.95**STEP)
            master_n = master - 0.02 * (first_hat / (jnp.sqrt(second_hat) + 1e-08) + 0.1 * master)
            master_n = jnp.where(keep, master_n, 0.0)
            res[0, rows, :] = master_n
            res[1, rows, :] = jnp.where(keep, first_n, 0.0)
            res[2, rows, :] = jnp.where(keep, second_n, 0.0)
            wts[rows, :] = master_n.astype(jnp.bfloat16)

        wts_copy(c).start()
        own_copy(c).start()
        for k in range(3):
            res_copy(k, c).start()

    for rep in (0, 1):

        @pl.when(even & (r == rep))
        def _():
            for k in range(3):
                die_copy(k, rep).wait_send()

    @pl.when(sends_head & (x < 3))
    def _():
        for k in range(3):
            head_copy(k).wait_send()

    @pl.when(head_wraps)
    def _():
        for part in range(4):
            for k in range(3):
                head_copy(k, part).wait_send()

    @pl.when(relays_head)
    def _():
        for k in range(3):
            head_relay_out(k, 0).wait_send()

    for rep in (0, 1):

        @pl.when(sends_tail & (down_rep == rep) & (x > 0))
        def _():
            for k in range(3):
                tail_copy(k, rep).wait_send()

        @pl.when(tail_wraps & (down_rep == rep))
        def _():
            for part in range(4):
                for k in range(3):
                    tail_copy(k, rep, part).wait_send()

        @pl.when(relays_tail & (tail_rep == rep))
        def _():
            for k in range(3):
                tail_relay_out(k, rep, 0).wait_send()

    @pl.loop(0, CHUNKS)
    def _(c):
        grad_copy(c).wait_send()
        for k in range(3):
            res_copy(k, c).wait()
        own_copy(c).wait()
        wts_copy(c).wait_send()
        wts_arrival(c).wait_recv()


def finish(in_m, in_f, in_s, in_w, out_m, out_f, out_s, out_w, sem):
    pairs = ((in_m, out_m), (in_f, out_f), (in_s, out_s), (in_w, out_w))
    copies = [pltpu.make_async_copy(src, dst, sem.at[i]) for i, (src, dst) in enumerate(pairs)]
    for copy in copies:
        copy.start()
    for copy in copies:
        copy.wait()


def local(old_master, old_first, old_second, grad_parts, old_offsets, new_offsets):
    new_cap, lanes = grad_parts.shape[1:]
    half = new_cap // 2
    hbm = pl.BlockSpec(memory_space=pltpu.HBM)
    free = pl.BlockSpec(memory_space=pl.ANY)
    state = jax.ShapeDtypeStruct((half, lanes), jnp.float32)
    dma = pltpu.SemaphoreType.DMA
    shapes = (state, state, state, jax.ShapeDtypeStruct((new_cap, lanes), jnp.bfloat16))
    results = pl.pallas_call(
        kernel,
        out_shape=shapes,
        in_specs=[hbm] * 6,
        out_specs=(free, free, free, free),
        scratch_shapes=[
            pltpu.SMEM(old_offsets.shape, jnp.int32),
            pltpu.SMEM(new_offsets.shape, jnp.int32),
            pltpu.VMEM((3, WINDOW, lanes), jnp.float32),
            pltpu.VMEM((3, WINDOW, lanes), jnp.float32),
            pltpu.VMEM((2, 3, EDGE // 4, lanes), jnp.float32),
            pltpu.VMEM((3, 3 * EDGE, lanes), jnp.float32),
            pltpu.VMEM((3, EDGE, lanes), jnp.float32),
            pltpu.VMEM((half, lanes), jnp.float32),
            pltpu.VMEM((half, lanes), jnp.float32),
            pltpu.VMEM((3, half, lanes), jnp.float32),
            pltpu.VMEM((half, lanes), jnp.bfloat16),
            dma((2,)),
            dma((3,)),
            dma,
            dma((3,)),
            dma((2, 3)),
            dma((2, 4, 3)),
            dma((2, 4, 3)),
            dma((2, 3)),
            dma((2, 3)),
            dma((CHUNKS,)),
            dma((CHUNKS,)),
            dma((CHUNKS,)),
            dma((CHUNKS,)),
            dma((3, CHUNKS)),
            dma((CHUNKS,)),
        ],
        compiler_params=pltpu.CompilerParams(
            collective_id=0, has_side_effects=True, vmem_limit_bytes=48 * 1024 * 1024
        ),
        name="move_and_update",
    )(old_offsets, new_offsets, old_master, old_first, old_second, grad_parts)
    master, first, second, weights = pl.pallas_call(
        finish,
        out_shape=shapes,
        in_specs=[free] * 4,
        out_specs=(hbm,) * 4,
        scratch_shapes=[dma((4,))],
        name="finish",
    )(*results)
    return (master[None, None], first[None, None], second[None, None], weights)


def solution(mesh):
    in_specs = (
        P("shard", None),
        P("shard", None),
        P("shard", None),
        P("rep", "shard", None),
        P(),
        P(),
    )
    out_specs = (
        P("shard", "rep", None, None),
        P("shard", "rep", None, None),
        P("shard", "rep", None, None),
        P("shard", None),
    )
    return jax.shard_map(local, mesh=mesh, in_specs=in_specs, out_specs=out_specs, check_vma=False)
```

```python
import functools

import jax
import jax.numpy as jnp
from jax import lax
from jax.experimental import pallas as pl
from jax.experimental.pallas import tpu as pltpu
from jax.sharding import PartitionSpec as P

STEP = 10
MESH = pl.DeviceIdType.MESH
JITTER = 512
EDGE = 2 * JITTER
WINDOW = 3584
CHUNKS = 8
SUB = 64


def within(start):
    return jnp.clip(start, 0, 2 * EDGE)


def kernel(
    old_off_in,
    new_off_in,
    old_m,
    old_f,
    old_s,
    grads,
    out_m,
    out_f,
    out_s,
    out_w,
    old_off,
    new_off,
    main,
    alt,
    relay,
    stage,
    edge,
    mine,
    theirs,
    res,
    wts,
    off_sem,
    in_sem,
    mine_sem,
    stage_sem,
    die_sem,
    head_sem,
    tail_sem,
    head_relay_sem,
    tail_relay_sem,
    grad_send,
    grad_recv,
    wts_send,
    wts_recv,
    res_sem,
    own_sem,
):
    olds = (old_m, old_f, old_s)
    outs = (out_m, out_f, out_s)
    old_cap = old_m.shape[0]
    half = mine.shape[0]
    size = half // CHUNKS
    r = lax.axis_index("rep")
    s = lax.axis_index("shard")
    owners = lax.axis_size("shard") // 2
    o = s // 2
    core = s % 2
    even = core == 0
    odd = core == 1
    other = (1 - r, s)

    x = o % 4

    up_rep = jnp.where(o % 16 == 15, 1 - r, r)
    down_rep = jnp.where(o % 16 == 0, 1 - r, r)
    sends_head = even & (up_rep == 0) & (o < owners - 1)
    gets_head = even & (r == 0) & (o > 0)
    sends_tail = even & (o > 0)
    gets_tail = odd & (o < owners - 1)
    count = 2 * owners
    head_to = (up_rep, lax.rem(s + 2, count))
    head_from = (down_rep, lax.rem(s + count - 2, count))
    tail_to = (down_rep, lax.rem(s + count - 1, count))
    tail_from = (up_rep, lax.rem(s + 1, count))
    die_to = (r, s + 1 - 2 * core)

    z_lo = (o // 4) % 4
    turn_up = jnp.where(z_lo == 3, 32, 0)
    turn_down = jnp.where(z_lo == 0, 32, 0)
    head_wraps = sends_head & (x == 3)
    head_unwraps = gets_head & (x == 0)
    tail_wraps = sends_tail & (x == 0)
    tail_unwraps = gets_tail & (x == 3)
    head_source = s - 1 + 2 * (3 - x) - turn_up
    head_rep = jnp.where(z_lo == 3, 1 - r, r)
    relays_head = odd & (head_rep == 0) & (head_source >= 0)
    tail_source = s - 1 - 2 * x + turn_down
    tail_rep = jnp.where(z_lo == 0, 1 - r, r)
    relays_tail = odd & (tail_source < count)
    head_relays = s + jnp.where(z_lo == 0, 24, -8) + 1
    tail_relays = s + jnp.where(z_lo == 3, -24, 8) - 6

    offsets = (
        pltpu.make_async_copy(old_off_in, old_off, off_sem.at[0]),
        pltpu.make_async_copy(new_off_in, new_off, off_sem.at[1]),
    )
    for copy in offsets:
        copy.start()
    my_grads = pltpu.make_async_copy(grads.at[0, pl.ds(r * half, half)], mine, mine_sem)
    my_grads.start()

    def load_own(k, rep):
        if rep == 0:
            return pltpu.make_async_copy(
                olds[k].at[pl.ds(0, WINDOW - EDGE)], main.at[k, pl.ds(EDGE, WINDOW - EDGE)], in_sem.at[k]
            )
        return pltpu.make_async_copy(olds[k].at[pl.ds(JITTER, WINDOW)], main.at[k], in_sem.at[k])

    def load_stage(k):
        rows = stage.shape[1]
        return pltpu.make_async_copy(olds[k].at[pl.ds(old_cap - rows, rows)], stage.at[k], stage_sem.at[k])

    def die_copy(k, rep):
        first = 1024 if rep == 0 else 2560
        rows = min(WINDOW, old_cap - first)
        return pltpu.make_async_remote_copy(
            olds[k].at[pl.ds(first, rows)],
            main.at[k, pl.ds(0, rows)],
            die_sem.at[0, k],
            die_sem.at[1, k],
            device_id=die_to,
            device_id_type=MESH,
        )

    def send(src, dst, sems, to):
        return pltpu.make_async_remote_copy(src, dst, sems[0], sems[1], device_id=to, device_id_type=MESH)

    quarter = EDGE // 4

    def head_copy(k, part=None):
        rows = pl.ds(0, EDGE) if part is None else pl.ds(part * quarter, quarter)
        at = 0 if part is None else part
        sems = (head_sem.at[0, at, k], head_sem.at[1, at, k])
        return send(edge.at[k, rows], main.at[k, rows], sems, head_to)

    def head_relay_in(k, part):
        rows = pl.ds(part * quarter, quarter)
        sems = (head_sem.at[0, part, k], head_relay_sem.at[0, k])
        to = (r, lax.rem(s - 2 * (3 - part) + 1 + turn_up + count, count))
        return send(edge.at[k, rows], relay.at[0, k], sems, to)

    def head_relay_out(k, part):
        rows = pl.ds(part * quarter, quarter)
        sems = (head_relay_sem.at[1, k], head_sem.at[1, part, k])
        return send(relay.at[0, k], main.at[k, rows], sems, (head_rep, lax.rem(head_source + 2, count)))

    def tail_place(rep):
        return (3072, JITTER) if rep == 0 else (1536, EDGE)

    def tail_copy(k, rep, part=None):
        first, rows = tail_place(rep)
        begin = 0
        if part is not None:
            rows //= 4
            begin = part * rows
        at = 0 if part is None else part
        sems = (tail_sem.at[0, at, k], tail_sem.at[1, at, k])
        return send(olds[k].at[pl.ds(begin, rows)], alt.at[k, pl.ds(first + begin, rows)], sems, tail_to)

    def tail_relay_in(k, rep, part):
        rows = tail_place(rep)[1] // 4
        sems = (tail_sem.at[0, part, k], tail_relay_sem.at[0, k])
        to = (r, lax.rem(s + 2 * part + 1 - turn_down + count, count))
        return send(olds[k].at[pl.ds(part * rows, rows)], relay.at[1, k, pl.ds(0, rows)], sems, to)

    def tail_relay_out(k, rep, part):
        first, rows = tail_place(rep)
        rows //= 4
        sems = (tail_relay_sem.at[1, k], tail_sem.at[1, part, k])
        to = (tail_rep, lax.rem(tail_source + count - 1, count))
        return send(relay.at[1, k, pl.ds(0, rows)], alt.at[k, pl.ds(first + part * rows, rows)], sems, to)

    def grad_copy(c):
        first = pl.multiple_of(c * size, 16)
        return pltpu.make_async_remote_copy(
            grads.at[0, pl.ds(pl.multiple_of((1 - r) * half + first, 16), size)],
            theirs.at[pl.ds(first, size)],
            grad_send.at[c],
            grad_recv.at[c],
            device_id=other,
            device_id_type=MESH,
        )

    def wts_copy(c):
        first = pl.multiple_of(c * size, 16)
        return pltpu.make_async_remote_copy(
            wts.at[pl.ds(first, size)],
            out_w.at[pl.ds(pl.multiple_of(r * half + first, 16), size)],
            wts_send.at[c],
            wts_recv.at[c],
            device_id=other,
            device_id_type=MESH,
        )

    def wts_arrival(c):
        first = pl.multiple_of(c * size, 16)
        return pltpu.make_async_remote_copy(
            wts.at[pl.ds(first, size)],
            out_w.at[pl.ds(pl.multiple_of((1 - r) * half + first, 16), size)],
            wts_send.at[c],
            wts_recv.at[c],
            device_id=other,
            device_id_type=MESH,
        )

    def own_copy(c):
        first = pl.multiple_of(c * size, 16)
        return pltpu.make_async_copy(
            wts.at[pl.ds(first, size)],
            out_w.at[pl.ds(pl.multiple_of(r * half + first, 16), size)],
            own_sem.at[c],
        )

    def res_copy(k, c):
        first = pl.multiple_of(c * size, 16)
        return pltpu.make_async_copy(
            res.at[k, pl.ds(first, size)], outs[k].at[pl.ds(first, size)], res_sem.at[k, c]
        )

    for rep in (0, 1):

        @pl.when(even & (r == rep))
        def _():
            for k in range(3):
                load_own(k, rep).start()

    @pl.when(sends_head)
    def _():
        for k in range(3):
            load_stage(k).start()

    barrier = pltpu.get_barrier_semaphore()
    pl.semaphore_signal(barrier, inc=1, device_id=other, device_id_type=MESH)

    @pl.when(odd)
    def _():
        pl.semaphore_signal(barrier, inc=1, device_id=die_to, device_id_type=MESH)

    @pl.when(gets_head & (x > 0))
    def _():
        pl.semaphore_signal(barrier, inc=1, device_id=head_from, device_id_type=MESH)

    @pl.when(head_unwraps)
    def _():
        for part in range(4):
            at = lax.rem(head_relays + 2 * part + count, count)
            pl.semaphore_signal(barrier, inc=1, device_id=(down_rep, at), device_id_type=MESH)

    @pl.when(gets_tail & (x < 3))
    def _():
        pl.semaphore_signal(barrier, inc=1, device_id=tail_from, device_id_type=MESH)

    @pl.when(tail_unwraps)
    def _():
        for part in range(4):
            at = lax.rem(tail_relays + 2 * part + count, count)
            pl.semaphore_signal(barrier, inc=1, device_id=(up_rep, at), device_id_type=MESH)

    @pl.when(relays_head)
    def _():
        pl.semaphore_signal(barrier, inc=1, device_id=(r, lax.rem(head_source + count, count)), device_id_type=MESH)

    @pl.when(relays_tail)
    def _():
        pl.semaphore_signal(barrier, inc=1, device_id=(r, lax.rem(tail_source, count)), device_id_type=MESH)

    targets = 1
    for cond, more in (
        (even, 1),
        (sends_head, 1),
        (head_wraps, 3),
        (sends_tail, 1),
        (tail_wraps, 3),
        (relays_head, 1),
        (relays_tail, 1),
    ):
        targets = targets + more * cond.astype(jnp.int32)
    pl.semaphore_wait(barrier, targets)

    for rep in (0, 1):

        @pl.when(sends_tail & (down_rep == rep) & (x > 0))
        def _():
            for k in range(3):
                tail_copy(k, rep).start()

        @pl.when(tail_wraps & (down_rep == rep))
        def _():
            for part in range(4):
                for k in range(3):
                    tail_relay_in(k, rep, part).start()

    @pl.loop(0, CHUNKS)
    def _(c):
        grad_copy(c).start()

    for rep in (0, 1):

        @pl.when(even & (r == rep))
        def _():
            for k in range(3):
                die_copy(k, rep).start()

    for copy in offsets:
        copy.wait()

    @pl.when(sends_head)
    def _():
        begin = within(old_off[o + 1] - old_off[o] - (old_cap - stage.shape[1]) - EDGE)
        for k in range(3):
            load_stage(k).wait()
        for k in range(3):

            @pl.loop(0, EDGE // SUB)
            def _(j):
                edge[k, pl.ds(pl.multiple_of(j * SUB, SUB), SUB), :] = stage[k, pl.ds(begin + j * SUB, SUB), :]

            @pl.when(x < 3)
            def _():
                head_copy(k).start()

            @pl.when(x == 3)
            def _():
                for part in range(4):
                    head_relay_in(k, part).start()

    for rep in (0, 1):
        for part in range(4):

            @pl.when(relays_tail & (tail_rep == rep) & (x == part))
            def _():
                for k in range(3):
                    tail_relay_in(k, rep, part).wait_recv()
                    tail_relay_out(k, rep, part).start()

    for part in range(4):

        @pl.when(relays_head & (x == part))
        def _():
            for k in range(3):
                head_relay_in(k, part).wait_recv()
                head_relay_out(k, part).start()

    for rep in (0, 1):

        @pl.when(even & (r == rep))
        def _():
            for k in range(3):
                load_own(k, rep).wait()

        @pl.when(odd & (r == rep))
        def _():
            for k in range(3):
                die_copy(k, rep).wait_recv()

    @pl.when(gets_head & (x > 0))
    def _():
        for k in range(3):
            head_copy(k).wait_recv()

    @pl.when(head_unwraps)
    def _():
        for part in range(4):
            for k in range(3):
                head_copy(k, part).wait_recv()

    for rep in (0, 1):

        @pl.when(gets_tail & (r == rep) & (x < 3))
        def _():
            for k in range(3):
                tail_copy(k, rep).wait_recv()

        @pl.when(tail_unwraps & (r == rep))
        def _():
            for part in range(4):
                for k in range(3):
                    tail_copy(k, rep, part).wait_recv()

    my_grads.wait()

    start = within(new_off[s] - old_off[o] + EDGE - 2 * EDGE * core)
    edge_start = within(new_off[s] - old_off[o + 1] + 2 * half)
    split = jnp.where(even, new_off[s + 1], old_off[o + 1])
    flat = new_off[s] + r * half
    stop = new_off[s + 1]

    @pl.loop(0, CHUNKS)
    def _(c):
        grad_copy(c).wait_recv()

        @pl.loop(0, size // SUB)
        def _(j):
            at = c * size + j * SUB
            rows = pl.ds(pl.multiple_of(at, SUB), SUB)
            row = flat + at + lax.broadcasted_iota(jnp.int32, (SUB, 128), 0)
            near = row < split
            keep = row < stop
            master, first, second = [
                jnp.where(near, main[k, pl.ds(start + at, SUB), :], alt[k, pl.ds(edge_start + at, SUB), :])
                for k in range(3)
            ]
            total = mine[rows, :] + theirs[rows, :]
            first_n = 0.9 * first + 0.1 * total
            second_n = 0.95 * second + 0.05 * total * total
            first_hat = first_n / (1.0 - 0.9**STEP)
            second_hat = second_n / (1.0 - 0.95**STEP)
            master_n = master - 0.02 * (first_hat / (jnp.sqrt(second_hat) + 1e-08) + 0.1 * master)
            master_n = jnp.where(keep, master_n, 0.0)
            res[0, rows, :] = master_n
            res[1, rows, :] = jnp.where(keep, first_n, 0.0)
            res[2, rows, :] = jnp.where(keep, second_n, 0.0)
            wts[rows, :] = master_n.astype(jnp.bfloat16)

        wts_copy(c).start()
        own_copy(c).start()
        for k in range(3):
            res_copy(k, c).start()

    for rep in (0, 1):

        @pl.when(even & (r == rep))
        def _():
            for k in range(3):
                die_copy(k, rep).wait_send()

    @pl.when(sends_head & (x < 3))
    def _():
        for k in range(3):
            head_copy(k).wait_send()

    @pl.when(head_wraps)
    def _():
        for part in range(4):
            for k in range(3):
                head_copy(k, part).wait_send()

    @pl.when(relays_head)
    def _():
        for k in range(3):
            head_relay_out(k, 0).wait_send()

    for rep in (0, 1):

        @pl.when(sends_tail & (down_rep == rep) & (x > 0))
        def _():
            for k in range(3):
                tail_copy(k, rep).wait_send()

        @pl.when(tail_wraps & (down_rep == rep))
        def _():
            for part in range(4):
                for k in range(3):
                    tail_copy(k, rep, part).wait_send()

        @pl.when(relays_tail & (tail_rep == rep))
        def _():
            for k in range(3):
                tail_relay_out(k, rep, 0).wait_send()

    @pl.loop(0, CHUNKS)
    def _(c):
        grad_copy(c).wait_send()
        for k in range(3):
            res_copy(k, c).wait()
        own_copy(c).wait()
        wts_copy(c).wait_send()
        wts_arrival(c).wait_recv()


def finish(in_m, in_f, in_s, in_w, out_m, out_f, out_s, out_w, sem):
    pairs = ((in_m, out_m), (in_f, out_f), (in_s, out_s), (in_w, out_w))
    copies = [pltpu.make_async_copy(src, dst, sem.at[i]) for i, (src, dst) in enumerate(pairs)]
    for copy in copies:
        copy.start()
    for copy in copies:
        copy.wait()


def local(old_master, old_first, old_second, grad_parts, old_offsets, new_offsets):
    new_cap, lanes = grad_parts.shape[1:]
    half = new_cap // 2
    hbm = pl.BlockSpec(memory_space=pltpu.HBM)
    free = pl.BlockSpec(memory_space=pl.ANY)
    state = jax.ShapeDtypeStruct((half, lanes), jnp.float32)
    dma = pltpu.SemaphoreType.DMA
    shapes = (state, state, state, jax.ShapeDtypeStruct((new_cap, lanes), jnp.bfloat16))
    results = pl.pallas_call(
        kernel,
        out_shape=shapes,
        in_specs=[hbm] * 6,
        out_specs=(free, free, free, free),
        scratch_shapes=[
            pltpu.SMEM(old_offsets.shape, jnp.int32),
            pltpu.SMEM(new_offsets.shape, jnp.int32),
            pltpu.VMEM((3, WINDOW, lanes), jnp.float32),
            pltpu.VMEM((3, WINDOW, lanes), jnp.float32),
            pltpu.VMEM((2, 3, EDGE // 4, lanes), jnp.float32),
            pltpu.VMEM((3, 3 * EDGE, lanes), jnp.float32),
            pltpu.VMEM((3, EDGE, lanes), jnp.float32),
            pltpu.VMEM((half, lanes), jnp.float32),
            pltpu.VMEM((half, lanes), jnp.float32),
            pltpu.VMEM((3, half, lanes), jnp.float32),
            pltpu.VMEM((half, lanes), jnp.bfloat16),
            dma((2,)),
            dma((3,)),
            dma,
            dma((3,)),
            dma((2, 3)),
            dma((2, 4, 3)),
            dma((2, 4, 3)),
            dma((2, 3)),
            dma((2, 3)),
            dma((CHUNKS,)),
            dma((CHUNKS,)),
            dma((CHUNKS,)),
            dma((CHUNKS,)),
            dma((3, CHUNKS)),
            dma((CHUNKS,)),
        ],
        compiler_params=pltpu.CompilerParams(
            collective_id=0, has_side_effects=True, vmem_limit_bytes=50 * 1024 * 1024
        ),
        name="move_and_update",
    )(old_offsets, new_offsets, old_master, old_first, old_second, grad_parts)
    master, first, second, weights = pl.pallas_call(
        finish,
        out_shape=shapes,
        in_specs=[pl.BlockSpec(memory_space=pltpu.VMEM)] * 4,
        out_specs=(hbm,) * 4,
        scratch_shapes=[dma((4,))],
        name="finish",
    )(*results)
    return (master[None, None], first[None, None], second[None, None], weights)


def solution(mesh):
    in_specs = (
        P("shard", None),
        P("shard", None),
        P("shard", None),
        P("rep", "shard", None),
        P(),
        P(),
    )
    out_specs = (
        P("shard", "rep", None, None),
        P("shard", "rep", None, None),
        P("shard", "rep", None, None),
        P("shard", None),
    )
    return jax.shard_map(local, mesh=mesh, in_specs=in_specs, out_specs=out_specs, check_vma=False)
```

```python
import functools

import jax
import jax.numpy as jnp
from jax import lax
from jax.experimental import pallas as pl
from jax.experimental.pallas import tpu as pltpu
from jax.sharding import PartitionSpec as P

STEP = 10
MESH = pl.DeviceIdType.MESH
JITTER = 512
EDGE = 2 * JITTER
WINDOW = 3584
CHUNKS = 8
SUB = 64


def within(start):
    return jnp.clip(start, 0, 2 * EDGE)


def kernel(
    old_off_in,
    new_off_in,
    old_m,
    old_f,
    old_s,
    grads,
    out_m,
    out_f,
    out_s,
    out_w,
    old_off,
    new_off,
    main,
    alt,
    relay,
    stage_m,
    stage_f,
    stage_s,
    edge,
    mine,
    theirs,
    res,
    wts,
    off_sem,
    in_sem,
    mine_sem,
    stage_sem,
    die_sem,
    head_sem,
    tail_sem,
    head_relay_sem,
    tail_relay_sem,
    grad_send,
    grad_recv,
    wts_send,
    wts_recv,
    res_sem,
    own_sem,
):
    olds = (old_m, old_f, old_s)
    outs = (out_m, out_f, out_s)
    stages = (stage_m, stage_f, stage_s)
    old_cap = old_m.shape[0]
    half = mine.shape[0]
    size = half // CHUNKS
    r = lax.axis_index("rep")
    s = lax.axis_index("shard")
    owners = lax.axis_size("shard") // 2
    o = s // 2
    core = s % 2
    even = core == 0
    odd = core == 1
    other = (1 - r, s)

    x = o % 4

    up_rep = jnp.where(o % 16 == 15, 1 - r, r)
    down_rep = jnp.where(o % 16 == 0, 1 - r, r)
    sends_head = even & (up_rep == 0) & (o < owners - 1)
    gets_head = even & (r == 0) & (o > 0)
    sends_tail = even & (o > 0)
    gets_tail = odd & (o < owners - 1)
    count = 2 * owners
    head_to = (up_rep, lax.rem(s + 2, count))
    head_from = (down_rep, lax.rem(s + count - 2, count))
    tail_to = (down_rep, lax.rem(s + count - 1, count))
    tail_from = (up_rep, lax.rem(s + 1, count))
    die_to = (r, s + 1 - 2 * core)

    z_lo = (o // 4) % 4
    turn_up = jnp.where(z_lo == 3, 32, 0)
    turn_down = jnp.where(z_lo == 0, 32, 0)
    head_wraps = sends_head & (x == 3)
    head_unwraps = gets_head & (x == 0)
    tail_wraps = sends_tail & (x == 0)
    tail_unwraps = gets_tail & (x == 3)
    head_source = s - 1 + 2 * (3 - x) - turn_up
    head_rep = jnp.where(z_lo == 3, 1 - r, r)
    relays_head = odd & (head_rep == 0) & (head_source >= 0)
    tail_source = s - 1 - 2 * x + turn_down
    tail_rep = jnp.where(z_lo == 0, 1 - r, r)
    relays_tail = odd & (tail_source < count)
    head_relays = s + jnp.where(z_lo == 0, 24, -8) + 1
    tail_relays = s + jnp.where(z_lo == 3, -24, 8) - 6

    offsets = (
        pltpu.make_async_copy(old_off_in, old_off, off_sem.at[0]),
        pltpu.make_async_copy(new_off_in, new_off, off_sem.at[1]),
    )
    for copy in offsets:
        copy.start()
    my_grads = pltpu.make_async_copy(grads.at[0, pl.ds(r * half, half)], mine, mine_sem)

    def load_own(k, rep):
        if rep == 0:
            return pltpu.make_async_copy(
                olds[k].at[pl.ds(0, WINDOW - EDGE)], main.at[k, pl.ds(EDGE, WINDOW - EDGE)], in_sem.at[k]
            )
        return pltpu.make_async_copy(olds[k].at[pl.ds(JITTER, WINDOW)], main.at[k], in_sem.at[k])

    def load_stage(k):
        rows = stage_m.shape[0]
        return pltpu.make_async_copy(olds[k].at[pl.ds(old_cap - rows, rows)], stages[k], stage_sem.at[k])

    def die_copy(k, rep):
        first = 1024 if rep == 0 else 2560
        rows = min(WINDOW, old_cap - first)
        return pltpu.make_async_remote_copy(
            olds[k].at[pl.ds(first, rows)],
            main.at[k, pl.ds(0, rows)],
            die_sem.at[0, k],
            die_sem.at[1, k],
            device_id=die_to,
            device_id_type=MESH,
        )

    def send(src, dst, sems, to):
        return pltpu.make_async_remote_copy(src, dst, sems[0], sems[1], device_id=to, device_id_type=MESH)

    quarter = EDGE // 4

    def head_copy(k, part=None):
        rows = pl.ds(0, EDGE) if part is None else pl.ds(part * quarter, quarter)
        at = 0 if part is None else part
        sems = (head_sem.at[0, at, k], head_sem.at[1, at, k])
        return send(edge.at[k, rows], main.at[k, rows], sems, head_to)

    def head_relay_in(k, part):
        rows = pl.ds(part * quarter, quarter)
        sems = (head_sem.at[0, part, k], head_relay_sem.at[0, k])
        to = (r, lax.rem(s - 2 * (3 - part) + 1 + turn_up + count, count))
        return send(edge.at[k, rows], relay.at[0, k], sems, to)

    def head_relay_out(k, part):
        rows = pl.ds(part * quarter, quarter)
        sems = (head_relay_sem.at[1, k], head_sem.at[1, part, k])
        return send(relay.at[0, k], main.at[k, rows], sems, (head_rep, lax.rem(head_source + 2, count)))

    def tail_place(rep):
        return (3072, JITTER) if rep == 0 else (1536, EDGE)

    def tail_copy(k, rep, part=None):
        first, rows = tail_place(rep)
        begin = 0
        if part is not None:
            rows //= 4
            begin = part * rows
        at = 0 if part is None else part
        sems = (tail_sem.at[0, at, k], tail_sem.at[1, at, k])
        return send(olds[k].at[pl.ds(begin, rows)], alt.at[k, pl.ds(first + begin, rows)], sems, tail_to)

    def tail_relay_in(k, rep, part):
        rows = tail_place(rep)[1] // 4
        sems = (tail_sem.at[0, part, k], tail_relay_sem.at[0, k])
        to = (r, lax.rem(s + 2 * part + 1 - turn_down + count, count))
        return send(olds[k].at[pl.ds(part * rows, rows)], relay.at[1, k, pl.ds(0, rows)], sems, to)

    def tail_relay_out(k, rep, part):
        first, rows = tail_place(rep)
        rows //= 4
        sems = (tail_relay_sem.at[1, k], tail_sem.at[1, part, k])
        to = (tail_rep, lax.rem(tail_source + count - 1, count))
        return send(relay.at[1, k, pl.ds(0, rows)], alt.at[k, pl.ds(first + part * rows, rows)], sems, to)

    def grad_copy(c):
        first = pl.multiple_of(c * size, 16)
        return pltpu.make_async_remote_copy(
            grads.at[0, pl.ds(pl.multiple_of((1 - r) * half + first, 16), size)],
            theirs.at[pl.ds(first, size)],
            grad_send.at[c],
            grad_recv.at[c],
            device_id=other,
            device_id_type=MESH,
        )

    def wts_copy(c):
        first = pl.multiple_of(c * size, 16)
        return pltpu.make_async_remote_copy(
            wts.at[pl.ds(first, size)],
            out_w.at[pl.ds(pl.multiple_of(r * half + first, 16), size)],
            wts_send.at[c],
            wts_recv.at[c],
            device_id=other,
            device_id_type=MESH,
        )

    def wts_arrival(c):
        first = pl.multiple_of(c * size, 16)
        return pltpu.make_async_remote_copy(
            wts.at[pl.ds(first, size)],
            out_w.at[pl.ds(pl.multiple_of((1 - r) * half + first, 16), size)],
            wts_send.at[c],
            wts_recv.at[c],
            device_id=other,
            device_id_type=MESH,
        )

    def own_copy(c):
        first = pl.multiple_of(c * size, 16)
        return pltpu.make_async_copy(
            wts.at[pl.ds(first, size)],
            out_w.at[pl.ds(pl.multiple_of(r * half + first, 16), size)],
            own_sem.at[c],
        )

    def res_copy(k, c):
        first = pl.multiple_of(c * size, 16)
        return pltpu.make_async_copy(
            res.at[k, pl.ds(first, size)], outs[k].at[pl.ds(first, size)], res_sem.at[k, c]
        )

    barrier = pltpu.get_barrier_semaphore()
    pl.semaphore_signal(barrier, inc=1, device_id=other, device_id_type=MESH)

    @pl.when(odd)
    def _():
        pl.semaphore_signal(barrier, inc=1, device_id=die_to, device_id_type=MESH)

    @pl.when(gets_head & (x > 0))
    def _():
        pl.semaphore_signal(barrier, inc=1, device_id=head_from, device_id_type=MESH)

    @pl.when(head_unwraps)
    def _():
        for part in range(4):
            at = lax.rem(head_relays + 2 * part + count, count)
            pl.semaphore_signal(barrier, inc=1, device_id=(down_rep, at), device_id_type=MESH)

    @pl.when(gets_tail & (x < 3))
    def _():
        pl.semaphore_signal(barrier, inc=1, device_id=tail_from, device_id_type=MESH)

    @pl.when(tail_unwraps)
    def _():
        for part in range(4):
            at = lax.rem(tail_relays + 2 * part + count, count)
            pl.semaphore_signal(barrier, inc=1, device_id=(up_rep, at), device_id_type=MESH)

    @pl.when(relays_head)
    def _():
        pl.semaphore_signal(barrier, inc=1, device_id=(r, lax.rem(head_source + count, count)), device_id_type=MESH)

    @pl.when(relays_tail)
    def _():
        pl.semaphore_signal(barrier, inc=1, device_id=(r, lax.rem(tail_source, count)), device_id_type=MESH)

    @pl.when(sends_head)
    def _():
        for k in range(3):
            load_stage(k).start()

    targets = 1
    for cond, more in (
        (even, 1),
        (sends_head, 1),
        (head_wraps, 3),
        (sends_tail, 1),
        (tail_wraps, 3),
        (relays_head, 1),
        (relays_tail, 1),
    ):
        targets = targets + more * cond.astype(jnp.int32)
    pl.semaphore_wait(barrier, targets)

    for rep in (0, 1):

        @pl.when(sends_tail & (down_rep == rep) & (x > 0))
        def _():
            for k in range(3):
                tail_copy(k, rep).start()

        @pl.when(tail_wraps & (down_rep == rep))
        def _():
            for part in range(4):
                for k in range(3):
                    tail_relay_in(k, rep, part).start()

    @pl.loop(0, CHUNKS)
    def _(c):
        grad_copy(c).start()

    for rep in (0, 1):

        @pl.when(even & (r == rep))
        def _():
            for k in range(3):
                die_copy(k, rep).start()

    for copy in offsets:
        copy.wait()

    for rep in (0, 1):

        @pl.when(even & (r == rep))
        def _():
            for k in range(3):
                load_own(k, rep).start()

    my_grads.start()

    @pl.when(sends_head)
    def _():
        begin = within(old_off[o + 1] - old_off[o] - (old_cap - stage_m.shape[0]) - EDGE)
        for k in range(3):
            load_stage(k).wait()

            @pl.loop(0, EDGE // SUB)
            def _(j):
                edge[k, pl.ds(pl.multiple_of(j * SUB, SUB), SUB), :] = stages[k][pl.ds(begin + j * SUB, SUB), :]

            @pl.when(x < 3)
            def _():
                head_copy(k).start()

            @pl.when(x == 3)
            def _():
                for part in range(4):
                    head_relay_in(k, part).start()

    for rep in (0, 1):
        for part in range(4):

            @pl.when(relays_tail & (tail_rep == rep) & (x == part))
            def _():
                for k in range(3):
                    tail_relay_in(k, rep, part).wait_recv()
                    tail_relay_out(k, rep, part).start()

    for part in range(4):

        @pl.when(relays_head & (x == part))
        def _():
            for k in range(3):
                head_relay_in(k, part).wait_recv()
                head_relay_out(k, part).start()

    for rep in (0, 1):

        @pl.when(even & (r == rep))
        def _():
            for k in range(3):
                load_own(k, rep).wait()

        @pl.when(odd & (r == rep))
        def _():
            for k in range(3):
                die_copy(k, rep).wait_recv()

    @pl.when(gets_head & (x > 0))
    def _():
        for k in range(3):
            head_copy(k).wait_recv()

    @pl.when(head_unwraps)
    def _():
        for part in range(4):
            for k in range(3):
                head_copy(k, part).wait_recv()

    for rep in (0, 1):

        @pl.when(gets_tail & (r == rep) & (x < 3))
        def _():
            for k in range(3):
                tail_copy(k, rep).wait_recv()

        @pl.when(tail_unwraps & (r == rep))
        def _():
            for part in range(4):
                for k in range(3):
                    tail_copy(k, rep, part).wait_recv()

    my_grads.wait()

    start = within(new_off[s] - old_off[o] + EDGE - 2 * EDGE * core)
    edge_start = within(new_off[s] - old_off[o + 1] + 2 * half)
    split = jnp.where(even, new_off[s + 1], old_off[o + 1])
    flat = new_off[s] + r * half
    stop = new_off[s + 1]

    @pl.loop(0, CHUNKS)
    def _(c):
        grad_copy(c).wait_recv()

        @pl.loop(0, size // SUB)
        def _(j):
            at = c * size + j * SUB
            rows = pl.ds(pl.multiple_of(at, SUB), SUB)
            row = flat + at + lax.broadcasted_iota(jnp.int32, (SUB, 128), 0)
            near = row < split
            keep = row < stop
            master, first, second = [
                jnp.where(near, main[k, pl.ds(start + at, SUB), :], alt[k, pl.ds(edge_start + at, SUB), :])
                for k in range(3)
            ]
            total = mine[rows, :] + theirs[rows, :]
            first_n = 0.9 * first + 0.1 * total
            second_n = 0.95 * second + 0.05 * total * total
            first_hat = first_n / (1.0 - 0.9**STEP)
            second_hat = second_n / (1.0 - 0.95**STEP)
            master_n = master - 0.02 * (first_hat / (jnp.sqrt(second_hat) + 1e-08) + 0.1 * master)
            master_n = jnp.where(keep, master_n, 0.0)
            res[0, rows, :] = master_n
            res[1, rows, :] = jnp.where(keep, first_n, 0.0)
            res[2, rows, :] = jnp.where(keep, second_n, 0.0)
            wts[rows, :] = master_n.astype(jnp.bfloat16)

        wts_copy(c).start()
        own_copy(c).start()
        for k in range(3):
            res_copy(k, c).start()

    for rep in (0, 1):

        @pl.when(even & (r == rep))
        def _():
            for k in range(3):
                die_copy(k, rep).wait_send()

    @pl.when(sends_head & (x < 3))
    def _():
        for k in range(3):
            head_copy(k).wait_send()

    @pl.when(head_wraps)
    def _():
        for part in range(4):
            for k in range(3):
                head_copy(k, part).wait_send()

    @pl.when(relays_head)
    def _():
        for k in range(3):
            head_relay_out(k, 0).wait_send()

    for rep in (0, 1):

        @pl.when(sends_tail & (down_rep == rep) & (x > 0))
        def _():
            for k in range(3):
                tail_copy(k, rep).wait_send()

        @pl.when(tail_wraps & (down_rep == rep))
        def _():
            for part in range(4):
                for k in range(3):
                    tail_copy(k, rep, part).wait_send()

        @pl.when(relays_tail & (tail_rep == rep))
        def _():
            for k in range(3):
                tail_relay_out(k, rep, 0).wait_send()

    @pl.loop(0, CHUNKS)
    def _(c):
        grad_copy(c).wait_send()
        for k in range(3):
            res_copy(k, c).wait()
        own_copy(c).wait()
        wts_copy(c).wait_send()
        wts_arrival(c).wait_recv()


def finish(in_m, in_f, in_s, in_w, out_m, out_f, out_s, out_w, vm, vf, vs, vw, in_sem, out_sem):
    ins, holds, outs = (in_m, in_f, in_s, in_w), (vm, vf, vs, vw), (out_m, out_f, out_s, out_w)
    loads = [pltpu.make_async_copy(ins[i], holds[i], in_sem.at[i]) for i in range(4)]
    stores = [pltpu.make_async_copy(holds[i], outs[i], out_sem.at[i]) for i in range(4)]
    for load in loads:
        load.start()
    for load, store in zip(loads, stores):
        load.wait()
        store.start()
    for store in stores:
        store.wait()


def local(old_master, old_first, old_second, grad_parts, old_offsets, new_offsets):
    new_cap, lanes = grad_parts.shape[1:]
    half = new_cap // 2
    hbm = pl.BlockSpec(memory_space=pltpu.HBM)
    free = pl.BlockSpec(memory_space=pl.ANY)
    state = jax.ShapeDtypeStruct((half, lanes), jnp.float32)
    dma = pltpu.SemaphoreType.DMA
    shapes = (state, state, state, jax.ShapeDtypeStruct((new_cap, lanes), jnp.bfloat16))
    results = pl.pallas_call(
        kernel,
        out_shape=shapes,
        in_specs=[hbm] * 6,
        out_specs=(free, free, free, free),
        scratch_shapes=[
            pltpu.SMEM(old_offsets.shape, jnp.int32),
            pltpu.SMEM(new_offsets.shape, jnp.int32),
            pltpu.VMEM((3, WINDOW, lanes), jnp.float32),
            pltpu.VMEM((3, WINDOW, lanes), jnp.float32),
            pltpu.VMEM((2, 3, EDGE // 4, lanes), jnp.float32),
            pltpu.VMEM((3 * EDGE, lanes), jnp.float32),
            pltpu.VMEM((3 * EDGE, lanes), jnp.float32),
            pltpu.VMEM((3 * EDGE, lanes), jnp.float32),
            pltpu.VMEM((3, EDGE, lanes), jnp.float32),
            pltpu.VMEM((half, lanes), jnp.float32),
            pltpu.VMEM((half, lanes), jnp.float32),
            pltpu.VMEM((3, half, lanes), jnp.float32),
            pltpu.VMEM((half, lanes), jnp.bfloat16),
            dma((2,)),
            dma((3,)),
            dma,
            dma((3,)),
            dma((2, 3)),
            dma((2, 4, 3)),
            dma((2, 4, 3)),
            dma((2, 3)),
            dma((2, 3)),
            dma((CHUNKS,)),
            dma((CHUNKS,)),
            dma((CHUNKS,)),
            dma((CHUNKS,)),
            dma((3, CHUNKS)),
            dma((CHUNKS,)),
        ],
        compiler_params=pltpu.CompilerParams(
            collective_id=0, has_side_effects=True, vmem_limit_bytes=60 * 1024 * 1024
        ),
        name="move_and_update",
    )(old_offsets, new_offsets, old_master, old_first, old_second, grad_parts)
    master, first, second, weights = pl.pallas_call(
        finish,
        out_shape=shapes,
        in_specs=[hbm] * 4,
        out_specs=(hbm,) * 4,
        scratch_shapes=[pltpu.VMEM(shape.shape, shape.dtype) for shape in shapes] + [dma((4,)), dma((4,))],
        compiler_params=pltpu.CompilerParams(vmem_limit_bytes=60 * 1024 * 1024),
        name="finish",
    )(*results)
    return (master[None, None], first[None, None], second[None, None], weights)


def solution(mesh):
    in_specs = (
        P("shard", None),
        P("shard", None),
        P("shard", None),
        P("rep", "shard", None),
        P(),
        P(),
    )
    out_specs = (
        P("shard", "rep", None, None),
        P("shard", "rep", None, None),
        P("shard", "rep", None, None),
        P("shard", None),
    )
    return jax.shard_map(local, mesh=mesh, in_specs=in_specs, out_specs=out_specs, check_vma=False)
```

```python
import functools

import jax
import jax.numpy as jnp
from jax import lax
from jax.experimental import pallas as pl
from jax.experimental.pallas import tpu as pltpu
from jax.sharding import PartitionSpec as P

STEP = 10
MESH = pl.DeviceIdType.MESH
JITTER = 512
EDGE = 2 * JITTER
WINDOW = 3584
CHUNKS = 8
SUB = 64
EARLY = 3


def within(start):
    return jnp.clip(start, 0, 2 * EDGE)


def kernel(
    old_off_in,
    new_off_in,
    old_m,
    old_f,
    old_s,
    grads,
    out_m,
    out_f,
    out_s,
    out_w,
    old_off,
    new_off,
    main,
    alt,
    relay,
    stage_m,
    stage_f,
    stage_s,
    edge,
    mine,
    theirs,
    res,
    wts,
    off_sem,
    in_sem,
    mine_sem,
    stage_sem,
    die_sem,
    head_sem,
    tail_sem,
    head_relay_sem,
    tail_relay_sem,
    grad_send,
    grad_recv,
    wts_send,
    wts_recv,
    res_sem,
    own_sem,
):
    olds = (old_m, old_f, old_s)
    outs = (out_m, out_f, out_s)
    stages = (stage_m, stage_f, stage_s)
    old_cap = old_m.shape[0]
    half = mine.shape[0]
    size = half // CHUNKS
    r = lax.axis_index("rep")
    s = lax.axis_index("shard")
    owners = lax.axis_size("shard") // 2
    o = s // 2
    core = s % 2
    even = core == 0
    odd = core == 1
    other = (1 - r, s)

    x = o % 4

    up_rep = r
    down_rep = r
    sends_head = even & (up_rep == 0) & (o < owners - 1)
    gets_head = even & (r == 0) & (o > 0)
    sends_tail = even & (o > 0)
    gets_tail = odd & (o < owners - 1)
    count = 2 * owners
    head_to = (up_rep, lax.rem(s + 2, count))
    head_from = (down_rep, lax.rem(s + count - 2, count))
    tail_to = (down_rep, lax.rem(s + count - 1, count))
    tail_from = (up_rep, lax.rem(s + 1, count))
    die_to = (r, s + 1 - 2 * core)

    z_lo = (o // 4) % 4
    turn_up = jnp.where(z_lo == 3, 32, 0)
    turn_down = jnp.where(z_lo == 0, 32, 0)
    head_wraps = sends_head & (x == 3)
    head_unwraps = gets_head & (x == 0)
    tail_wraps = sends_tail & (x == 0)
    tail_unwraps = gets_tail & (x == 3)
    head_source = s - 1 + 2 * (3 - x) - turn_up
    head_rep = r
    relays_head = odd & (head_rep == 0) & (head_source >= 0)
    tail_source = s - 1 - 2 * x + turn_down
    tail_rep = r
    relays_tail = odd & (tail_source < count)
    head_relays = s + jnp.where(z_lo == 0, 24, -8) + 1
    tail_relays = s + jnp.where(z_lo == 3, -24, 8) - 6

    offsets = (
        pltpu.make_async_copy(old_off_in, old_off, off_sem.at[0]),
        pltpu.make_async_copy(new_off_in, new_off, off_sem.at[1]),
    )
    for copy in offsets:
        copy.start()
    my_grads = pltpu.make_async_copy(grads.at[0, pl.ds(r * half, half)], mine, mine_sem)

    def load_own(k, rep):
        if rep == 0:
            return pltpu.make_async_copy(
                olds[k].at[pl.ds(0, WINDOW - EDGE)], main.at[k, pl.ds(EDGE, WINDOW - EDGE)], in_sem.at[k]
            )
        return pltpu.make_async_copy(olds[k].at[pl.ds(JITTER, WINDOW)], main.at[k], in_sem.at[k])

    def load_stage(k):
        rows = stage_m.shape[0]
        return pltpu.make_async_copy(olds[k].at[pl.ds(old_cap - rows, rows)], stages[k], stage_sem.at[k])

    def die_copy(k, rep):
        first = 1024 if rep == 0 else 2560
        rows = min(WINDOW, old_cap - first)
        return pltpu.make_async_remote_copy(
            olds[k].at[pl.ds(first, rows)],
            main.at[k, pl.ds(0, rows)],
            die_sem.at[0, k],
            die_sem.at[1, k],
            device_id=die_to,
            device_id_type=MESH,
        )

    def send(src, dst, sems, to):
        return pltpu.make_async_remote_copy(src, dst, sems[0], sems[1], device_id=to, device_id_type=MESH)

    quarter = EDGE // 4

    def head_copy(k, part=None):
        rows = pl.ds(0, EDGE) if part is None else pl.ds(part * quarter, quarter)
        at = 0 if part is None else part
        sems = (head_sem.at[0, at, k], head_sem.at[1, at, k])
        return send(edge.at[k, rows], main.at[k, rows], sems, head_to)

    def head_relay_in(k, part):
        rows = pl.ds(part * quarter, quarter)
        sems = (head_sem.at[0, part, k], head_relay_sem.at[0, k])
        to = (r, lax.rem(s - 2 * (3 - part) + 1 + turn_up + count, count))
        return send(edge.at[k, rows], relay.at[0, k], sems, to)

    def head_relay_out(k, part):
        rows = pl.ds(part * quarter, quarter)
        sems = (head_relay_sem.at[1, k], head_sem.at[1, part, k])
        return send(relay.at[0, k], main.at[k, rows], sems, (head_rep, lax.rem(head_source + 2, count)))

    def tail_place(rep):
        return (3072, JITTER) if rep == 0 else (1536, EDGE)

    def tail_copy(k, rep, part=None):
        first, rows = tail_place(rep)
        begin = 0
        if part is not None:
            rows //= 4
            begin = part * rows
        at = 0 if part is None else part
        sems = (tail_sem.at[0, at, k], tail_sem.at[1, at, k])
        return send(olds[k].at[pl.ds(begin, rows)], alt.at[k, pl.ds(first + begin, rows)], sems, tail_to)

    def tail_relay_in(k, rep, part):
        rows = tail_place(rep)[1] // 4
        sems = (tail_sem.at[0, part, k], tail_relay_sem.at[0, k])
        to = (r, lax.rem(s + 2 * part + 1 - turn_down + count, count))
        return send(olds[k].at[pl.ds(part * rows, rows)], relay.at[1, k, pl.ds(0, rows)], sems, to)

    def tail_relay_out(k, rep, part):
        first, rows = tail_place(rep)
        rows //= 4
        sems = (tail_relay_sem.at[1, k], tail_sem.at[1, part, k])
        to = (tail_rep, lax.rem(tail_source + count - 1, count))
        return send(relay.at[1, k, pl.ds(0, rows)], alt.at[k, pl.ds(first + part * rows, rows)], sems, to)

    def grad_copy(c):
        first = pl.multiple_of(c * size, 16)
        return pltpu.make_async_remote_copy(
            grads.at[0, pl.ds(pl.multiple_of((1 - r) * half + first, 16), size)],
            theirs.at[pl.ds(first, size)],
            grad_send.at[c],
            grad_recv.at[c],
            device_id=other,
            device_id_type=MESH,
        )

    def wts_copy(c):
        first = pl.multiple_of(c * size, 16)
        return pltpu.make_async_remote_copy(
            wts.at[pl.ds(first, size)],
            out_w.at[pl.ds(pl.multiple_of(r * half + first, 16), size)],
            wts_send.at[c],
            wts_recv.at[c],
            device_id=other,
            device_id_type=MESH,
        )

    def wts_arrival(c):
        first = pl.multiple_of(c * size, 16)
        return pltpu.make_async_remote_copy(
            wts.at[pl.ds(first, size)],
            out_w.at[pl.ds(pl.multiple_of((1 - r) * half + first, 16), size)],
            wts_send.at[c],
            wts_recv.at[c],
            device_id=other,
            device_id_type=MESH,
        )

    def own_copy(c):
        first = pl.multiple_of(c * size, 16)
        return pltpu.make_async_copy(
            wts.at[pl.ds(first, size)],
            out_w.at[pl.ds(pl.multiple_of(r * half + first, 16), size)],
            own_sem.at[c],
        )

    def res_copy(k, c):
        first = pl.multiple_of(c * size, 16)
        return pltpu.make_async_copy(
            res.at[k, pl.ds(first, size)], outs[k].at[pl.ds(first, size)], res_sem.at[k, c]
        )

    @pl.when(sends_head)
    def _():
        for k in range(3):
            load_stage(k).start()

    barrier = pltpu.get_barrier_semaphore()
    pl.semaphore_signal(barrier, inc=1, device_id=other, device_id_type=MESH)

    @pl.when(odd)
    def _():
        pl.semaphore_signal(barrier, inc=1, device_id=die_to, device_id_type=MESH)

    @pl.when(gets_head & (x > 0))
    def _():
        pl.semaphore_signal(barrier, inc=1, device_id=head_from, device_id_type=MESH)

    @pl.when(head_unwraps)
    def _():
        for part in range(4):
            at = lax.rem(head_relays + 2 * part + count, count)
            pl.semaphore_signal(barrier, inc=1, device_id=(down_rep, at), device_id_type=MESH)

    @pl.when(gets_tail & (x < 3))
    def _():
        pl.semaphore_signal(barrier, inc=1, device_id=tail_from, device_id_type=MESH)

    @pl.when(tail_unwraps)
    def _():
        for part in range(4):
            at = lax.rem(tail_relays + 2 * part + count, count)
            pl.semaphore_signal(barrier, inc=1, device_id=(up_rep, at), device_id_type=MESH)

    @pl.when(relays_head)
    def _():
        pl.semaphore_signal(barrier, inc=1, device_id=(r, lax.rem(head_source + count, count)), device_id_type=MESH)

    @pl.when(relays_tail)
    def _():
        pl.semaphore_signal(barrier, inc=1, device_id=(r, lax.rem(tail_source, count)), device_id_type=MESH)

    targets = 1
    for cond, more in (
        (even, 1),
        (sends_head, 1),
        (head_wraps, 3),
        (sends_tail, 1),
        (tail_wraps, 3),
        (relays_head, 1),
        (relays_tail, 1),
    ):
        targets = targets + more * cond.astype(jnp.int32)
    pl.semaphore_wait(barrier, targets)

    for rep in (0, 1):

        @pl.when(sends_tail & (down_rep == rep) & (x > 0))
        def _():
            for k in range(3):
                tail_copy(k, rep).start()

        @pl.when(tail_wraps & (down_rep == rep))
        def _():
            for part in range(4):
                for k in range(3):
                    tail_relay_in(k, rep, part).start()

    early = jnp.where(odd, EARLY, CHUNKS)

    @pl.loop(0, early)
    def _(c):
        grad_copy(c).start()

    for copy in offsets:
        copy.wait()

    @pl.when(sends_head)
    def _():
        begin = within(old_off[o + 1] - old_off[o] - (old_cap - stage_m.shape[0]) - EDGE)
        for k in range(3):
            load_stage(k).wait()

            @pl.loop(0, EDGE // SUB)
            def _(j):
                edge[k, pl.ds(pl.multiple_of(j * SUB, SUB), SUB), :] = stages[k][pl.ds(begin + j * SUB, SUB), :]

            @pl.when(x < 3)
            def _():
                head_copy(k).start()

            @pl.when(x == 3)
            def _():
                for part in range(4):
                    head_relay_in(k, part).start()

    for rep in (0, 1):

        @pl.when(even & (r == rep))
        def _():
            for k in range(3):
                die_copy(k, rep).start()

    for rep in (0, 1):

        @pl.when(even & (r == rep))
        def _():
            for k in range(3):
                load_own(k, rep).start()

    my_grads.start()

    for rep in (0, 1):
        for part in range(4):

            @pl.when(relays_tail & (tail_rep == rep) & (x == part))
            def _():
                for k in range(3):
                    tail_relay_in(k, rep, part).wait_recv()
                    tail_relay_out(k, rep, part).start()

    for part in range(4):

        @pl.when(relays_head & (x == part))
        def _():
            for k in range(3):
                head_relay_in(k, part).wait_recv()
                head_relay_out(k, part).start()

    @pl.loop(early, CHUNKS)
    def _(c):
        grad_copy(c).start()

    for rep in (0, 1):

        @pl.when(even & (r == rep))
        def _():
            for k in range(3):
                load_own(k, rep).wait()

        @pl.when(odd & (r == rep))
        def _():
            for k in range(3):
                die_copy(k, rep).wait_recv()

    @pl.when(gets_head & (x > 0))
    def _():
        for k in range(3):
            head_copy(k).wait_recv()

    @pl.when(head_unwraps)
    def _():
        for part in range(4):
            for k in range(3):
                head_copy(k, part).wait_recv()

    for rep in (0, 1):

        @pl.when(gets_tail & (r == rep) & (x < 3))
        def _():
            for k in range(3):
                tail_copy(k, rep).wait_recv()

        @pl.when(tail_unwraps & (r == rep))
        def _():
            for part in range(4):
                for k in range(3):
                    tail_copy(k, rep, part).wait_recv()

    my_grads.wait()

    start = within(new_off[s] - old_off[o] + EDGE - 2 * EDGE * core)
    edge_start = within(new_off[s] - old_off[o + 1] + 2 * half)
    split = jnp.where(even, new_off[s + 1], old_off[o + 1])
    flat = new_off[s] + r * half
    stop = new_off[s + 1]

    @pl.loop(0, CHUNKS)
    def _(c):
        grad_copy(c).wait_recv()

        @pl.loop(0, size // SUB)
        def _(j):
            at = c * size + j * SUB
            rows = pl.ds(pl.multiple_of(at, SUB), SUB)
            row = flat + at + lax.broadcasted_iota(jnp.int32, (SUB, 128), 0)
            near = row < split
            keep = row < stop
            master, first, second = [
                jnp.where(near, main[k, pl.ds(start + at, SUB), :], alt[k, pl.ds(edge_start + at, SUB), :])
                for k in range(3)
            ]
            total = mine[rows, :] + theirs[rows, :]
            first_n = 0.9 * first + 0.1 * total
            second_n = 0.95 * second + 0.05 * total * total
            first_hat = first_n / (1.0 - 0.9**STEP)
            second_hat = second_n / (1.0 - 0.95**STEP)
            master_n = master - 0.02 * (first_hat / (jnp.sqrt(second_hat) + 1e-08) + 0.1 * master)
            master_n = jnp.where(keep, master_n, 0.0)
            res[0, rows, :] = master_n
            res[1, rows, :] = jnp.where(keep, first_n, 0.0)
            res[2, rows, :] = jnp.where(keep, second_n, 0.0)
            wts[rows, :] = master_n.astype(jnp.bfloat16)

        wts_copy(c).start()
        own_copy(c).start()
        for k in range(3):
            res_copy(k, c).start()

    for rep in (0, 1):

        @pl.when(even & (r == rep))
        def _():
            for k in range(3):
                die_copy(k, rep).wait_send()

    @pl.when(sends_head & (x < 3))
    def _():
        for k in range(3):
            head_copy(k).wait_send()

    @pl.when(head_wraps)
    def _():
        for part in range(4):
            for k in range(3):
                head_copy(k, part).wait_send()

    @pl.when(relays_head)
    def _():
        for k in range(3):
            head_relay_out(k, 0).wait_send()

    for rep in (0, 1):

        @pl.when(sends_tail & (down_rep == rep) & (x > 0))
        def _():
            for k in range(3):
                tail_copy(k, rep).wait_send()

        @pl.when(tail_wraps & (down_rep == rep))
        def _():
            for part in range(4):
                for k in range(3):
                    tail_copy(k, rep, part).wait_send()

        @pl.when(relays_tail & (tail_rep == rep))
        def _():
            for k in range(3):
                tail_relay_out(k, rep, 0).wait_send()

    @pl.loop(0, CHUNKS)
    def _(c):
        grad_copy(c).wait_send()
        for k in range(3):
            res_copy(k, c).wait()
        own_copy(c).wait()
        wts_copy(c).wait_send()
        wts_arrival(c).wait_recv()


def finish(in_m, in_f, in_s, in_w, out_m, out_f, out_s, out_w, vm, vf, vs, vw, in_sem, out_sem):
    ins, holds, outs = (in_m, in_f, in_s, in_w), (vm, vf, vs, vw), (out_m, out_f, out_s, out_w)
    loads = [pltpu.make_async_copy(ins[i], holds[i], in_sem.at[i]) for i in range(4)]
    stores = [pltpu.make_async_copy(holds[i], outs[i], out_sem.at[i]) for i in range(4)]
    for load in loads:
        load.start()
    for load, store in zip(loads, stores):
        load.wait()
        store.start()
    for store in stores:
        store.wait()


def local(old_master, old_first, old_second, grad_parts, old_offsets, new_offsets):
    new_cap, lanes = grad_parts.shape[1:]
    half = new_cap // 2
    hbm = pl.BlockSpec(memory_space=pltpu.HBM)
    free = pl.BlockSpec(memory_space=pl.ANY)
    state = jax.ShapeDtypeStruct((half, lanes), jnp.float32)
    dma = pltpu.SemaphoreType.DMA
    shapes = (state, state, state, jax.ShapeDtypeStruct((new_cap, lanes), jnp.bfloat16))
    results = pl.pallas_call(
        kernel,
        out_shape=shapes,
        in_specs=[hbm] * 6,
        out_specs=(free, free, free, free),
        scratch_shapes=[
            pltpu.SMEM(old_offsets.shape, jnp.int32),
            pltpu.SMEM(new_offsets.shape, jnp.int32),
            pltpu.VMEM((3, WINDOW, lanes), jnp.float32),
            pltpu.VMEM((3, WINDOW, lanes), jnp.float32),
            pltpu.VMEM((2, 3, EDGE // 4, lanes), jnp.float32),
            pltpu.VMEM((3 * EDGE, lanes), jnp.float32),
            pltpu.VMEM((3 * EDGE, lanes), jnp.float32),
            pltpu.VMEM((3 * EDGE, lanes), jnp.float32),
            pltpu.VMEM((3, EDGE, lanes), jnp.float32),
            pltpu.VMEM((half, lanes), jnp.float32),
            pltpu.VMEM((half, lanes), jnp.float32),
            pltpu.VMEM((3, half, lanes), jnp.float32),
            pltpu.VMEM((half, lanes), jnp.bfloat16),
            dma((2,)),
            dma((3,)),
            dma,
            dma((3,)),
            dma((2, 3)),
            dma((2, 4, 3)),
            dma((2, 4, 3)),
            dma((2, 3)),
            dma((2, 3)),
            dma((CHUNKS,)),
            dma((CHUNKS,)),
            dma((CHUNKS,)),
            dma((CHUNKS,)),
            dma((3, CHUNKS)),
            dma((CHUNKS,)),
        ],
        compiler_params=pltpu.CompilerParams(
            collective_id=0, has_side_effects=True, vmem_limit_bytes=60 * 1024 * 1024
        ),
        name="move_and_update",
    )(old_offsets, new_offsets, old_master, old_first, old_second, grad_parts)
    master, first, second, weights = pl.pallas_call(
        finish,
        out_shape=shapes,
        in_specs=[hbm] * 4,
        out_specs=(hbm,) * 4,
        scratch_shapes=[pltpu.VMEM(shape.shape, shape.dtype) for shape in shapes] + [dma((4,)), dma((4,))],
        compiler_params=pltpu.CompilerParams(vmem_limit_bytes=60 * 1024 * 1024),
        name="finish",
    )(*results)
    return (master[None, None], first[None, None], second[None, None], weights)


def solution(mesh):
    in_specs = (
        P("shard", None),
        P("shard", None),
        P("shard", None),
        P("rep", "shard", None),
        P(),
        P(),
    )
    out_specs = (
        P("shard", "rep", None, None),
        P("shard", "rep", None, None),
        P("shard", "rep", None, None),
        P("shard", None),
    )
    return jax.shard_map(local, mesh=mesh, in_specs=in_specs, out_specs=out_specs, check_vma=False)
```

```python
import functools

import jax
import jax.numpy as jnp
from jax import lax
from jax.experimental import pallas as pl
from jax.experimental.pallas import tpu as pltpu
from jax.sharding import PartitionSpec as P

STEP = 10
MESH = pl.DeviceIdType.MESH
JITTER = 512
EDGE = 2 * JITTER
PACK = 1024
WINDOW = 3584
CHUNKS = 8
SUB = 64
EARLY = 4


def within(start):
    return jnp.clip(start, 0, 2 * EDGE)


def kernel(
    old_off_in,
    new_off_in,
    old_m,
    old_f,
    old_s,
    grads,
    out_m,
    out_f,
    out_s,
    out_w,
    old_off,
    new_off,
    main,
    alt,
    relay,
    stage_m,
    stage_f,
    stage_s,
    edge,
    mine,
    theirs,
    near_grads,
    far_grads,
    pack,
    packed,
    res,
    wts,
    off_sem,
    in_sem,
    mine_sem,
    stage_sem,
    die_sem,
    head_sem,
    tail_sem,
    head_relay_sem,
    tail_relay_sem,
    pack_sem,
    pass_sem,
    grad_send,
    grad_recv,
    wts_send,
    wts_recv,
    res_sem,
    own_sem,
):
    olds = (old_m, old_f, old_s)
    outs = (out_m, out_f, out_s)
    stages = (stage_m, stage_f, stage_s)
    old_cap = old_m.shape[0]
    half = mine.shape[0]
    size = half // CHUNKS
    r = lax.axis_index("rep")
    s = lax.axis_index("shard")
    owners = lax.axis_size("shard") // 2
    o = s // 2
    core = s % 2
    even = core == 0
    odd = core == 1
    other = (1 - r, s)

    x = o % 4

    up_rep = r
    down_rep = r
    sends_head = even & (up_rep == 0) & (o < owners - 1)
    gets_head = even & (r == 0) & (o > 0)
    sends_tail = even & (o > 0)
    gets_tail = odd & (o < owners - 1)
    count = 2 * owners
    head_to = (up_rep, lax.rem(s + 2, count))
    head_from = (down_rep, lax.rem(s + count - 2, count))
    tail_to = (down_rep, lax.rem(s + count - 1, count))
    tail_from = (up_rep, lax.rem(s + 1, count))
    die_to = (r, s + 1 - 2 * core)

    z_lo = (o // 4) % 4
    turn_up = jnp.where(z_lo == 3, 32, 0)
    turn_down = jnp.where(z_lo == 0, 32, 0)
    head_wraps = sends_head & (x == 3)
    head_unwraps = gets_head & (x == 0)
    tail_wraps = sends_tail & (x == 0)
    tail_unwraps = gets_tail & (x == 3)
    head_source = s - 1 + 2 * (3 - x) - turn_up
    head_rep = r
    relays_head = odd & (head_rep == 0) & (head_source >= 0)
    tail_source = s - 1 - 2 * x + turn_down
    tail_rep = r
    relays_tail = odd & (tail_source < count)
    head_relays = s + jnp.where(z_lo == 0, 24, -8) + 1
    tail_relays = s + jnp.where(z_lo == 3, -24, 8) - 6

    offsets = (
        pltpu.make_async_copy(old_off_in, old_off, off_sem.at[0]),
        pltpu.make_async_copy(new_off_in, new_off, off_sem.at[1]),
    )
    for copy in offsets:
        copy.start()
    my_grads = pltpu.make_async_copy(grads.at[0, pl.ds(r * half, half)], mine, mine_sem)

    def load_own(k, rep):
        if rep == 0:
            return pltpu.make_async_copy(
                olds[k].at[pl.ds(0, WINDOW - EDGE)], main.at[k, pl.ds(EDGE, WINDOW - EDGE)], in_sem.at[k]
            )
        return pltpu.make_async_copy(olds[k].at[pl.ds(JITTER, WINDOW)], main.at[k], in_sem.at[k])

    def load_stage(k):
        rows = stage_m.shape[0]
        return pltpu.make_async_copy(olds[k].at[pl.ds(old_cap - rows, rows)], stages[k], stage_sem.at[k])

    def die_copy(k, rep):
        first = 1024 if rep == 0 else 2560
        rows = min(WINDOW, old_cap - first)
        return pltpu.make_async_remote_copy(
            olds[k].at[pl.ds(first, rows)],
            main.at[k, pl.ds(0, rows)],
            die_sem.at[0, k],
            die_sem.at[1, k],
            device_id=die_to,
            device_id_type=MESH,
        )

    def send(src, dst, sems, to):
        return pltpu.make_async_remote_copy(src, dst, sems[0], sems[1], device_id=to, device_id_type=MESH)

    quarter = EDGE // 4

    def head_copy(k, part=None):
        rows = pl.ds(0, EDGE) if part is None else pl.ds(part * quarter, quarter)
        at = 0 if part is None else part
        sems = (head_sem.at[0, at, k], head_sem.at[1, at, k])
        return send(edge.at[k, rows], main.at[k, rows], sems, head_to)

    def head_relay_in(k, part):
        rows = pl.ds(part * quarter, quarter)
        sems = (head_sem.at[0, part, k], head_relay_sem.at[0, k])
        to = (r, lax.rem(s - 2 * (3 - part) + 1 + turn_up + count, count))
        return send(edge.at[k, rows], relay.at[0, k], sems, to)

    def head_relay_out(k, part):
        rows = pl.ds(part * quarter, quarter)
        sems = (head_relay_sem.at[1, k], head_sem.at[1, part, k])
        return send(relay.at[0, k], main.at[k, rows], sems, (head_rep, lax.rem(head_source + 2, count)))

    def tail_place(rep):
        return (3072, JITTER) if rep == 0 else (1536, EDGE)

    def tail_copy(k, rep, part=None):
        first, rows = tail_place(rep)
        begin = 0
        if part is not None:
            rows //= 4
            begin = part * rows
        at = 0 if part is None else part
        sems = (tail_sem.at[0, at, k], tail_sem.at[1, at, k])
        return send(olds[k].at[pl.ds(begin, rows)], alt.at[k, pl.ds(first + begin, rows)], sems, tail_to)

    def tail_relay_in(k, rep, part):
        rows = tail_place(rep)[1] // 4
        sems = (tail_sem.at[0, part, k], tail_relay_sem.at[0, k])
        to = (r, lax.rem(s + 2 * part + 1 - turn_down + count, count))
        return send(olds[k].at[pl.ds(part * rows, rows)], relay.at[1, k, pl.ds(0, rows)], sems, to)

    def tail_relay_out(k, rep, part):
        first, rows = tail_place(rep)
        rows //= 4
        sems = (tail_relay_sem.at[1, k], tail_sem.at[1, part, k])
        to = (tail_rep, lax.rem(tail_source + count - 1, count))
        return send(relay.at[1, k, pl.ds(0, rows)], alt.at[k, pl.ds(first + part * rows, rows)], sems, to)

    piece = PACK // CHUNKS

    def grad_copy(c, rep):
        if rep == 1:
            rows = pl.ds(pl.multiple_of(c * size, 16), size)
            src, dst = grads.at[0, rows], theirs.at[rows]
        else:
            src = pack.at[pl.ds(pl.multiple_of(c * piece, 16), piece)]
            dst = packed.at[pl.ds(pl.multiple_of(core * PACK + c * piece, 16), piece)]
        return send(src, dst, (grad_send.at[c], grad_recv.at[c]), other)

    def pass_copy(c):
        rows = packed.at[pl.ds(pl.multiple_of(core * PACK + c * piece, 16), piece)]
        return send(rows, rows, (pass_sem.at[0, c], pass_sem.at[1, c]), die_to)

    def near_copy(at):
        if at == 0:
            return pltpu.make_async_copy(grads.at[0, pl.ds(half, PACK)], near_grads, pack_sem.at[0])
        rows = half - PACK
        sems = (pack_sem.at[1], pack_sem.at[2])
        return send(grads.at[0, pl.ds(half + PACK, rows)], near_grads.at[pl.ds(0, rows)], sems, die_to)

    def far_copy(at):
        if at == 1:
            rows = far_grads.at[pl.ds(half - PACK, half)]
            return pltpu.make_async_copy(grads.at[0, pl.ds(half, half)], rows, pack_sem.at[0])
        sems = (pack_sem.at[1], pack_sem.at[2])
        return send(grads.at[0, pl.ds(half, PACK)], far_grads.at[pl.ds(half, PACK)], sems, die_to)

    def start_grads(first, last):
        for rep in (0, 1):

            @pl.when(r == rep)
            def _():
                @pl.loop(first, last)
                def _(c):
                    grad_copy(c, rep).start()

    def wts_copy(c):
        first = pl.multiple_of(c * size, 16)
        return pltpu.make_async_remote_copy(
            wts.at[pl.ds(first, size)],
            out_w.at[pl.ds(pl.multiple_of(r * half + first, 16), size)],
            wts_send.at[c],
            wts_recv.at[c],
            device_id=other,
            device_id_type=MESH,
        )

    def wts_arrival(c):
        first = pl.multiple_of(c * size, 16)
        return pltpu.make_async_remote_copy(
            wts.at[pl.ds(first, size)],
            out_w.at[pl.ds(pl.multiple_of((1 - r) * half + first, 16), size)],
            wts_send.at[c],
            wts_recv.at[c],
            device_id=other,
            device_id_type=MESH,
        )

    def own_copy(c):
        first = pl.multiple_of(c * size, 16)
        return pltpu.make_async_copy(
            wts.at[pl.ds(first, size)],
            out_w.at[pl.ds(pl.multiple_of(r * half + first, 16), size)],
            own_sem.at[c],
        )

    def res_copy(k, c):
        first = pl.multiple_of(c * size, 16)
        return pltpu.make_async_copy(
            res.at[k, pl.ds(first, size)], outs[k].at[pl.ds(first, size)], res_sem.at[k, c]
        )

    @pl.when(sends_head)
    def _():
        for k in range(3):
            load_stage(k).start()

    @pl.when((r == 0) & even)
    def _():
        near_copy(0).start()

    @pl.when((r == 0) & odd)
    def _():
        far_copy(1).start()

    barrier = pltpu.get_barrier_semaphore()
    pl.semaphore_signal(barrier, inc=1, device_id=other, device_id_type=MESH)

    pl.semaphore_signal(barrier, inc=1, device_id=die_to, device_id_type=MESH)

    @pl.when(gets_head & (x > 0))
    def _():
        pl.semaphore_signal(barrier, inc=1, device_id=head_from, device_id_type=MESH)

    @pl.when(head_unwraps)
    def _():
        for part in range(4):
            at = lax.rem(head_relays + 2 * part + count, count)
            pl.semaphore_signal(barrier, inc=1, device_id=(down_rep, at), device_id_type=MESH)

    @pl.when(gets_tail & (x < 3))
    def _():
        pl.semaphore_signal(barrier, inc=1, device_id=tail_from, device_id_type=MESH)

    @pl.when(tail_unwraps)
    def _():
        for part in range(4):
            at = lax.rem(tail_relays + 2 * part + count, count)
            pl.semaphore_signal(barrier, inc=1, device_id=(up_rep, at), device_id_type=MESH)

    @pl.when(relays_head)
    def _():
        pl.semaphore_signal(barrier, inc=1, device_id=(r, lax.rem(head_source + count, count)), device_id_type=MESH)

    @pl.when(relays_tail)
    def _():
        pl.semaphore_signal(barrier, inc=1, device_id=(r, lax.rem(tail_source, count)), device_id_type=MESH)

    targets = 2
    for cond, more in (
        (sends_head, 1),
        (head_wraps, 3),
        (sends_tail, 1),
        (tail_wraps, 3),
        (relays_head, 1),
        (relays_tail, 1),
    ):
        targets = targets + more * cond.astype(jnp.int32)
    pl.semaphore_wait(barrier, targets)

    early = jnp.where(odd, EARLY, CHUNKS)

    @pl.when(r == 1)
    def _():
        @pl.loop(0, early)
        def _(c):
            grad_copy(c, 1).start()

    @pl.when((r == 0) & even)
    def _():
        near_copy(1).start()

    @pl.when((r == 0) & odd)
    def _():
        far_copy(0).start()

    for rep in (0, 1):

        @pl.when(tail_wraps & (down_rep == rep))
        def _():
            for part in range(4):
                for k in range(3):
                    tail_relay_in(k, rep, part).start()

    for copy in offsets:
        copy.wait()

    pair = s - core
    first_rows = jnp.clip(new_off[pair + 1] - new_off[pair] - half, 0, half)

    @pl.when((r == 0) & even)
    def _():
        near_copy(0).wait()
        far_copy(0).wait_recv()

    @pl.when((r == 0) & odd)
    def _():
        far_copy(1).wait()
        near_copy(1).wait_recv()

    @pl.when(r == 0)
    def _():
        @pl.loop(0, PACK // SUB)
        def _(j):
            at = j * SUB
            rows = pl.ds(pl.multiple_of(at, SUB), SUB)
            row = core * PACK + at + lax.broadcasted_iota(jnp.int32, (SUB, 128), 0)
            far = far_grads[pl.ds(half - first_rows + at, SUB), :]
            pack[rows, :] = jnp.where(row < first_rows, near_grads[rows, :], far)

    @pl.when(r == 0)
    def _():
        @pl.loop(0, CHUNKS)
        def _(c):
            grad_copy(c, 0).start()

    @pl.when(sends_head)
    def _():
        begin = within(old_off[o + 1] - old_off[o] - (old_cap - stage_m.shape[0]) - EDGE)
        for k in range(3):
            load_stage(k).wait()

            @pl.loop(0, EDGE // SUB)
            def _(j):
                edge[k, pl.ds(pl.multiple_of(j * SUB, SUB), SUB), :] = stages[k][pl.ds(begin + j * SUB, SUB), :]

            @pl.when(x < 3)
            def _():
                head_copy(k).start()

            @pl.when(x == 3)
            def _():
                for part in range(4):
                    head_relay_in(k, part).start()

    for rep in (0, 1):

        @pl.when(sends_tail & (down_rep == rep) & (x > 0))
        def _():
            for k in range(3):
                tail_copy(k, rep).start()

    for rep in (0, 1):

        @pl.when(even & (r == rep))
        def _():
            for k in range(3):
                die_copy(k, rep).start()

    for rep in (0, 1):

        @pl.when(even & (r == rep))
        def _():
            for k in range(3):
                load_own(k, rep).start()

    my_grads.start()

    for part in range(4):

        @pl.when(relays_head & (x == part))
        def _():
            for k in range(3):
                head_relay_in(k, part).wait_recv()
                head_relay_out(k, part).start()

    for rep in (0, 1):
        for part in range(4):

            @pl.when(relays_tail & (tail_rep == rep) & (x == part))
            def _():
                for k in range(3):
                    tail_relay_in(k, rep, part).wait_recv()
                    tail_relay_out(k, rep, part).start()

    @pl.when(r == 1)
    def _():
        @pl.loop(early, CHUNKS)
        def _(c):
            grad_copy(c, 1).start()

    passes = jnp.where(even, CHUNKS, (half - PACK) // piece)
    arrivals = jnp.where(odd, CHUNKS, (half - PACK) // piece)

    @pl.when(r == 1)
    def _():
        @pl.loop(0, CHUNKS)
        def _(c):
            grad_copy(c, 0).wait_recv()

            @pl.when(c < passes)
            def _():
                pass_copy(c).start()

    for rep in (0, 1):

        @pl.when(even & (r == rep))
        def _():
            for k in range(3):
                load_own(k, rep).wait()

        @pl.when(odd & (r == rep))
        def _():
            for k in range(3):
                die_copy(k, rep).wait_recv()

    @pl.when(gets_head & (x > 0))
    def _():
        for k in range(3):
            head_copy(k).wait_recv()

    @pl.when(head_unwraps)
    def _():
        for part in range(4):
            for k in range(3):
                head_copy(k, part).wait_recv()

    for rep in (0, 1):

        @pl.when(gets_tail & (r == rep) & (x < 3))
        def _():
            for k in range(3):
                tail_copy(k, rep).wait_recv()

        @pl.when(tail_unwraps & (r == rep))
        def _():
            for part in range(4):
                for k in range(3):
                    tail_copy(k, rep, part).wait_recv()

    my_grads.wait()

    start = within(new_off[s] - old_off[o] + EDGE - 2 * EDGE * core)
    edge_start = within(new_off[s] - old_off[o + 1] + 2 * half)
    split = jnp.where(even, new_off[s + 1], old_off[o + 1])
    flat = new_off[s] + r * half
    stop = new_off[s + 1]

    def update(c, their_rows):
        @pl.loop(0, size // SUB)
        def _(j):
            at = c * size + j * SUB
            rows = pl.ds(pl.multiple_of(at, SUB), SUB)
            row = flat + at + lax.broadcasted_iota(jnp.int32, (SUB, 128), 0)
            near = row < split
            keep = row < stop
            master, first, second = [
                jnp.where(near, main[k, pl.ds(start + at, SUB), :], alt[k, pl.ds(edge_start + at, SUB), :])
                for k in range(3)
            ]
            total = mine[rows, :] + their_rows(at)
            first_n = 0.9 * first + 0.1 * total
            second_n = 0.95 * second + 0.05 * total * total
            first_hat = first_n / (1.0 - 0.9**STEP)
            second_hat = second_n / (1.0 - 0.95**STEP)
            master_n = master - 0.02 * (first_hat / (jnp.sqrt(second_hat) + 1e-08) + 0.1 * master)
            master_n = jnp.where(keep, master_n, 0.0)
            res[0, rows, :] = master_n
            res[1, rows, :] = jnp.where(keep, first_n, 0.0)
            res[2, rows, :] = jnp.where(keep, second_n, 0.0)
            wts[rows, :] = master_n.astype(jnp.bfloat16)

        wts_copy(c).start()
        own_copy(c).start()
        for k in range(3):
            res_copy(k, c).start()

    @pl.when(r == 0)
    def _():
        @pl.loop(0, CHUNKS)
        def _(c):
            grad_copy(c, 1).wait_recv()
            update(c, lambda at: theirs[pl.ds(pl.multiple_of(at, SUB), SUB), :])

    @pl.when(r == 1)
    def _():
        @pl.loop(0, arrivals)
        def _(c):
            there = packed.at[pl.ds(pl.multiple_of((1 - core) * PACK + c * piece, 16), piece)]
            send(there, there, (pass_sem.at[0, c], pass_sem.at[1, c]), die_to).wait_recv()

        @pl.loop(0, CHUNKS)
        def _(c):
            update(c, lambda at: packed[pl.ds(core * first_rows + at, SUB), :])

    for rep in (0, 1):

        @pl.when(even & (r == rep))
        def _():
            for k in range(3):
                die_copy(k, rep).wait_send()

    @pl.when(sends_head & (x < 3))
    def _():
        for k in range(3):
            head_copy(k).wait_send()

    @pl.when(head_wraps)
    def _():
        for part in range(4):
            for k in range(3):
                head_copy(k, part).wait_send()

    @pl.when(relays_head)
    def _():
        for k in range(3):
            head_relay_out(k, 0).wait_send()

    for rep in (0, 1):

        @pl.when(sends_tail & (down_rep == rep) & (x > 0))
        def _():
            for k in range(3):
                tail_copy(k, rep).wait_send()

        @pl.when(tail_wraps & (down_rep == rep))
        def _():
            for part in range(4):
                for k in range(3):
                    tail_copy(k, rep, part).wait_send()

        @pl.when(relays_tail & (tail_rep == rep))
        def _():
            for k in range(3):
                tail_relay_out(k, rep, 0).wait_send()

    @pl.when((r == 0) & even)
    def _():
        near_copy(1).wait_send()

    @pl.when((r == 0) & odd)
    def _():
        far_copy(0).wait_send()

    @pl.when(r == 1)
    def _():
        @pl.loop(0, passes)
        def _(c):
            pass_copy(c).wait_send()

    for rep in (0, 1):

        @pl.when(r == rep)
        def _():
            @pl.loop(0, CHUNKS)
            def _(c):
                grad_copy(c, rep).wait_send()

    @pl.loop(0, CHUNKS)
    def _(c):
        for k in range(3):
            res_copy(k, c).wait()
        own_copy(c).wait()
        wts_copy(c).wait_send()
        wts_arrival(c).wait_recv()


def finish(in_m, in_f, in_s, in_w, out_m, out_f, out_s, out_w, vm, vf, vs, vw, in_sem, out_sem):
    ins, holds, outs = (in_m, in_f, in_s, in_w), (vm, vf, vs, vw), (out_m, out_f, out_s, out_w)
    loads = [pltpu.make_async_copy(ins[i], holds[i], in_sem.at[i]) for i in range(4)]
    stores = [pltpu.make_async_copy(holds[i], outs[i], out_sem.at[i]) for i in range(4)]
    for load in loads:
        load.start()
    for load, store in zip(loads, stores):
        load.wait()
        store.start()
    for store in stores:
        store.wait()


def local(old_master, old_first, old_second, grad_parts, old_offsets, new_offsets):
    new_cap, lanes = grad_parts.shape[1:]
    half = new_cap // 2
    hbm = pl.BlockSpec(memory_space=pltpu.HBM)
    free = pl.BlockSpec(memory_space=pl.ANY)
    state = jax.ShapeDtypeStruct((half, lanes), jnp.float32)
    dma = pltpu.SemaphoreType.DMA
    shapes = (state, state, state, jax.ShapeDtypeStruct((new_cap, lanes), jnp.bfloat16))
    results = pl.pallas_call(
        kernel,
        out_shape=shapes,
        in_specs=[hbm] * 6,
        out_specs=(free, free, free, free),
        scratch_shapes=[
            pltpu.SMEM(old_offsets.shape, jnp.int32),
            pltpu.SMEM(new_offsets.shape, jnp.int32),
            pltpu.VMEM((3, WINDOW, lanes), jnp.float32),
            pltpu.VMEM((3, WINDOW, lanes), jnp.float32),
            pltpu.VMEM((2, 3, EDGE // 4, lanes), jnp.float32),
            pltpu.VMEM((3 * EDGE, lanes), jnp.float32),
            pltpu.VMEM((3 * EDGE, lanes), jnp.float32),
            pltpu.VMEM((3 * EDGE, lanes), jnp.float32),
            pltpu.VMEM((3, EDGE, lanes), jnp.float32),
            pltpu.VMEM((half, lanes), jnp.float32),
            pltpu.VMEM((half, lanes), jnp.float32),
            pltpu.VMEM((PACK, lanes), jnp.float32),
            pltpu.VMEM((half + PACK, lanes), jnp.float32),
            pltpu.VMEM((PACK, lanes), jnp.float32),
            pltpu.VMEM((2 * half, lanes), jnp.float32),
            pltpu.VMEM((3, half, lanes), jnp.float32),
            pltpu.VMEM((half, lanes), jnp.bfloat16),
            dma((2,)),
            dma((3,)),
            dma,
            dma((3,)),
            dma((2, 3)),
            dma((2, 4, 3)),
            dma((2, 4, 3)),
            dma((2, 3)),
            dma((2, 3)),
            dma((3,)),
            dma((2, CHUNKS)),
            dma((CHUNKS,)),
            dma((CHUNKS,)),
            dma((CHUNKS,)),
            dma((CHUNKS,)),
            dma((3, CHUNKS)),
            dma((CHUNKS,)),
        ],
        compiler_params=pltpu.CompilerParams(
            collective_id=0, has_side_effects=True, vmem_limit_bytes=60 * 1024 * 1024
        ),
        name="move_and_update",
    )(old_offsets, new_offsets, old_master, old_first, old_second, grad_parts)
    master, first, second, weights = pl.pallas_call(
        finish,
        out_shape=shapes,
        in_specs=[hbm] * 4,
        out_specs=(hbm,) * 4,
        scratch_shapes=[pltpu.VMEM(shape.shape, shape.dtype) for shape in shapes] + [dma((4,)), dma((4,))],
        compiler_params=pltpu.CompilerParams(vmem_limit_bytes=60 * 1024 * 1024),
        name="finish",
    )(*results)
    return (master[None, None], first[None, None], second[None, None], weights)


def solution(mesh):
    in_specs = (
        P("shard", None),
        P("shard", None),
        P("shard", None),
        P("rep", "shard", None),
        P(),
        P(),
    )
    out_specs = (
        P("shard", "rep", None, None),
        P("shard", "rep", None, None),
        P("shard", "rep", None, None),
        P("shard", None),
    )
    return jax.shard_map(local, mesh=mesh, in_specs=in_specs, out_specs=out_specs, check_vma=False)
```

```python
import functools

import jax
import jax.numpy as jnp
from jax import lax
from jax.experimental import pallas as pl
from jax.experimental.pallas import tpu as pltpu
from jax.sharding import PartitionSpec as P

STEP = 10
MESH = pl.DeviceIdType.MESH
JITTER = 512
EDGE = 2 * JITTER
PACK = 1024
WINDOW = 3584
CHUNKS = 8
SUB = 64
EARLY = 5


def within(start):
    return jnp.clip(start, 0, 2 * EDGE)


def kernel(
    old_off_in,
    new_off_in,
    old_m,
    old_f,
    old_s,
    grads,
    out_m,
    out_f,
    out_s,
    out_w,
    out_q,
    old_off,
    new_off,
    main,
    alt,
    relay,
    stage_m,
    stage_f,
    stage_s,
    edge,
    mine,
    theirs,
    near_rows,
    far_rows,
    pack,
    packed,
    short_pack,
    short_packed,
    res,
    wts,
    off_sem,
    in_sem,
    mine_sem,
    stage_sem,
    die_sem,
    head_sem,
    tail_sem,
    head_relay_sem,
    tail_relay_sem,
    pack_sem,
    pass_sem,
    grad_send,
    grad_recv,
    wts_send,
    wts_recv,
    res_sem,
    own_sem,
    short_sem,
):
    olds = (old_m, old_f, old_s)
    outs = (out_m, out_f, out_s)
    stages = (stage_m, stage_f, stage_s)
    old_cap = old_m.shape[0]
    half = mine.shape[0]
    size = half // CHUNKS
    r = lax.axis_index("rep")
    s = lax.axis_index("shard")
    owners = lax.axis_size("shard") // 2
    o = s // 2
    core = s % 2
    even = core == 0
    odd = core == 1
    other = (1 - r, s)

    x = o % 4

    up_rep = r
    down_rep = r
    sends_head = even & (up_rep == 0) & (o < owners - 1)
    gets_head = even & (r == 0) & (o > 0)
    sends_tail = even & (o > 0)
    gets_tail = odd & (o < owners - 1)
    count = 2 * owners
    head_to = (up_rep, lax.rem(s + 2, count))
    head_from = (down_rep, lax.rem(s + count - 2, count))
    tail_to = (down_rep, lax.rem(s + count - 1, count))
    tail_from = (up_rep, lax.rem(s + 1, count))
    die_to = (r, s + 1 - 2 * core)

    z_lo = (o // 4) % 4
    turn_up = jnp.where(z_lo == 3, 32, 0)
    turn_down = jnp.where(z_lo == 0, 32, 0)
    head_wraps = sends_head & (x == 3)
    head_unwraps = gets_head & (x == 0)
    tail_wraps = sends_tail & (x == 0)
    tail_unwraps = gets_tail & (x == 3)
    head_source = s - 1 + 2 * (3 - x) - turn_up
    head_rep = r
    relays_head = odd & (head_rep == 0) & (head_source >= 0)
    tail_source = s - 1 - 2 * x + turn_down
    tail_rep = r
    relays_tail = odd & (tail_source < count)
    head_relays = s + jnp.where(z_lo == 0, 24, -8) + 1
    tail_relays = s + jnp.where(z_lo == 3, -24, 8) - 6

    offsets = (
        pltpu.make_async_copy(old_off_in, old_off, off_sem.at[0]),
        pltpu.make_async_copy(new_off_in, new_off, off_sem.at[1]),
    )
    for copy in offsets:
        copy.start()
    my_grads = pltpu.make_async_copy(grads.at[0, pl.ds(r * half, half)], mine, mine_sem)

    def load_own(k, rep):
        if rep == 0:
            return pltpu.make_async_copy(
                olds[k].at[pl.ds(0, WINDOW - EDGE)], main.at[k, pl.ds(EDGE, WINDOW - EDGE)], in_sem.at[k]
            )
        return pltpu.make_async_copy(olds[k].at[pl.ds(JITTER, WINDOW)], main.at[k], in_sem.at[k])

    def load_stage(k):
        rows = stage_m.shape[0]
        return pltpu.make_async_copy(olds[k].at[pl.ds(old_cap - rows, rows)], stages[k], stage_sem.at[k])

    def die_copy(k, rep):
        first = 1024 if rep == 0 else 2560
        rows = min(WINDOW, old_cap - first)
        return pltpu.make_async_remote_copy(
            olds[k].at[pl.ds(first, rows)],
            main.at[k, pl.ds(0, rows)],
            die_sem.at[0, k],
            die_sem.at[1, k],
            device_id=die_to,
            device_id_type=MESH,
        )

    def send(src, dst, sems, to):
        return pltpu.make_async_remote_copy(src, dst, sems[0], sems[1], device_id=to, device_id_type=MESH)

    quarter = EDGE // 4

    def head_copy(k, part=None):
        rows = pl.ds(0, EDGE) if part is None else pl.ds(part * quarter, quarter)
        at = 0 if part is None else part
        sems = (head_sem.at[0, at, k], head_sem.at[1, at, k])
        return send(edge.at[k, rows], main.at[k, rows], sems, head_to)

    def head_relay_in(k, part):
        rows = pl.ds(part * quarter, quarter)
        sems = (head_sem.at[0, part, k], head_relay_sem.at[0, k])
        to = (r, lax.rem(s - 2 * (3 - part) + 1 + turn_up + count, count))
        return send(edge.at[k, rows], relay.at[0, k], sems, to)

    def head_relay_out(k, part):
        rows = pl.ds(part * quarter, quarter)
        sems = (head_relay_sem.at[1, k], head_sem.at[1, part, k])
        return send(relay.at[0, k], main.at[k, rows], sems, (head_rep, lax.rem(head_source + 2, count)))

    def tail_place(rep):
        return (3072, JITTER) if rep == 0 else (1536, EDGE)

    def tail_copy(k, rep, part=None):
        first, rows = tail_place(rep)
        begin = 0
        if part is not None:
            rows //= 4
            begin = part * rows
        at = 0 if part is None else part
        sems = (tail_sem.at[0, at, k], tail_sem.at[1, at, k])
        return send(olds[k].at[pl.ds(begin, rows)], alt.at[k, pl.ds(first + begin, rows)], sems, tail_to)

    def tail_relay_in(k, rep, part):
        rows = tail_place(rep)[1] // 4
        sems = (tail_sem.at[0, part, k], tail_relay_sem.at[0, k])
        to = (r, lax.rem(s + 2 * part + 1 - turn_down + count, count))
        return send(olds[k].at[pl.ds(part * rows, rows)], relay.at[1, k, pl.ds(0, rows)], sems, to)

    def tail_relay_out(k, rep, part):
        first, rows = tail_place(rep)
        rows //= 4
        sems = (tail_relay_sem.at[1, k], tail_sem.at[1, part, k])
        to = (tail_rep, lax.rem(tail_source + count - 1, count))
        return send(relay.at[1, k, pl.ds(0, rows)], alt.at[k, pl.ds(first + part * rows, rows)], sems, to)

    piece = PACK // CHUNKS

    def grad_copy(c, rep):
        if rep == 1:
            rows = pl.ds(pl.multiple_of(c * size, 16), size)
            src, dst = grads.at[0, rows], theirs.at[rows]
        else:
            src = pack.at[pl.ds(pl.multiple_of(c * piece, 16), piece)]
            dst = packed.at[pl.ds(pl.multiple_of(core * PACK + c * piece, 16), piece)]
        return send(src, dst, (grad_send.at[c], grad_recv.at[c]), other)

    def pass_copy(c):
        rows = packed.at[pl.ds(pl.multiple_of(core * PACK + c * piece, 16), piece)]
        return send(rows, rows, (pass_sem.at[0, c], pass_sem.at[1, c]), die_to)

    def grad_rows(first, rows):
        return grads.at[0, pl.ds(half + first, rows)]

    def master_rows(first, rows):
        return res.at[0, pl.ds(first, rows)]

    def near_copy(at, source):
        if at == 0:
            return pltpu.make_async_copy(source(0, PACK), near_rows, pack_sem.at[0])
        rows = half - PACK
        return send(source(PACK, rows), near_rows.at[pl.ds(0, rows)], (pack_sem.at[1], pack_sem.at[2]), die_to)

    def far_copy(at, source):
        if at == 1:
            return pltpu.make_async_copy(source(0, half), far_rows.at[pl.ds(half - PACK, half)], pack_sem.at[0])
        return send(source(0, PACK), far_rows.at[pl.ds(half, PACK)], (pack_sem.at[1], pack_sem.at[2]), die_to)

    def pack_rows(at):
        row = core * PACK + at + lax.broadcasted_iota(jnp.int32, (SUB, 128), 0)
        far = far_rows[pl.ds(half - first_rows + at, SUB), :]
        return jnp.where(row < first_rows, near_rows[pl.ds(pl.multiple_of(at, SUB), SUB), :], far)

    def short_copy(c):
        src = short_pack.at[pl.ds(pl.multiple_of(c * piece, 16), piece)]
        dst = short_packed.at[pl.ds(pl.multiple_of(core * PACK + c * piece, 16), piece)]
        return send(src, dst, (wts_send.at[c], wts_recv.at[c]), other)

    def short_place(c, at):
        return pl.ds(pl.multiple_of(at * PACK + c * piece, 16), piece)

    def short_pass(c, at):
        rows = short_place(c, at)
        return send(short_packed.at[rows], out_q.at[rows], (pass_sem.at[0, c], pass_sem.at[1, c]), die_to)

    def short_keep(c):
        rows = short_place(c, core)
        return pltpu.make_async_copy(short_packed.at[rows], out_q.at[rows], short_sem.at[c])

    def start_grads(first, last):
        for rep in (0, 1):

            @pl.when(r == rep)
            def _():
                @pl.loop(first, last)
                def _(c):
                    grad_copy(c, rep).start()

    def wts_copy(c):
        first = pl.multiple_of(c * size, 16)
        return pltpu.make_async_remote_copy(
            wts.at[pl.ds(first, size)],
            out_w.at[pl.ds(pl.multiple_of(r * half + first, 16), size)],
            wts_send.at[c],
            wts_recv.at[c],
            device_id=other,
            device_id_type=MESH,
        )

    def wts_arrival(c):
        first = pl.multiple_of(c * size, 16)
        return pltpu.make_async_remote_copy(
            wts.at[pl.ds(first, size)],
            out_w.at[pl.ds(pl.multiple_of((1 - r) * half + first, 16), size)],
            wts_send.at[c],
            wts_recv.at[c],
            device_id=other,
            device_id_type=MESH,
        )

    def own_copy(c):
        first = pl.multiple_of(c * size, 16)
        return pltpu.make_async_copy(
            wts.at[pl.ds(first, size)],
            out_w.at[pl.ds(pl.multiple_of(r * half + first, 16), size)],
            own_sem.at[c],
        )

    def res_copy(k, c):
        first = pl.multiple_of(c * size, 16)
        return pltpu.make_async_copy(
            res.at[k, pl.ds(first, size)], outs[k].at[pl.ds(first, size)], res_sem.at[k, c]
        )

    @pl.when(sends_head)
    def _():
        for k in range(3):
            load_stage(k).start()

    @pl.when((r == 0) & even)
    def _():
        near_copy(0, grad_rows).start()

    @pl.when((r == 0) & odd)
    def _():
        far_copy(1, grad_rows).start()

    barrier = pltpu.get_barrier_semaphore()
    pl.semaphore_signal(barrier, inc=1, device_id=other, device_id_type=MESH)

    pl.semaphore_signal(barrier, inc=1, device_id=die_to, device_id_type=MESH)

    @pl.when(gets_head & (x > 0))
    def _():
        pl.semaphore_signal(barrier, inc=1, device_id=head_from, device_id_type=MESH)

    @pl.when(head_unwraps)
    def _():
        for part in range(4):
            at = lax.rem(head_relays + 2 * part + count, count)
            pl.semaphore_signal(barrier, inc=1, device_id=(down_rep, at), device_id_type=MESH)

    @pl.when(gets_tail & (x < 3))
    def _():
        pl.semaphore_signal(barrier, inc=1, device_id=tail_from, device_id_type=MESH)

    @pl.when(tail_unwraps)
    def _():
        for part in range(4):
            at = lax.rem(tail_relays + 2 * part + count, count)
            pl.semaphore_signal(barrier, inc=1, device_id=(up_rep, at), device_id_type=MESH)

    @pl.when(relays_head)
    def _():
        pl.semaphore_signal(barrier, inc=1, device_id=(r, lax.rem(head_source + count, count)), device_id_type=MESH)

    @pl.when(relays_tail)
    def _():
        pl.semaphore_signal(barrier, inc=1, device_id=(r, lax.rem(tail_source, count)), device_id_type=MESH)

    targets = 2
    for cond, more in (
        (sends_head, 1),
        (head_wraps, 3),
        (sends_tail, 1),
        (tail_wraps, 3),
        (relays_head, 1),
        (relays_tail, 1),
    ):
        targets = targets + more * cond.astype(jnp.int32)
    pl.semaphore_wait(barrier, targets)

    early = jnp.where(odd, EARLY, CHUNKS)

    @pl.when(r == 1)
    def _():
        @pl.loop(0, early)
        def _(c):
            grad_copy(c, 1).start()

    @pl.when((r == 0) & even)
    def _():
        near_copy(1, grad_rows).start()

    @pl.when((r == 0) & odd)
    def _():
        far_copy(0, grad_rows).start()

    for rep in (0, 1):

        @pl.when(tail_wraps & (down_rep == rep))
        def _():
            for part in range(4):
                for k in range(3):
                    tail_relay_in(k, rep, part).start()

    for copy in offsets:
        copy.wait()

    pair = s - core
    first_rows = jnp.clip(new_off[pair + 1] - new_off[pair] - half, 0, half)

    @pl.when((r == 0) & even)
    def _():
        near_copy(0, grad_rows).wait()
        far_copy(0, grad_rows).wait_recv()

    @pl.when((r == 0) & odd)
    def _():
        far_copy(1, grad_rows).wait()
        near_copy(1, grad_rows).wait_recv()

    @pl.when(r == 0)
    def _():
        @pl.loop(0, PACK // SUB)
        def _(j):
            pack[pl.ds(pl.multiple_of(j * SUB, SUB), SUB), :] = pack_rows(j * SUB)

    @pl.when(r == 0)
    def _():
        @pl.loop(0, CHUNKS)
        def _(c):
            grad_copy(c, 0).start()

    @pl.when(sends_head)
    def _():
        begin = within(old_off[o + 1] - old_off[o] - (old_cap - stage_m.shape[0]) - EDGE)
        for k in range(3):
            load_stage(k).wait()

            @pl.loop(0, EDGE // SUB)
            def _(j):
                edge[k, pl.ds(pl.multiple_of(j * SUB, SUB), SUB), :] = stages[k][pl.ds(begin + j * SUB, SUB), :]

            @pl.when(x < 3)
            def _():
                head_copy(k).start()

            @pl.when(x == 3)
            def _():
                for part in range(4):
                    head_relay_in(k, part).start()

    for rep in (0, 1):

        @pl.when(sends_tail & (down_rep == rep) & (x > 0))
        def _():
            for k in range(3):
                tail_copy(k, rep).start()

    for rep in (0, 1):

        @pl.when(even & (r == rep))
        def _():
            for k in range(3):
                die_copy(k, rep).start()

    for rep in (0, 1):

        @pl.when(even & (r == rep))
        def _():
            for k in range(3):
                load_own(k, rep).start()

    my_grads.start()

    for part in range(4):

        @pl.when(relays_head & (x == part))
        def _():
            for k in range(3):
                head_relay_in(k, part).wait_recv()
                head_relay_out(k, part).start()

    for rep in (0, 1):
        for part in range(4):

            @pl.when(relays_tail & (tail_rep == rep) & (x == part))
            def _():
                for k in range(3):
                    tail_relay_in(k, rep, part).wait_recv()
                    tail_relay_out(k, rep, part).start()

    @pl.when(r == 1)
    def _():
        @pl.loop(early, CHUNKS)
        def _(c):
            grad_copy(c, 1).start()

    passes = jnp.where(even, CHUNKS, (half - PACK) // piece)
    arrivals = jnp.where(odd, CHUNKS, (half - PACK) // piece)

    @pl.when(r == 1)
    def _():
        @pl.loop(0, CHUNKS)
        def _(c):
            grad_copy(c, 0).wait_recv()

            @pl.when(c < passes)
            def _():
                pass_copy(c).start()

    for rep in (0, 1):

        @pl.when(even & (r == rep))
        def _():
            for k in range(3):
                load_own(k, rep).wait()

        @pl.when(odd & (r == rep))
        def _():
            for k in range(3):
                die_copy(k, rep).wait_recv()

    @pl.when(gets_head & (x > 0))
    def _():
        for k in range(3):
            head_copy(k).wait_recv()

    @pl.when(head_unwraps)
    def _():
        for part in range(4):
            for k in range(3):
                head_copy(k, part).wait_recv()

    for rep in (0, 1):

        @pl.when(gets_tail & (r == rep) & (x < 3))
        def _():
            for k in range(3):
                tail_copy(k, rep).wait_recv()

        @pl.when(tail_unwraps & (r == rep))
        def _():
            for part in range(4):
                for k in range(3):
                    tail_copy(k, rep, part).wait_recv()

    my_grads.wait()

    start = within(new_off[s] - old_off[o] + EDGE - 2 * EDGE * core)
    edge_start = within(new_off[s] - old_off[o + 1] + 2 * half)
    split = jnp.where(even, new_off[s + 1], old_off[o + 1])
    flat = new_off[s] + r * half
    stop = new_off[s + 1]

    def update(c, their_rows):
        @pl.loop(0, size // SUB)
        def _(j):
            at = c * size + j * SUB
            rows = pl.ds(pl.multiple_of(at, SUB), SUB)
            row = flat + at + lax.broadcasted_iota(jnp.int32, (SUB, 128), 0)
            near = row < split
            keep = row < stop
            master, first, second = [
                jnp.where(near, main[k, pl.ds(start + at, SUB), :], alt[k, pl.ds(edge_start + at, SUB), :])
                for k in range(3)
            ]
            total = mine[rows, :] + their_rows(at)
            first_n = 0.9 * first + 0.1 * total
            second_n = 0.95 * second + 0.05 * total * total
            first_hat = first_n / (1.0 - 0.9**STEP)
            second_hat = second_n / (1.0 - 0.95**STEP)
            master_n = master - 0.02 * (first_hat / (jnp.sqrt(second_hat) + 1e-08) + 0.1 * master)
            master_n = jnp.where(keep, master_n, 0.0)
            res[0, rows, :] = master_n
            res[1, rows, :] = jnp.where(keep, first_n, 0.0)
            res[2, rows, :] = jnp.where(keep, second_n, 0.0)
            wts[rows, :] = master_n.astype(jnp.bfloat16)

        own_copy(c).start()
        for k in range(3):
            res_copy(k, c).start()

    @pl.when(r == 0)
    def _():
        @pl.loop(0, CHUNKS)
        def _(c):
            grad_copy(c, 1).wait_recv()
            update(c, lambda at: theirs[pl.ds(pl.multiple_of(at, SUB), SUB), :])
            wts_copy(c).start()

        @pl.loop(0, CHUNKS)
        def _(c):
            short_copy(c).wait_recv()
            short_keep(c).start()

            @pl.when(c < passes)
            def _():
                short_pass(c, core).start()


    @pl.when(r == 1)
    def _():
        @pl.loop(0, arrivals)
        def _(c):
            there = packed.at[pl.ds(pl.multiple_of((1 - core) * PACK + c * piece, 16), piece)]
            send(there, there, (pass_sem.at[0, c], pass_sem.at[1, c]), die_to).wait_recv()

        @pl.loop(0, CHUNKS)
        def _(c):
            update(c, lambda at: packed[pl.ds(core * first_rows + at, SUB), :])

            @pl.when((c == (PACK - 1) // size) & even)
            def _():
                near_copy(0, master_rows).start()

            @pl.when((c == (PACK - 1) // size) & odd)
            def _():
                far_copy(0, master_rows).start()

        @pl.when(even)
        def _():
            near_copy(1, master_rows).start()
            near_copy(0, master_rows).wait()
            far_copy(0, master_rows).wait_recv()

        @pl.when(odd)
        def _():
            far_copy(1, master_rows).start()
            far_copy(1, master_rows).wait()
            near_copy(1, master_rows).wait_recv()

        @pl.loop(0, CHUNKS)
        def _(c):
            @pl.loop(0, piece // SUB)
            def _(j):
                at = c * piece + j * SUB
                short_pack[pl.ds(pl.multiple_of(at, SUB), SUB), :] = pack_rows(at).astype(jnp.bfloat16)

            short_copy(c).start()


    for rep in (0, 1):

        @pl.when(even & (r == rep))
        def _():
            for k in range(3):
                die_copy(k, rep).wait_send()

    @pl.when(sends_head & (x < 3))
    def _():
        for k in range(3):
            head_copy(k).wait_send()

    @pl.when(head_wraps)
    def _():
        for part in range(4):
            for k in range(3):
                head_copy(k, part).wait_send()

    @pl.when(relays_head)
    def _():
        for k in range(3):
            head_relay_out(k, 0).wait_send()

    for rep in (0, 1):

        @pl.when(sends_tail & (down_rep == rep) & (x > 0))
        def _():
            for k in range(3):
                tail_copy(k, rep).wait_send()

        @pl.when(tail_wraps & (down_rep == rep))
        def _():
            for part in range(4):
                for k in range(3):
                    tail_copy(k, rep, part).wait_send()

        @pl.when(relays_tail & (tail_rep == rep))
        def _():
            for k in range(3):
                tail_relay_out(k, rep, 0).wait_send()

    @pl.when(even)
    def _():
        near_copy(1, grad_rows).wait_send()

    @pl.when(odd)
    def _():
        far_copy(0, grad_rows).wait_send()

    for rep in (0, 1):

        @pl.when(r == rep)
        def _():
            @pl.loop(0, CHUNKS)
            def _(c):
                grad_copy(c, rep).wait_send()
                own_copy(c).wait()
                for k in range(3):
                    res_copy(k, c).wait()

    @pl.when(r == 0)
    def _():
        @pl.loop(0, CHUNKS)
        def _(c):
            wts_copy(c).wait_send()
            short_keep(c).wait()

        @pl.loop(0, passes)
        def _(c):
            short_pass(c, core).wait_send()

        @pl.loop(0, arrivals)
        def _(c):
            short_pass(c, 1 - core).wait_recv()

    @pl.when(r == 1)
    def _():
        @pl.loop(0, passes)
        def _(c):
            pass_copy(c).wait_send()

        @pl.loop(0, CHUNKS)
        def _(c):
            short_copy(c).wait_send()
            wts_arrival(c).wait_recv()


def finish(
    off_in, in_m, in_f, in_s, in_w, in_q, out_m, out_f, out_s, out_w, off, vm, vf, vs, vw, vq, wide, in_sem, out_sem
):
    r = lax.axis_index("rep")
    s = lax.axis_index("shard")
    core = s % 2
    half = vm.shape[0]
    top, low = pl.ds(0, half), pl.ds(half, half)
    load_off = pltpu.make_async_copy(off_in, off, in_sem.at[0])
    load_q = pltpu.make_async_copy(in_q, vq, in_sem.at[1])
    pairs = [(in_m, vm, out_m), (in_f, vf, out_f), (in_s, vs, out_s), (in_w.at[top], vw.at[top], out_w.at[top])]
    loads = [pltpu.make_async_copy(src, hold, in_sem.at[2 + i]) for i, (src, hold, _) in enumerate(pairs)]
    stores = [pltpu.make_async_copy(hold, dst, out_sem.at[i]) for i, (_, hold, dst) in enumerate(pairs)]
    load_low = pltpu.make_async_copy(in_w.at[low], vw.at[low], in_sem.at[1])
    store_low = pltpu.make_async_copy(vw.at[low], out_w.at[low], out_sem.at[4])
    load_off.start()

    @pl.when(r == 0)
    def _():
        load_q.start()

    @pl.when(r == 1)
    def _():
        load_low.start()

    for load in loads:
        load.start()
    load_off.wait()

    @pl.when(r == 0)
    def _():
        pair = s - core
        first_rows = jnp.clip(off[pair + 1] - off[pair] - half, 0, half)
        live = off[s + 1] - off[s] - half
        load_q.wait()

        @pl.loop(0, vq.shape[0] // SUB)
        def _(j):
            rows = pl.ds(pl.multiple_of(j * SUB, SUB), SUB)
            wide[rows, :] = vq[rows, :].astype(jnp.float32)

        @pl.loop(0, half // SUB)
        def _(j):
            row = j * SUB + lax.broadcasted_iota(jnp.int32, (SUB, 128), 0)
            mine = jnp.where(row < live, wide[pl.ds(core * first_rows + j * SUB, SUB), :], 0.0)
            vw[pl.ds(pl.multiple_of(half + j * SUB, SUB), SUB), :] = mine.astype(jnp.bfloat16)

    @pl.when(r == 1)
    def _():
        load_low.wait()

    store_low.start()
    for load, store in zip(loads, stores):
        load.wait()
        store.start()
    for store in stores:
        store.wait()
    store_low.wait()


def local(old_master, old_first, old_second, grad_parts, old_offsets, new_offsets):
    new_cap, lanes = grad_parts.shape[1:]
    half = new_cap // 2
    hbm = pl.BlockSpec(memory_space=pltpu.HBM)
    free = pl.BlockSpec(memory_space=pl.ANY)
    state = jax.ShapeDtypeStruct((half, lanes), jnp.float32)
    dma = pltpu.SemaphoreType.DMA
    shapes = (state, state, state, jax.ShapeDtypeStruct((new_cap, lanes), jnp.bfloat16))
    short = jax.ShapeDtypeStruct((2 * PACK, lanes), jnp.bfloat16)
    results = pl.pallas_call(
        kernel,
        out_shape=shapes + (short,),
        in_specs=[hbm] * 6,
        out_specs=(free,) * 5,
        scratch_shapes=[
            pltpu.SMEM(old_offsets.shape, jnp.int32),
            pltpu.SMEM(new_offsets.shape, jnp.int32),
            pltpu.VMEM((3, WINDOW, lanes), jnp.float32),
            pltpu.VMEM((3, WINDOW, lanes), jnp.float32),
            pltpu.VMEM((2, 3, EDGE // 4, lanes), jnp.float32),
            pltpu.VMEM((3 * EDGE, lanes), jnp.float32),
            pltpu.VMEM((3 * EDGE, lanes), jnp.float32),
            pltpu.VMEM((3 * EDGE, lanes), jnp.float32),
            pltpu.VMEM((3, EDGE, lanes), jnp.float32),
            pltpu.VMEM((half, lanes), jnp.float32),
            pltpu.VMEM((half, lanes), jnp.float32),
            pltpu.VMEM((PACK, lanes), jnp.float32),
            pltpu.VMEM((half + PACK, lanes), jnp.float32),
            pltpu.VMEM((PACK, lanes), jnp.float32),
            pltpu.VMEM((2 * half, lanes), jnp.float32),
            pltpu.VMEM((PACK, lanes), jnp.bfloat16),
            pltpu.VMEM((2 * PACK, lanes), jnp.bfloat16),
            pltpu.VMEM((3, half, lanes), jnp.float32),
            pltpu.VMEM((half, lanes), jnp.bfloat16),
            dma((2,)),
            dma((3,)),
            dma,
            dma((3,)),
            dma((2, 3)),
            dma((2, 4, 3)),
            dma((2, 4, 3)),
            dma((2, 3)),
            dma((2, 3)),
            dma((3,)),
            dma((2, CHUNKS)),
            dma((CHUNKS,)),
            dma((CHUNKS,)),
            dma((CHUNKS,)),
            dma((CHUNKS,)),
            dma((3, CHUNKS)),
            dma((CHUNKS,)),
            dma((CHUNKS,)),
        ],
        compiler_params=pltpu.CompilerParams(
            collective_id=0, has_side_effects=True, vmem_limit_bytes=60 * 1024 * 1024
        ),
        name="move_and_update",
    )(old_offsets, new_offsets, old_master, old_first, old_second, grad_parts)
    master, first, second, weights = pl.pallas_call(
        finish,
        out_shape=shapes,
        in_specs=[hbm] * 6,
        out_specs=(hbm,) * 4,
        scratch_shapes=[pltpu.SMEM(new_offsets.shape, jnp.int32)]
        + [pltpu.VMEM(shape.shape, shape.dtype) for shape in shapes + (short,)]
        + [pltpu.VMEM((new_cap, lanes), jnp.float32), dma((6,)), dma((5,))],
        compiler_params=pltpu.CompilerParams(vmem_limit_bytes=60 * 1024 * 1024),
        name="finish",
    )(new_offsets, *results)
    return (master[None, None], first[None, None], second[None, None], weights)


def solution(mesh):
    in_specs = (
        P("shard", None),
        P("shard", None),
        P("shard", None),
        P("rep", "shard", None),
        P(),
        P(),
    )
    out_specs = (
        P("shard", "rep", None, None),
        P("shard", "rep", None, None),
        P("shard", "rep", None, None),
        P("shard", None),
    )
    return jax.shard_map(local, mesh=mesh, in_specs=in_specs, out_specs=out_specs, check_vma=False)
```

```python
import functools

import jax
import jax.numpy as jnp
from jax import lax
from jax.experimental import pallas as pl
from jax.experimental.pallas import tpu as pltpu
from jax.sharding import PartitionSpec as P

STEP = 10
MESH = pl.DeviceIdType.MESH
JITTER = 512
EDGE = 2 * JITTER
PACK = 1024
WINDOW = 3584
CHUNKS = 8
SUB = 64
EARLY = 3


def within(start):
    return jnp.clip(start, 0, 2 * EDGE)


def kernel(
    old_off_in,
    new_off_in,
    old_m,
    old_f,
    old_s,
    grads,
    out_m,
    out_f,
    out_s,
    out_w,
    out_q,
    old_off,
    new_off,
    main,
    alt,
    relay,
    stage_m,
    stage_f,
    stage_s,
    edge,
    mine,
    theirs,
    near_rows,
    far_rows,
    pack,
    packed,
    short_pack,
    short_packed,
    res,
    wts,
    off_sem,
    in_sem,
    mine_sem,
    stage_sem,
    die_sem,
    head_sem,
    tail_sem,
    head_relay_sem,
    tail_relay_sem,
    pack_sem,
    pass_sem,
    grad_send,
    grad_recv,
    wts_send,
    wts_recv,
    res_sem,
    own_sem,
    short_sem,
):
    olds = (old_m, old_f, old_s)
    outs = (out_m, out_f, out_s)
    stages = (stage_m, stage_f, stage_s)
    old_cap = old_m.shape[0]
    half = mine.shape[0]
    size = half // CHUNKS
    r = lax.axis_index("rep")
    s = lax.axis_index("shard")
    owners = lax.axis_size("shard") // 2
    o = s // 2
    core = s % 2
    even = core == 0
    odd = core == 1
    other = (1 - r, s)

    x = o % 4

    up_rep = r
    down_rep = r
    sends_head = even & (up_rep == 0) & (o < owners - 1)
    gets_head = even & (r == 0) & (o > 0)
    sends_tail = even & (o > 0)
    gets_tail = odd & (o < owners - 1)
    count = 2 * owners
    head_to = (up_rep, lax.rem(s + 2, count))
    head_from = (down_rep, lax.rem(s + count - 2, count))
    tail_to = (down_rep, lax.rem(s + count - 1, count))
    tail_from = (up_rep, lax.rem(s + 1, count))
    die_to = (r, s + 1 - 2 * core)

    z_lo = (o // 4) % 4
    turn_up = jnp.where(z_lo == 3, 32, 0)
    turn_down = jnp.where(z_lo == 0, 32, 0)
    head_wraps = sends_head & (x == 3)
    head_unwraps = gets_head & (x == 0)
    tail_wraps = sends_tail & (x == 0)
    tail_unwraps = gets_tail & (x == 3)
    head_source = s - 1 + 2 * (3 - x) - turn_up
    head_rep = r
    relays_head = odd & (head_rep == 0) & (head_source >= 0)
    tail_source = s - 1 - 2 * x + turn_down
    tail_rep = r
    relays_tail = odd & (tail_source < count)
    head_relays = s + jnp.where(z_lo == 0, 24, -8) + 1
    tail_relays = s + jnp.where(z_lo == 3, -24, 8) - 6

    offsets = (
        pltpu.make_async_copy(old_off_in, old_off, off_sem.at[0]),
        pltpu.make_async_copy(new_off_in, new_off, off_sem.at[1]),
    )
    for copy in offsets:
        copy.start()
    my_grads = pltpu.make_async_copy(grads.at[0, pl.ds(r * half, half)], mine, mine_sem)

    def load_own(k, rep):
        if rep == 0:
            return pltpu.make_async_copy(
                olds[k].at[pl.ds(0, WINDOW - EDGE)], main.at[k, pl.ds(EDGE, WINDOW - EDGE)], in_sem.at[k]
            )
        return pltpu.make_async_copy(olds[k].at[pl.ds(JITTER, WINDOW)], main.at[k], in_sem.at[k])

    def load_stage(k):
        rows = stage_m.shape[0]
        return pltpu.make_async_copy(olds[k].at[pl.ds(old_cap - rows, rows)], stages[k], stage_sem.at[k])

    def die_copy(k, rep):
        first = 1024 if rep == 0 else 2560
        rows = min(WINDOW, old_cap - first)
        return pltpu.make_async_remote_copy(
            olds[k].at[pl.ds(first, rows)],
            main.at[k, pl.ds(0, rows)],
            die_sem.at[0, k],
            die_sem.at[1, k],
            device_id=die_to,
            device_id_type=MESH,
        )

    def send(src, dst, sems, to):
        return pltpu.make_async_remote_copy(src, dst, sems[0], sems[1], device_id=to, device_id_type=MESH)

    quarter = EDGE // 4

    def head_copy(k, part=None):
        rows = pl.ds(0, EDGE) if part is None else pl.ds(part * quarter, quarter)
        at = 0 if part is None else part
        sems = (head_sem.at[0, at, k], head_sem.at[1, at, k])
        return send(edge.at[k, rows], main.at[k, rows], sems, head_to)

    def head_relay_in(k, part):
        rows = pl.ds(part * quarter, quarter)
        sems = (head_sem.at[0, part, k], head_relay_sem.at[0, k])
        to = (r, lax.rem(s - 2 * (3 - part) + 1 + turn_up + count, count))
        return send(edge.at[k, rows], relay.at[0, k], sems, to)

    def head_relay_out(k, part):
        rows = pl.ds(part * quarter, quarter)
        sems = (head_relay_sem.at[1, k], head_sem.at[1, part, k])
        return send(relay.at[0, k], main.at[k, rows], sems, (head_rep, lax.rem(head_source + 2, count)))

    def tail_place(rep):
        return (3072, JITTER) if rep == 0 else (1536, EDGE)

    def tail_copy(k, rep, part=None):
        first, rows = tail_place(rep)
        begin = 0
        if part is not None:
            rows //= 4
            begin = part * rows
        at = 0 if part is None else part
        sems = (tail_sem.at[0, at, k], tail_sem.at[1, at, k])
        return send(olds[k].at[pl.ds(begin, rows)], alt.at[k, pl.ds(first + begin, rows)], sems, tail_to)

    def tail_relay_in(k, rep, part):
        rows = tail_place(rep)[1] // 4
        sems = (tail_sem.at[0, part, k], tail_relay_sem.at[0, k])
        to = (r, lax.rem(s + 2 * part + 1 - turn_down + count, count))
        return send(olds[k].at[pl.ds(part * rows, rows)], relay.at[1, k, pl.ds(0, rows)], sems, to)

    def tail_relay_out(k, rep, part):
        first, rows = tail_place(rep)
        rows //= 4
        sems = (tail_relay_sem.at[1, k], tail_sem.at[1, part, k])
        to = (tail_rep, lax.rem(tail_source + count - 1, count))
        return send(relay.at[1, k, pl.ds(0, rows)], alt.at[k, pl.ds(first + part * rows, rows)], sems, to)

    piece = PACK // CHUNKS

    def grad_copy(c, rep):
        if rep == 1:
            rows = pl.ds(pl.multiple_of(c * size, 16), size)
            src, dst = grads.at[0, rows], theirs.at[rows]
        else:
            src = pack.at[pl.ds(pl.multiple_of(c * piece, 16), piece)]
            dst = packed.at[pl.ds(pl.multiple_of(core * PACK + c * piece, 16), piece)]
        return send(src, dst, (grad_send.at[c], grad_recv.at[c]), other)

    def pass_copy(c):
        rows = packed.at[pl.ds(pl.multiple_of(core * PACK + c * piece, 16), piece)]
        return send(rows, rows, (pass_sem.at[0, c], pass_sem.at[1, c]), die_to)

    def grad_rows(first, rows):
        return grads.at[0, pl.ds(half + first, rows)]

    def master_rows(first, rows):
        return res.at[0, pl.ds(first, rows)]

    def near_copy(at, source):
        if at == 0:
            return pltpu.make_async_copy(source(0, PACK), near_rows, pack_sem.at[0])
        rows = half - PACK
        return send(source(PACK, rows), near_rows.at[pl.ds(0, rows)], (pack_sem.at[1], pack_sem.at[2]), die_to)

    def far_copy(at, source):
        if at == 1:
            return pltpu.make_async_copy(source(0, half), far_rows.at[pl.ds(half - PACK, half)], pack_sem.at[0])
        return send(source(0, PACK), far_rows.at[pl.ds(half, PACK)], (pack_sem.at[1], pack_sem.at[2]), die_to)

    def pack_rows(at):
        row = core * PACK + at + lax.broadcasted_iota(jnp.int32, (SUB, 128), 0)
        far = far_rows[pl.ds(half - first_rows + at, SUB), :]
        return jnp.where(row < first_rows, near_rows[pl.ds(pl.multiple_of(at, SUB), SUB), :], far)

    def short_copy(c):
        src = short_pack.at[pl.ds(pl.multiple_of(c * piece, 16), piece)]
        dst = short_packed.at[pl.ds(pl.multiple_of(core * PACK + c * piece, 16), piece)]
        return send(src, dst, (wts_send.at[c], wts_recv.at[c]), other)

    def short_place(c, at):
        return pl.ds(pl.multiple_of(at * PACK + c * piece, 16), piece)

    def short_pass(c, at):
        rows = short_place(c, at)
        return send(short_packed.at[rows], out_q.at[rows], (pass_sem.at[0, c], pass_sem.at[1, c]), die_to)

    def short_keep(c):
        rows = short_place(c, core)
        return pltpu.make_async_copy(short_packed.at[rows], out_q.at[rows], short_sem.at[c])

    def start_grads(first, last):
        for rep in (0, 1):

            @pl.when(r == rep)
            def _():
                @pl.loop(first, last)
                def _(c):
                    grad_copy(c, rep).start()

    def wts_copy(c):
        first = pl.multiple_of(c * size, 16)
        return pltpu.make_async_remote_copy(
            wts.at[pl.ds(first, size)],
            out_w.at[pl.ds(pl.multiple_of(r * half + first, 16), size)],
            wts_send.at[c],
            wts_recv.at[c],
            device_id=other,
            device_id_type=MESH,
        )

    def wts_arrival(c):
        first = pl.multiple_of(c * size, 16)
        return pltpu.make_async_remote_copy(
            wts.at[pl.ds(first, size)],
            out_w.at[pl.ds(pl.multiple_of((1 - r) * half + first, 16), size)],
            wts_send.at[c],
            wts_recv.at[c],
            device_id=other,
            device_id_type=MESH,
        )

    def own_copy(c):
        first = pl.multiple_of(c * size, 16)
        return pltpu.make_async_copy(
            wts.at[pl.ds(first, size)],
            out_w.at[pl.ds(pl.multiple_of(r * half + first, 16), size)],
            own_sem.at[c],
        )

    def res_copy(k, c):
        first = pl.multiple_of(c * size, 16)
        return pltpu.make_async_copy(
            res.at[k, pl.ds(first, size)], outs[k].at[pl.ds(first, size)], res_sem.at[k, c]
        )

    @pl.when(sends_head)
    def _():
        for k in range(3):
            load_stage(k).start()

    @pl.when((r == 0) & even)
    def _():
        near_copy(0, grad_rows).start()

    @pl.when((r == 0) & odd)
    def _():
        far_copy(1, grad_rows).start()

    barrier = pltpu.get_barrier_semaphore()
    pl.semaphore_signal(barrier, inc=1, device_id=other, device_id_type=MESH)

    pl.semaphore_signal(barrier, inc=1, device_id=die_to, device_id_type=MESH)

    @pl.when(gets_head & (x > 0))
    def _():
        pl.semaphore_signal(barrier, inc=1, device_id=head_from, device_id_type=MESH)

    @pl.when(head_unwraps)
    def _():
        for part in range(4):
            at = lax.rem(head_relays + 2 * part + count, count)
            pl.semaphore_signal(barrier, inc=1, device_id=(down_rep, at), device_id_type=MESH)

    @pl.when(gets_tail & (x < 3))
    def _():
        pl.semaphore_signal(barrier, inc=1, device_id=tail_from, device_id_type=MESH)

    @pl.when(tail_unwraps)
    def _():
        for part in range(4):
            at = lax.rem(tail_relays + 2 * part + count, count)
            pl.semaphore_signal(barrier, inc=1, device_id=(up_rep, at), device_id_type=MESH)

    @pl.when(relays_head)
    def _():
        pl.semaphore_signal(barrier, inc=1, device_id=(r, lax.rem(head_source + count, count)), device_id_type=MESH)

    @pl.when(relays_tail)
    def _():
        pl.semaphore_signal(barrier, inc=1, device_id=(r, lax.rem(tail_source, count)), device_id_type=MESH)

    targets = 2
    for cond, more in (
        (sends_head, 1),
        (head_wraps, 3),
        (sends_tail, 1),
        (tail_wraps, 3),
        (relays_head, 1),
        (relays_tail, 1),
    ):
        targets = targets + more * cond.astype(jnp.int32)
    pl.semaphore_wait(barrier, targets)

    early = EARLY

    @pl.when(r == 1)
    def _():
        @pl.loop(0, early)
        def _(c):
            grad_copy(c, 1).start()

    @pl.when((r == 0) & even)
    def _():
        near_copy(1, grad_rows).start()

    @pl.when((r == 0) & odd)
    def _():
        far_copy(0, grad_rows).start()

    for rep in (0, 1):

        @pl.when(tail_wraps & (down_rep == rep))
        def _():
            for part in range(4):
                for k in range(3):
                    tail_relay_in(k, rep, part).start()

    for copy in offsets:
        copy.wait()

    pair = s - core
    first_rows = jnp.clip(new_off[pair + 1] - new_off[pair] - half, 0, half)

    @pl.when((r == 0) & even)
    def _():
        near_copy(0, grad_rows).wait()
        far_copy(0, grad_rows).wait_recv()

    @pl.when((r == 0) & odd)
    def _():
        far_copy(1, grad_rows).wait()
        near_copy(1, grad_rows).wait_recv()

    @pl.when(r == 0)
    def _():
        @pl.loop(0, PACK // SUB)
        def _(j):
            pack[pl.ds(pl.multiple_of(j * SUB, SUB), SUB), :] = pack_rows(j * SUB)

    @pl.when(r == 0)
    def _():
        @pl.loop(0, CHUNKS)
        def _(c):
            grad_copy(c, 0).start()

    @pl.when(sends_head)
    def _():
        begin = within(old_off[o + 1] - old_off[o] - (old_cap - stage_m.shape[0]) - EDGE)
        for k in range(3):
            load_stage(k).wait()

            @pl.loop(0, EDGE // SUB)
            def _(j):
                edge[k, pl.ds(pl.multiple_of(j * SUB, SUB), SUB), :] = stages[k][pl.ds(begin + j * SUB, SUB), :]

            @pl.when(x < 3)
            def _():
                head_copy(k).start()

            @pl.when(x == 3)
            def _():
                for part in range(4):
                    head_relay_in(k, part).start()

    for rep in (0, 1):

        @pl.when(sends_tail & (down_rep == rep) & (x > 0))
        def _():
            for k in range(3):
                tail_copy(k, rep).start()

    for rep in (0, 1):

        @pl.when(even & (r == rep))
        def _():
            for k in range(3):
                die_copy(k, rep).start()

    for rep in (0, 1):

        @pl.when(even & (r == rep))
        def _():
            for k in range(3):
                load_own(k, rep).start()

    my_grads.start()

    for part in range(4):

        @pl.when(relays_head & (x == part))
        def _():
            for k in range(3):
                head_relay_in(k, part).wait_recv()
                head_relay_out(k, part).start()

    for rep in (0, 1):
        for part in range(4):

            @pl.when(relays_tail & (tail_rep == rep) & (x == part))
            def _():
                for k in range(3):
                    tail_relay_in(k, rep, part).wait_recv()
                    tail_relay_out(k, rep, part).start()

    @pl.when((r == 1) & odd)
    def _():
        @pl.loop(early, CHUNKS)
        def _(c):
            grad_copy(c, 1).start()

    passes = jnp.where(even, CHUNKS, (half - PACK) // piece)
    arrivals = jnp.where(odd, CHUNKS, (half - PACK) // piece)

    @pl.when(r == 1)
    def _():
        @pl.loop(0, CHUNKS)
        def _(c):
            grad_copy(c, 0).wait_recv()

            @pl.when(even & (c == 0))
            def _():
                @pl.loop(early, CHUNKS)
                def _(d):
                    grad_copy(d, 1).start()

            @pl.when(c < passes)
            def _():
                pass_copy(c).start()

    for rep in (0, 1):

        @pl.when(even & (r == rep))
        def _():
            for k in range(3):
                load_own(k, rep).wait()

        @pl.when(odd & (r == rep))
        def _():
            for k in range(3):
                die_copy(k, rep).wait_recv()

    @pl.when(gets_head & (x > 0))
    def _():
        for k in range(3):
            head_copy(k).wait_recv()

    @pl.when(head_unwraps)
    def _():
        for part in range(4):
            for k in range(3):
                head_copy(k, part).wait_recv()

    for rep in (0, 1):

        @pl.when(gets_tail & (r == rep) & (x < 3))
        def _():
            for k in range(3):
                tail_copy(k, rep).wait_recv()

        @pl.when(tail_unwraps & (r == rep))
        def _():
            for part in range(4):
                for k in range(3):
                    tail_copy(k, rep, part).wait_recv()

    my_grads.wait()

    start = within(new_off[s] - old_off[o] + EDGE - 2 * EDGE * core)
    edge_start = within(new_off[s] - old_off[o + 1] + 2 * half)
    split = jnp.where(even, new_off[s + 1], old_off[o + 1])
    flat = new_off[s] + r * half
    stop = new_off[s + 1]

    def update(c, their_rows):
        @pl.loop(0, size // SUB)
        def _(j):
            at = c * size + j * SUB
            rows = pl.ds(pl.multiple_of(at, SUB), SUB)
            row = flat + at + lax.broadcasted_iota(jnp.int32, (SUB, 128), 0)
            near = row < split
            keep = row < stop
            master, first, second = [
                jnp.where(near, main[k, pl.ds(start + at, SUB), :], alt[k, pl.ds(edge_start + at, SUB), :])
                for k in range(3)
            ]
            total = mine[rows, :] + their_rows(at)
            first_n = 0.9 * first + 0.1 * total
            second_n = 0.95 * second + 0.05 * total * total
            first_hat = first_n / (1.0 - 0.9**STEP)
            second_hat = second_n / (1.0 - 0.95**STEP)
            master_n = master - 0.02 * (first_hat / (jnp.sqrt(second_hat) + 1e-08) + 0.1 * master)
            master_n = jnp.where(keep, master_n, 0.0)
            res[0, rows, :] = master_n
            res[1, rows, :] = jnp.where(keep, first_n, 0.0)
            res[2, rows, :] = jnp.where(keep, second_n, 0.0)
            wts[rows, :] = master_n.astype(jnp.bfloat16)

        own_copy(c).start()
        for k in range(3):
            res_copy(k, c).start()

    @pl.when(r == 0)
    def _():
        @pl.loop(0, CHUNKS)
        def _(c):
            grad_copy(c, 1).wait_recv()
            update(c, lambda at: theirs[pl.ds(pl.multiple_of(at, SUB), SUB), :])
            wts_copy(c).start()

        @pl.loop(0, CHUNKS)
        def _(c):
            short_copy(c).wait_recv()
            short_keep(c).start()

            @pl.when(c < passes)
            def _():
                short_pass(c, core).start()


    @pl.when(r == 1)
    def _():
        @pl.loop(0, arrivals)
        def _(c):
            there = packed.at[pl.ds(pl.multiple_of((1 - core) * PACK + c * piece, 16), piece)]
            send(there, there, (pass_sem.at[0, c], pass_sem.at[1, c]), die_to).wait_recv()

        @pl.loop(0, CHUNKS)
        def _(c):
            update(c, lambda at: packed[pl.ds(core * first_rows + at, SUB), :])

            @pl.when((c == (PACK - 1) // size) & even)
            def _():
                near_copy(0, master_rows).start()

            @pl.when((c == (PACK - 1) // size) & odd)
            def _():
                far_copy(0, master_rows).start()

        @pl.when(even)
        def _():
            near_copy(1, master_rows).start()
            near_copy(0, master_rows).wait()
            far_copy(0, master_rows).wait_recv()

        @pl.when(odd)
        def _():
            far_copy(1, master_rows).start()
            far_copy(1, master_rows).wait()
            near_copy(1, master_rows).wait_recv()

        @pl.loop(0, CHUNKS)
        def _(c):
            @pl.loop(0, piece // SUB)
            def _(j):
                at = c * piece + j * SUB
                short_pack[pl.ds(pl.multiple_of(at, SUB), SUB), :] = pack_rows(at).astype(jnp.bfloat16)

            short_copy(c).start()


    for rep in (0, 1):

        @pl.when(even & (r == rep))
        def _():
            for k in range(3):
                die_copy(k, rep).wait_send()

    @pl.when(sends_head & (x < 3))
    def _():
        for k in range(3):
            head_copy(k).wait_send()

    @pl.when(head_wraps)
    def _():
        for part in range(4):
            for k in range(3):
                head_copy(k, part).wait_send()

    @pl.when(relays_head)
    def _():
        for k in range(3):
            head_relay_out(k, 0).wait_send()

    for rep in (0, 1):

        @pl.when(sends_tail & (down_rep == rep) & (x > 0))
        def _():
            for k in range(3):
                tail_copy(k, rep).wait_send()

        @pl.when(tail_wraps & (down_rep == rep))
        def _():
            for part in range(4):
                for k in range(3):
                    tail_copy(k, rep, part).wait_send()

        @pl.when(relays_tail & (tail_rep == rep))
        def _():
            for k in range(3):
                tail_relay_out(k, rep, 0).wait_send()

    @pl.when(even)
    def _():
        near_copy(1, grad_rows).wait_send()

    @pl.when(odd)
    def _():
        far_copy(0, grad_rows).wait_send()

    for rep in (0, 1):

        @pl.when(r == rep)
        def _():
            @pl.loop(0, CHUNKS)
            def _(c):
                grad_copy(c, rep).wait_send()
                own_copy(c).wait()
                for k in range(3):
                    res_copy(k, c).wait()

    @pl.when(r == 0)
    def _():
        @pl.loop(0, CHUNKS)
        def _(c):
            wts_copy(c).wait_send()
            short_keep(c).wait()

        @pl.loop(0, passes)
        def _(c):
            short_pass(c, core).wait_send()

        @pl.loop(0, arrivals)
        def _(c):
            short_pass(c, 1 - core).wait_recv()

    @pl.when(r == 1)
    def _():
        @pl.loop(0, passes)
        def _(c):
            pass_copy(c).wait_send()

        @pl.loop(0, CHUNKS)
        def _(c):
            short_copy(c).wait_send()
            wts_arrival(c).wait_recv()


def finish(
    off_in, in_m, in_f, in_s, in_w, in_q, out_m, out_f, out_s, out_w, off, vm, vf, vs, vw, vq, wide, in_sem, out_sem
):
    r = lax.axis_index("rep")
    s = lax.axis_index("shard")
    core = s % 2
    half = vm.shape[0]
    top, low = pl.ds(0, half), pl.ds(half, half)
    load_off = pltpu.make_async_copy(off_in, off, in_sem.at[0])
    load_q = pltpu.make_async_copy(in_q, vq, in_sem.at[1])
    pairs = [(in_m, vm, out_m), (in_f, vf, out_f), (in_s, vs, out_s), (in_w.at[top], vw.at[top], out_w.at[top])]
    loads = [pltpu.make_async_copy(src, hold, in_sem.at[2 + i]) for i, (src, hold, _) in enumerate(pairs)]
    stores = [pltpu.make_async_copy(hold, dst, out_sem.at[i]) for i, (_, hold, dst) in enumerate(pairs)]
    load_low = pltpu.make_async_copy(in_w.at[low], vw.at[low], in_sem.at[1])
    store_low = pltpu.make_async_copy(vw.at[low], out_w.at[low], out_sem.at[4])
    load_off.start()

    @pl.when(r == 0)
    def _():
        load_q.start()

    @pl.when(r == 1)
    def _():
        load_low.start()

    for load in loads:
        load.start()
    for load, store in zip(loads, stores):
        load.wait()
        store.start()
    load_off.wait()

    @pl.when(r == 0)
    def _():
        pair = s - core
        first_rows = jnp.clip(off[pair + 1] - off[pair] - half, 0, half)
        live = off[s + 1] - off[s] - half
        load_q.wait()

        @pl.loop(0, vq.shape[0] // SUB)
        def _(j):
            rows = pl.ds(pl.multiple_of(j * SUB, SUB), SUB)
            wide[rows, :] = vq[rows, :].astype(jnp.float32)

        @pl.loop(0, half // SUB)
        def _(j):
            row = j * SUB + lax.broadcasted_iota(jnp.int32, (SUB, 128), 0)
            mine = jnp.where(row < live, wide[pl.ds(core * first_rows + j * SUB, SUB), :], 0.0)
            vw[pl.ds(pl.multiple_of(half + j * SUB, SUB), SUB), :] = mine.astype(jnp.bfloat16)

    @pl.when(r == 1)
    def _():
        load_low.wait()

    store_low.start()
    for store in stores:
        store.wait()
    store_low.wait()


def local(old_master, old_first, old_second, grad_parts, old_offsets, new_offsets):
    new_cap, lanes = grad_parts.shape[1:]
    half = new_cap // 2
    hbm = pl.BlockSpec(memory_space=pltpu.HBM)
    free = pl.BlockSpec(memory_space=pl.ANY)
    state = jax.ShapeDtypeStruct((half, lanes), jnp.float32)
    dma = pltpu.SemaphoreType.DMA
    shapes = (state, state, state, jax.ShapeDtypeStruct((new_cap, lanes), jnp.bfloat16))
    short = jax.ShapeDtypeStruct((2 * PACK, lanes), jnp.bfloat16)
    results = pl.pallas_call(
        kernel,
        out_shape=shapes + (short,),
        in_specs=[hbm] * 6,
        out_specs=(free,) * 5,
        scratch_shapes=[
            pltpu.SMEM(old_offsets.shape, jnp.int32),
            pltpu.SMEM(new_offsets.shape, jnp.int32),
            pltpu.VMEM((3, WINDOW, lanes), jnp.float32),
            pltpu.VMEM((3, WINDOW, lanes), jnp.float32),
            pltpu.VMEM((2, 3, EDGE // 4, lanes), jnp.float32),
            pltpu.VMEM((3 * EDGE, lanes), jnp.float32),
            pltpu.VMEM((3 * EDGE, lanes), jnp.float32),
            pltpu.VMEM((3 * EDGE, lanes), jnp.float32),
            pltpu.VMEM((3, EDGE, lanes), jnp.float32),
            pltpu.VMEM((half, lanes), jnp.float32),
            pltpu.VMEM((half, lanes), jnp.float32),
            pltpu.VMEM((PACK, lanes), jnp.float32),
            pltpu.VMEM((half + PACK, lanes), jnp.float32),
            pltpu.VMEM((PACK, lanes), jnp.float32),
            pltpu.VMEM((2 * half, lanes), jnp.float32),
            pltpu.VMEM((PACK, lanes), jnp.bfloat16),
            pltpu.VMEM((2 * PACK, lanes), jnp.bfloat16),
            pltpu.VMEM((3, half, lanes), jnp.float32),
            pltpu.VMEM((half, lanes), jnp.bfloat16),
            dma((2,)),
            dma((3,)),
            dma,
            dma((3,)),
            dma((2, 3)),
            dma((2, 4, 3)),
            dma((2, 4, 3)),
            dma((2, 3)),
            dma((2, 3)),
            dma((3,)),
            dma((2, CHUNKS)),
            dma((CHUNKS,)),
            dma((CHUNKS,)),
            dma((CHUNKS,)),
            dma((CHUNKS,)),
            dma((3, CHUNKS)),
            dma((CHUNKS,)),
            dma((CHUNKS,)),
        ],
        compiler_params=pltpu.CompilerParams(
            collective_id=0, has_side_effects=True, vmem_limit_bytes=60 * 1024 * 1024
        ),
        name="move_and_update",
    )(old_offsets, new_offsets, old_master, old_first, old_second, grad_parts)
    master, first, second, weights = pl.pallas_call(
        finish,
        out_shape=shapes,
        in_specs=[hbm] * 6,
        out_specs=(hbm,) * 4,
        scratch_shapes=[pltpu.SMEM(new_offsets.shape, jnp.int32)]
        + [pltpu.VMEM(shape.shape, shape.dtype) for shape in shapes + (short,)]
        + [pltpu.VMEM((new_cap, lanes), jnp.float32), dma((6,)), dma((5,))],
        compiler_params=pltpu.CompilerParams(vmem_limit_bytes=60 * 1024 * 1024),
        name="finish",
    )(new_offsets, *results)
    return (master[None, None], first[None, None], second[None, None], weights)


def solution(mesh):
    in_specs = (
        P("shard", None),
        P("shard", None),
        P("shard", None),
        P("rep", "shard", None),
        P(),
        P(),
    )
    out_specs = (
        P("shard", "rep", None, None),
        P("shard", "rep", None, None),
        P("shard", "rep", None, None),
        P("shard", None),
    )
    return jax.shard_map(local, mesh=mesh, in_specs=in_specs, out_specs=out_specs, check_vma=False)
```

```python
import functools

import jax
import jax.numpy as jnp
from jax import lax
from jax.experimental import pallas as pl
from jax.experimental.pallas import tpu as pltpu
from jax.sharding import PartitionSpec as P

STEP = 10
MESH = pl.DeviceIdType.MESH
JITTER = 512
EDGE = 2 * JITTER
PACK = 1024
WINDOW = 3584
CHUNKS = 8
SUB = 64
EARLY = 4
PROMPT = 5


def within(start):
    return jnp.clip(start, 0, 2 * EDGE)


def kernel(
    old_off_in,
    new_off_in,
    old_m,
    old_f,
    old_s,
    grads,
    out_m,
    out_f,
    out_s,
    out_w,
    out_q,
    old_off,
    new_off,
    main,
    alt,
    relay,
    stage_m,
    stage_f,
    stage_s,
    edge,
    mine,
    theirs,
    near_rows,
    far_rows,
    pack,
    packed,
    short_pack,
    short_packed,
    res,
    wts,
    off_sem,
    in_sem,
    mine_sem,
    stage_sem,
    die_sem,
    head_sem,
    tail_sem,
    head_relay_sem,
    tail_relay_sem,
    pack_sem,
    pass_sem,
    grad_send,
    grad_recv,
    wts_send,
    wts_recv,
    res_sem,
    own_sem,
    short_sem,
):
    olds = (old_m, old_f, old_s)
    outs = (out_m, out_f, out_s)
    stages = (stage_m, stage_f, stage_s)
    old_cap = old_m.shape[0]
    half = mine.shape[0]
    size = half // CHUNKS
    r = lax.axis_index("rep")
    s = lax.axis_index("shard")
    owners = lax.axis_size("shard") // 2
    o = s // 2
    core = s % 2
    even = core == 0
    odd = core == 1
    other = (1 - r, s)

    x = o % 4

    up_rep = r
    down_rep = r
    sends_head = even & (up_rep == 0) & (o < owners - 1)
    gets_head = even & (r == 0) & (o > 0)
    sends_tail = even & (o > 0)
    gets_tail = odd & (o < owners - 1)
    count = 2 * owners
    head_to = (up_rep, lax.rem(s + 2, count))
    head_from = (down_rep, lax.rem(s + count - 2, count))
    tail_to = (down_rep, lax.rem(s + count - 1, count))
    tail_from = (up_rep, lax.rem(s + 1, count))
    die_to = (r, s + 1 - 2 * core)

    z_lo = (o // 4) % 4
    turn_up = jnp.where(z_lo == 3, 32, 0)
    turn_down = jnp.where(z_lo == 0, 32, 0)
    head_wraps = sends_head & (x == 3)
    head_unwraps = gets_head & (x == 0)
    tail_wraps = sends_tail & (x == 0)
    tail_unwraps = gets_tail & (x == 3)
    head_source = s - 1 + 2 * (3 - x) - turn_up
    head_rep = r
    relays_head = odd & (head_rep == 0) & (head_source >= 0)
    tail_source = s - 2 * x + turn_down
    tail_rep = r
    relays_tail = even & (tail_source < count) & ((x > 0) | (z_lo == 0))
    head_relays = s + jnp.where(z_lo == 0, 24, -8) + 1
    tail_relays = s + jnp.where(z_lo == 3, -24, 8) - 7

    offsets = (
        pltpu.make_async_copy(old_off_in, old_off, off_sem.at[0]),
        pltpu.make_async_copy(new_off_in, new_off, off_sem.at[1]),
    )
    for copy in offsets:
        copy.start()
    my_grads = pltpu.make_async_copy(grads.at[0, pl.ds(r * half, half)], mine, mine_sem)

    def load_own(k, rep):
        if rep == 0:
            return pltpu.make_async_copy(
                olds[k].at[pl.ds(0, WINDOW - EDGE)], main.at[k, pl.ds(EDGE, WINDOW - EDGE)], in_sem.at[k]
            )
        return pltpu.make_async_copy(olds[k].at[pl.ds(JITTER, WINDOW)], main.at[k], in_sem.at[k])

    def load_stage(k):
        rows = stage_m.shape[0]
        return pltpu.make_async_copy(olds[k].at[pl.ds(old_cap - rows, rows)], stages[k], stage_sem.at[k])

    def die_copy(k, rep):
        first = 1024 if rep == 0 else 2560
        rows = min(WINDOW, old_cap - first)
        return pltpu.make_async_remote_copy(
            olds[k].at[pl.ds(first, rows)],
            main.at[k, pl.ds(0, rows)],
            die_sem.at[0, k],
            die_sem.at[1, k],
            device_id=die_to,
            device_id_type=MESH,
        )

    def send(src, dst, sems, to):
        return pltpu.make_async_remote_copy(src, dst, sems[0], sems[1], device_id=to, device_id_type=MESH)

    quarter = EDGE // 4

    def head_copy(k, part=None):
        rows = pl.ds(0, EDGE) if part is None else pl.ds(part * quarter, quarter)
        at = 0 if part is None else part
        sems = (head_sem.at[0, at, k], head_sem.at[1, at, k])
        return send(edge.at[k, rows], main.at[k, rows], sems, head_to)

    def head_relay_in(k, part):
        rows = pl.ds(part * quarter, quarter)
        sems = (head_sem.at[0, part, k], head_relay_sem.at[0, k])
        to = (r, lax.rem(s - 2 * (3 - part) + 1 + turn_up + count, count))
        return send(edge.at[k, rows], relay.at[0, k], sems, to)

    def head_relay_out(k, part):
        rows = pl.ds(part * quarter, quarter)
        sems = (head_relay_sem.at[1, k], head_sem.at[1, part, k])
        return send(relay.at[0, k], main.at[k, rows], sems, (head_rep, lax.rem(head_source + 2, count)))

    def tail_place(rep):
        return (3072, JITTER) if rep == 0 else (1536, EDGE)

    def tail_copy(k, rep, part=None):
        first, rows = tail_place(rep)
        begin = 0
        if part is not None:
            rows //= 4
            begin = part * rows
        at = 0 if part is None else part
        sems = (tail_sem.at[0, at, k], tail_sem.at[1, at, k])
        return send(olds[k].at[pl.ds(begin, rows)], alt.at[k, pl.ds(first + begin, rows)], sems, tail_to)

    def tail_relay_in(k, rep, part):
        rows = tail_place(rep)[1] // 4
        sems = (tail_sem.at[0, part, k], tail_relay_sem.at[0, k])
        to = (r, lax.rem(s + 2 * part - turn_down + count, count))
        return send(olds[k].at[pl.ds(part * rows, rows)], relay.at[1, k, pl.ds(0, rows)], sems, to)

    def tail_relay_out(k, rep, part):
        first, rows = tail_place(rep)
        rows //= 4
        sems = (tail_relay_sem.at[1, k], tail_sem.at[1, part, k])
        to = (tail_rep, lax.rem(tail_source + count - 1, count))
        return send(relay.at[1, k, pl.ds(0, rows)], alt.at[k, pl.ds(first + part * rows, rows)], sems, to)

    piece = PACK // CHUNKS

    def grad_copy(c, rep):
        if rep == 1:
            rows = pl.ds(pl.multiple_of(c * size, 16), size)
            src, dst = grads.at[0, rows], theirs.at[rows]
        else:
            src = pack.at[pl.ds(pl.multiple_of(c * piece, 16), piece)]
            dst = packed.at[pl.ds(pl.multiple_of(core * PACK + c * piece, 16), piece)]
        return send(src, dst, (grad_send.at[c], grad_recv.at[c]), other)

    def pass_copy(c):
        rows = packed.at[pl.ds(pl.multiple_of(core * PACK + c * piece, 16), piece)]
        return send(rows, rows, (pass_sem.at[0, c], pass_sem.at[1, c]), die_to)

    def grad_rows(first, rows):
        return grads.at[0, pl.ds(half + first, rows)]

    def master_rows(first, rows):
        return res.at[0, pl.ds(first, rows)]

    def near_copy(at, source):
        if at == 0:
            return pltpu.make_async_copy(source(0, PACK), near_rows, pack_sem.at[0])
        rows = half - PACK
        return send(source(PACK, rows), near_rows.at[pl.ds(0, rows)], (pack_sem.at[1], pack_sem.at[2]), die_to)

    def far_copy(at, source):
        if at == 1:
            return pltpu.make_async_copy(source(0, half), far_rows.at[pl.ds(half - PACK, half)], pack_sem.at[0])
        return send(source(0, PACK), far_rows.at[pl.ds(half, PACK)], (pack_sem.at[1], pack_sem.at[2]), die_to)

    def pack_rows(at):
        row = core * PACK + at + lax.broadcasted_iota(jnp.int32, (SUB, 128), 0)
        far = far_rows[pl.ds(half - first_rows + at, SUB), :]
        return jnp.where(row < first_rows, near_rows[pl.ds(pl.multiple_of(at, SUB), SUB), :], far)

    def short_copy(c):
        src = short_pack.at[pl.ds(pl.multiple_of(c * piece, 16), piece)]
        dst = short_packed.at[pl.ds(pl.multiple_of(core * PACK + c * piece, 16), piece)]
        return send(src, dst, (wts_send.at[c], wts_recv.at[c]), other)

    def short_place(c, at):
        return pl.ds(pl.multiple_of(at * PACK + c * piece, 16), piece)

    def short_pass(c, at):
        rows = short_place(c, at)
        return send(short_packed.at[rows], out_q.at[rows], (pass_sem.at[0, c], pass_sem.at[1, c]), die_to)

    def short_keep(c):
        rows = short_place(c, core)
        return pltpu.make_async_copy(short_packed.at[rows], out_q.at[rows], short_sem.at[c])

    def start_grads(first, last):
        for rep in (0, 1):

            @pl.when(r == rep)
            def _():
                @pl.loop(first, last)
                def _(c):
                    grad_copy(c, rep).start()

    def wts_copy(c):
        first = pl.multiple_of(c * size, 16)
        return pltpu.make_async_remote_copy(
            wts.at[pl.ds(first, size)],
            out_w.at[pl.ds(pl.multiple_of(r * half + first, 16), size)],
            wts_send.at[c],
            wts_recv.at[c],
            device_id=other,
            device_id_type=MESH,
        )

    def wts_arrival(c):
        first = pl.multiple_of(c * size, 16)
        return pltpu.make_async_remote_copy(
            wts.at[pl.ds(first, size)],
            out_w.at[pl.ds(pl.multiple_of((1 - r) * half + first, 16), size)],
            wts_send.at[c],
            wts_recv.at[c],
            device_id=other,
            device_id_type=MESH,
        )

    def own_copy(c):
        first = pl.multiple_of(c * size, 16)
        return pltpu.make_async_copy(
            wts.at[pl.ds(first, size)],
            out_w.at[pl.ds(pl.multiple_of(r * half + first, 16), size)],
            own_sem.at[c],
        )

    def res_copy(k, c):
        first = pl.multiple_of(c * size, 16)
        return pltpu.make_async_copy(
            res.at[k, pl.ds(first, size)], outs[k].at[pl.ds(first, size)], res_sem.at[k, c]
        )

    @pl.when(sends_head)
    def _():
        for k in range(3):
            load_stage(k).start()

    @pl.when((r == 0) & even)
    def _():
        near_copy(0, grad_rows).start()

    @pl.when((r == 0) & odd)
    def _():
        far_copy(1, grad_rows).start()

    barrier = pltpu.get_barrier_semaphore()
    pl.semaphore_signal(barrier, inc=1, device_id=other, device_id_type=MESH)

    pl.semaphore_signal(barrier, inc=1, device_id=die_to, device_id_type=MESH)

    @pl.when(gets_head & (x > 0))
    def _():
        pl.semaphore_signal(barrier, inc=1, device_id=head_from, device_id_type=MESH)

    @pl.when(head_unwraps)
    def _():
        for part in range(4):
            at = lax.rem(head_relays + 2 * part + count, count)
            pl.semaphore_signal(barrier, inc=1, device_id=(down_rep, at), device_id_type=MESH)

    @pl.when(gets_tail & (x < 3))
    def _():
        pl.semaphore_signal(barrier, inc=1, device_id=tail_from, device_id_type=MESH)

    @pl.when(tail_unwraps)
    def _():
        for part in range(4):
            at = lax.rem(tail_relays + 2 * part + count, count)
            pl.semaphore_signal(barrier, inc=1, device_id=(up_rep, at), device_id_type=MESH)

    @pl.when(relays_head)
    def _():
        pl.semaphore_signal(barrier, inc=1, device_id=(r, lax.rem(head_source + count, count)), device_id_type=MESH)

    @pl.when(relays_tail)
    def _():
        pl.semaphore_signal(barrier, inc=1, device_id=(r, lax.rem(tail_source, count)), device_id_type=MESH)

    targets = 2
    for cond, more in (
        (sends_head, 1),
        (head_wraps, 3),
        (sends_tail, 1),
        (tail_wraps, 3),
        (relays_head, 1),
        (relays_tail, 1),
    ):
        targets = targets + more * cond.astype(jnp.int32)
    pl.semaphore_wait(barrier, targets)

    early = EARLY

    @pl.when(r == 1)
    def _():
        @pl.loop(0, early)
        def _(c):
            grad_copy(c, 1).start()

    @pl.when((r == 0) & even)
    def _():
        near_copy(1, grad_rows).start()

    @pl.when((r == 0) & odd)
    def _():
        far_copy(0, grad_rows).start()

    for rep in (0, 1):

        @pl.when(tail_wraps & (down_rep == rep))
        def _():
            for part in (1, 2, 3):
                for k in range(3):
                    tail_relay_in(k, rep, part).start()

            @pl.when(z_lo == 0)
            def _():
                for k in range(3):
                    tail_relay_in(k, rep, 0).start()

            @pl.when(z_lo > 0)
            def _():
                for k in range(3):
                    tail_copy(k, rep, 0).start()

    for copy in offsets:
        copy.wait()

    pair = s - core
    first_rows = jnp.clip(new_off[pair + 1] - new_off[pair] - half, 0, half)

    @pl.when((r == 0) & even)
    def _():
        near_copy(0, grad_rows).wait()
        far_copy(0, grad_rows).wait_recv()

    @pl.when((r == 0) & odd)
    def _():
        far_copy(1, grad_rows).wait()
        near_copy(1, grad_rows).wait_recv()

    @pl.when(r == 0)
    def _():
        @pl.loop(0, PACK // SUB)
        def _(j):
            pack[pl.ds(pl.multiple_of(j * SUB, SUB), SUB), :] = pack_rows(j * SUB)

    prompt = jnp.where(odd & (z_lo == 3), PROMPT, CHUNKS)

    @pl.when(r == 0)
    def _():
        @pl.loop(0, prompt)
        def _(c):
            grad_copy(c, 0).start()

    @pl.when(sends_head)
    def _():
        begin = within(old_off[o + 1] - old_off[o] - (old_cap - stage_m.shape[0]) - EDGE)
        for k in range(3):
            load_stage(k).wait()

            @pl.loop(0, EDGE // SUB)
            def _(j):
                edge[k, pl.ds(pl.multiple_of(j * SUB, SUB), SUB), :] = stages[k][pl.ds(begin + j * SUB, SUB), :]

            @pl.when(x < 3)
            def _():
                head_copy(k).start()

            @pl.when(x == 3)
            def _():
                for part in range(4):
                    head_relay_in(k, part).start()

    for rep in (0, 1):

        @pl.when(sends_tail & (down_rep == rep) & (x > 0))
        def _():
            for k in range(3):
                tail_copy(k, rep).start()

    for rep in (0, 1):

        @pl.when(even & (r == rep))
        def _():
            for k in range(3):
                die_copy(k, rep).start()

    for rep in (0, 1):

        @pl.when(even & (r == rep))
        def _():
            for k in range(3):
                load_own(k, rep).start()

    my_grads.start()

    for part in range(4):

        @pl.when(relays_head & (x == part))
        def _():
            for k in range(3):
                head_relay_in(k, part).wait_recv()
                head_relay_out(k, part).start()

    for rep in (0, 1):
        for part in range(4):

            @pl.when(relays_tail & (tail_rep == rep) & (x == part))
            def _():
                for k in range(3):
                    tail_relay_in(k, rep, part).wait_recv()
                    tail_relay_out(k, rep, part).start()

    @pl.when(r == 0)
    def _():
        @pl.loop(prompt, CHUNKS)
        def _(c):
            grad_copy(c, 0).start()

    passes = jnp.where(even, CHUNKS, (half - PACK) // piece)
    arrivals = jnp.where(odd, CHUNKS, (half - PACK) // piece)

    @pl.when(r == 1)
    def _():
        @pl.loop(0, CHUNKS)
        def _(c):
            grad_copy(c, 0).wait_recv()

            @pl.when(c == 0)
            def _():
                @pl.loop(early, CHUNKS)
                def _(d):
                    grad_copy(d, 1).start()

            @pl.when(c < passes)
            def _():
                pass_copy(c).start()

    for rep in (0, 1):

        @pl.when(even & (r == rep))
        def _():
            for k in range(3):
                load_own(k, rep).wait()

        @pl.when(odd & (r == rep))
        def _():
            for k in range(3):
                die_copy(k, rep).wait_recv()

    @pl.when(gets_head & (x > 0))
    def _():
        for k in range(3):
            head_copy(k).wait_recv()

    @pl.when(head_unwraps)
    def _():
        for part in range(4):
            for k in range(3):
                head_copy(k, part).wait_recv()

    for rep in (0, 1):

        @pl.when(gets_tail & (r == rep) & (x < 3))
        def _():
            for k in range(3):
                tail_copy(k, rep).wait_recv()

        @pl.when(tail_unwraps & (r == rep))
        def _():
            for part in range(4):
                for k in range(3):
                    tail_copy(k, rep, part).wait_recv()

    my_grads.wait()

    start = within(new_off[s] - old_off[o] + EDGE - 2 * EDGE * core)
    edge_start = within(new_off[s] - old_off[o + 1] + 2 * half)
    split = jnp.where(even, new_off[s + 1], old_off[o + 1])
    flat = new_off[s] + r * half
    stop = new_off[s + 1]

    def update(c, their_rows):
        @pl.loop(0, size // SUB)
        def _(j):
            at = c * size + j * SUB
            rows = pl.ds(pl.multiple_of(at, SUB), SUB)
            row = flat + at + lax.broadcasted_iota(jnp.int32, (SUB, 128), 0)
            near = row < split
            keep = row < stop
            master, first, second = [
                jnp.where(near, main[k, pl.ds(start + at, SUB), :], alt[k, pl.ds(edge_start + at, SUB), :])
                for k in range(3)
            ]
            total = mine[rows, :] + their_rows(at)
            first_n = 0.9 * first + 0.1 * total
            second_n = 0.95 * second + 0.05 * total * total
            first_hat = first_n / (1.0 - 0.9**STEP)
            second_hat = second_n / (1.0 - 0.95**STEP)
            master_n = master - 0.02 * (first_hat / (jnp.sqrt(second_hat) + 1e-08) + 0.1 * master)
            master_n = jnp.where(keep, master_n, 0.0)
            res[0, rows, :] = master_n
            res[1, rows, :] = jnp.where(keep, first_n, 0.0)
            res[2, rows, :] = jnp.where(keep, second_n, 0.0)
            wts[rows, :] = master_n.astype(jnp.bfloat16)

        own_copy(c).start()
        for k in range(3):
            res_copy(k, c).start()

    @pl.when(r == 0)
    def _():
        @pl.loop(0, CHUNKS)
        def _(c):
            grad_copy(c, 1).wait_recv()
            update(c, lambda at: theirs[pl.ds(pl.multiple_of(at, SUB), SUB), :])
            wts_copy(c).start()

        @pl.loop(0, CHUNKS)
        def _(c):
            short_copy(c).wait_recv()
            short_keep(c).start()

            @pl.when(c < passes)
            def _():
                short_pass(c, core).start()


    @pl.when(r == 1)
    def _():
        @pl.loop(0, arrivals)
        def _(c):
            there = packed.at[pl.ds(pl.multiple_of((1 - core) * PACK + c * piece, 16), piece)]
            send(there, there, (pass_sem.at[0, c], pass_sem.at[1, c]), die_to).wait_recv()

        @pl.loop(0, CHUNKS)
        def _(c):
            update(c, lambda at: packed[pl.ds(core * first_rows + at, SUB), :])

            @pl.when((c == (PACK - 1) // size) & even)
            def _():
                near_copy(0, master_rows).start()

            @pl.when((c == (PACK - 1) // size) & odd)
            def _():
                far_copy(0, master_rows).start()

        @pl.when(even)
        def _():
            near_copy(1, master_rows).start()
            near_copy(0, master_rows).wait()
            far_copy(0, master_rows).wait_recv()

        @pl.when(odd)
        def _():
            far_copy(1, master_rows).start()
            far_copy(1, master_rows).wait()
            near_copy(1, master_rows).wait_recv()

        @pl.loop(0, CHUNKS)
        def _(c):
            @pl.loop(0, piece // SUB)
            def _(j):
                at = c * piece + j * SUB
                short_pack[pl.ds(pl.multiple_of(at, SUB), SUB), :] = pack_rows(at).astype(jnp.bfloat16)

            short_copy(c).start()


    for rep in (0, 1):

        @pl.when(even & (r == rep))
        def _():
            for k in range(3):
                die_copy(k, rep).wait_send()

    @pl.when(sends_head & (x < 3))
    def _():
        for k in range(3):
            head_copy(k).wait_send()

    @pl.when(head_wraps)
    def _():
        for part in range(4):
            for k in range(3):
                head_copy(k, part).wait_send()

    @pl.when(relays_head)
    def _():
        for k in range(3):
            head_relay_out(k, 0).wait_send()

    for rep in (0, 1):

        @pl.when(sends_tail & (down_rep == rep) & (x > 0))
        def _():
            for k in range(3):
                tail_copy(k, rep).wait_send()

        @pl.when(tail_wraps & (down_rep == rep))
        def _():
            for part in range(4):
                for k in range(3):
                    tail_copy(k, rep, part).wait_send()

        @pl.when(relays_tail & (tail_rep == rep))
        def _():
            for k in range(3):
                tail_relay_out(k, rep, 0).wait_send()

    @pl.when(even)
    def _():
        near_copy(1, grad_rows).wait_send()

    @pl.when(odd)
    def _():
        far_copy(0, grad_rows).wait_send()

    for rep in (0, 1):

        @pl.when(r == rep)
        def _():
            @pl.loop(0, CHUNKS)
            def _(c):
                grad_copy(c, rep).wait_send()
                own_copy(c).wait()
                for k in range(3):
                    res_copy(k, c).wait()

    @pl.when(r == 0)
    def _():
        @pl.loop(0, CHUNKS)
        def _(c):
            wts_copy(c).wait_send()
            short_keep(c).wait()

        @pl.loop(0, passes)
        def _(c):
            short_pass(c, core).wait_send()

        @pl.loop(0, arrivals)
        def _(c):
            short_pass(c, 1 - core).wait_recv()

    @pl.when(r == 1)
    def _():
        @pl.loop(0, passes)
        def _(c):
            pass_copy(c).wait_send()

        @pl.loop(0, CHUNKS)
        def _(c):
            short_copy(c).wait_send()
            wts_arrival(c).wait_recv()


def finish(
    off_in, in_m, in_f, in_s, in_w, in_q, out_m, out_f, out_s, out_w, off, vm, vf, vs, vw, vq, wide, in_sem, out_sem
):
    r = lax.axis_index("rep")
    s = lax.axis_index("shard")
    core = s % 2
    half = vm.shape[0]
    top, low = pl.ds(0, half), pl.ds(half, half)
    load_off = pltpu.make_async_copy(off_in, off, in_sem.at[0])
    load_q = pltpu.make_async_copy(in_q, vq, in_sem.at[1])
    pairs = [(in_m, vm, out_m), (in_f, vf, out_f), (in_s, vs, out_s), (in_w.at[top], vw.at[top], out_w.at[top])]
    loads = [pltpu.make_async_copy(src, hold, in_sem.at[2 + i]) for i, (src, hold, _) in enumerate(pairs)]
    stores = [pltpu.make_async_copy(hold, dst, out_sem.at[i]) for i, (_, hold, dst) in enumerate(pairs)]
    load_low = pltpu.make_async_copy(in_w.at[low], vw.at[low], in_sem.at[1])
    store_low = pltpu.make_async_copy(vw.at[low], out_w.at[low], out_sem.at[4])
    load_off.start()

    @pl.when(r == 0)
    def _():
        load_q.start()

    @pl.when(r == 1)
    def _():
        load_low.start()

    for load in loads:
        load.start()
    for load, store in zip(loads, stores):
        load.wait()
        store.start()
    load_off.wait()

    @pl.when(r == 0)
    def _():
        pair = s - core
        first_rows = jnp.clip(off[pair + 1] - off[pair] - half, 0, half)
        live = off[s + 1] - off[s] - half
        load_q.wait()

        @pl.loop(0, vq.shape[0] // SUB)
        def _(j):
            rows = pl.ds(pl.multiple_of(j * SUB, SUB), SUB)
            wide[rows, :] = vq[rows, :].astype(jnp.float32)

        @pl.loop(0, half // SUB)
        def _(j):
            row = j * SUB + lax.broadcasted_iota(jnp.int32, (SUB, 128), 0)
            mine = jnp.where(row < live, wide[pl.ds(core * first_rows + j * SUB, SUB), :], 0.0)
            vw[pl.ds(pl.multiple_of(half + j * SUB, SUB), SUB), :] = mine.astype(jnp.bfloat16)

    @pl.when(r == 1)
    def _():
        load_low.wait()

    store_low.start()
    for store in stores:
        store.wait()
    store_low.wait()


def local(old_master, old_first, old_second, grad_parts, old_offsets, new_offsets):
    new_cap, lanes = grad_parts.shape[1:]
    half = new_cap // 2
    hbm = pl.BlockSpec(memory_space=pltpu.HBM)
    free = pl.BlockSpec(memory_space=pl.ANY)
    state = jax.ShapeDtypeStruct((half, lanes), jnp.float32)
    dma = pltpu.SemaphoreType.DMA
    shapes = (state, state, state, jax.ShapeDtypeStruct((new_cap, lanes), jnp.bfloat16))
    short = jax.ShapeDtypeStruct((2 * PACK, lanes), jnp.bfloat16)
    results = pl.pallas_call(
        kernel,
        out_shape=shapes + (short,),
        in_specs=[hbm] * 6,
        out_specs=(free,) * 5,
        scratch_shapes=[
            pltpu.SMEM(old_offsets.shape, jnp.int32),
            pltpu.SMEM(new_offsets.shape, jnp.int32),
            pltpu.VMEM((3, WINDOW, lanes), jnp.float32),
            pltpu.VMEM((3, WINDOW, lanes), jnp.float32),
            pltpu.VMEM((2, 3, EDGE // 4, lanes), jnp.float32),
            pltpu.VMEM((3 * EDGE, lanes), jnp.float32),
            pltpu.VMEM((3 * EDGE, lanes), jnp.float32),
            pltpu.VMEM((3 * EDGE, lanes), jnp.float32),
            pltpu.VMEM((3, EDGE, lanes), jnp.float32),
            pltpu.VMEM((half, lanes), jnp.float32),
            pltpu.VMEM((half, lanes), jnp.float32),
            pltpu.VMEM((PACK, lanes), jnp.float32),
            pltpu.VMEM((half + PACK, lanes), jnp.float32),
            pltpu.VMEM((PACK, lanes), jnp.float32),
            pltpu.VMEM((2 * half, lanes), jnp.float32),
            pltpu.VMEM((PACK, lanes), jnp.bfloat16),
            pltpu.VMEM((2 * PACK, lanes), jnp.bfloat16),
            pltpu.VMEM((3, half, lanes), jnp.float32),
            pltpu.VMEM((half, lanes), jnp.bfloat16),
            dma((2,)),
            dma((3,)),
            dma,
            dma((3,)),
            dma((2, 3)),
            dma((2, 4, 3)),
            dma((2, 4, 3)),
            dma((2, 3)),
            dma((2, 3)),
            dma((3,)),
            dma((2, CHUNKS)),
            dma((CHUNKS,)),
            dma((CHUNKS,)),
            dma((CHUNKS,)),
            dma((CHUNKS,)),
            dma((3, CHUNKS)),
            dma((CHUNKS,)),
            dma((CHUNKS,)),
        ],
        compiler_params=pltpu.CompilerParams(
            collective_id=0, has_side_effects=True, vmem_limit_bytes=60 * 1024 * 1024
        ),
        name="move_and_update",
    )(old_offsets, new_offsets, old_master, old_first, old_second, grad_parts)
    master, first, second, weights = pl.pallas_call(
        finish,
        out_shape=shapes,
        in_specs=[hbm] * 6,
        out_specs=(hbm,) * 4,
        scratch_shapes=[pltpu.SMEM(new_offsets.shape, jnp.int32)]
        + [pltpu.VMEM(shape.shape, shape.dtype) for shape in shapes + (short,)]
        + [pltpu.VMEM((new_cap, lanes), jnp.float32), dma((6,)), dma((5,))],
        compiler_params=pltpu.CompilerParams(vmem_limit_bytes=60 * 1024 * 1024),
        name="finish",
    )(new_offsets, *results)
    return (master[None, None], first[None, None], second[None, None], weights)


def solution(mesh):
    in_specs = (
        P("shard", None),
        P("shard", None),
        P("shard", None),
        P("rep", "shard", None),
        P(),
        P(),
    )
    out_specs = (
        P("shard", "rep", None, None),
        P("shard", "rep", None, None),
        P("shard", "rep", None, None),
        P("shard", None),
    )
    return jax.shard_map(local, mesh=mesh, in_specs=in_specs, out_specs=out_specs, check_vma=False)
```

```python
import functools

import jax
import jax.numpy as jnp
from jax import lax
from jax.experimental import pallas as pl
from jax.experimental.pallas import tpu as pltpu
from jax.sharding import PartitionSpec as P

STEP = 10
MESH = pl.DeviceIdType.MESH
JITTER = 512
EDGE = 2 * JITTER
PACK = 1024
WINDOW = 3584
CHUNKS = 8
SUB = 64
EARLY = 4
PROMPT = 5


def within(start):
    return jnp.clip(start, 0, 2 * EDGE)


def kernel(
    old_off_in,
    new_off_in,
    old_m,
    old_f,
    old_s,
    grads,
    out_m,
    out_f,
    out_s,
    out_w,
    out_q,
    old_off,
    new_off,
    main,
    alt,
    relay,
    stage_m,
    stage_f,
    stage_s,
    edge,
    mine,
    theirs,
    near_rows,
    far_rows,
    pack,
    packed,
    short_pack,
    short_packed,
    res,
    wts,
    off_sem,
    in_sem,
    mine_sem,
    stage_sem,
    die_sem,
    head_sem,
    tail_sem,
    head_relay_sem,
    tail_relay_sem,
    pack_sem,
    pass_sem,
    grad_send,
    grad_recv,
    wts_send,
    wts_recv,
    res_sem,
    own_sem,
    short_sem,
):
    olds = (old_m, old_f, old_s)
    outs = (out_m, out_f, out_s)
    stages = (stage_m, stage_f, stage_s)
    old_cap = old_m.shape[0]
    half = mine.shape[0]
    size = half // CHUNKS
    r = lax.axis_index("rep")
    s = lax.axis_index("shard")
    owners = lax.axis_size("shard") // 2
    o = s // 2
    core = s % 2
    even = core == 0
    odd = core == 1
    other = (1 - r, s)

    x = o % 4

    up_rep = r
    down_rep = r
    sends_head = even & (up_rep == 0) & (o < owners - 1)
    gets_head = even & (r == 0) & (o > 0)
    sends_tail = even & (o > 0)
    gets_tail = odd & (o < owners - 1)
    count = 2 * owners
    head_to = (up_rep, lax.rem(s + 2, count))
    head_from = (down_rep, lax.rem(s + count - 2, count))
    tail_to = (down_rep, lax.rem(s + count - 1, count))
    tail_from = (up_rep, lax.rem(s + 1, count))
    die_to = (r, s + 1 - 2 * core)

    z_lo = (o // 4) % 4
    turn_up = jnp.where(z_lo == 3, 32, 0)
    turn_down = jnp.where(z_lo == 0, 32, 0)
    head_wraps = sends_head & (x == 3)
    head_unwraps = gets_head & (x == 0)
    tail_wraps = sends_tail & (x == 0)
    tail_unwraps = gets_tail & (x == 3)
    head_source = s - 1 + 2 * (3 - x) - turn_up
    head_rep = r
    relays_head = odd & (head_rep == 0) & (head_source >= 0)
    tail_source = s - 2 * x + turn_down
    tail_rep = r
    relays_tail = even & (tail_source < count) & ((x > 0) | (z_lo == 0))
    head_relays = s + jnp.where(z_lo == 0, 24, -8) + 1
    tail_relays = s + jnp.where(z_lo == 3, -24, 8) - 7

    barrier = pltpu.get_barrier_semaphore()
    pl.semaphore_signal(barrier, inc=1, device_id=other, device_id_type=MESH)

    offsets = (
        pltpu.make_async_copy(old_off_in, old_off, off_sem.at[0]),
        pltpu.make_async_copy(new_off_in, new_off, off_sem.at[1]),
    )
    for copy in offsets:
        copy.start()
    my_grads = pltpu.make_async_copy(grads.at[0, pl.ds(r * half, half)], mine, mine_sem)

    def load_own(k, rep):
        if rep == 0:
            return pltpu.make_async_copy(
                olds[k].at[pl.ds(0, WINDOW - EDGE)], main.at[k, pl.ds(EDGE, WINDOW - EDGE)], in_sem.at[k]
            )
        return pltpu.make_async_copy(olds[k].at[pl.ds(JITTER, WINDOW)], main.at[k], in_sem.at[k])

    def load_stage(k):
        rows = stage_m.shape[0]
        return pltpu.make_async_copy(olds[k].at[pl.ds(old_cap - rows, rows)], stages[k], stage_sem.at[k])

    def die_copy(k, rep):
        first = 1024 if rep == 0 else 2560
        rows = min(WINDOW, old_cap - first)
        return pltpu.make_async_remote_copy(
            olds[k].at[pl.ds(first, rows)],
            main.at[k, pl.ds(0, rows)],
            die_sem.at[0, k],
            die_sem.at[1, k],
            device_id=die_to,
            device_id_type=MESH,
        )

    def send(src, dst, sems, to):
        return pltpu.make_async_remote_copy(src, dst, sems[0], sems[1], device_id=to, device_id_type=MESH)

    quarter = EDGE // 4

    def head_copy(k, part=None):
        rows = pl.ds(0, EDGE) if part is None else pl.ds(part * quarter, quarter)
        at = 0 if part is None else part
        sems = (head_sem.at[0, at, k], head_sem.at[1, at, k])
        return send(edge.at[k, rows], main.at[k, rows], sems, head_to)

    def head_relay_in(k, part):
        rows = pl.ds(part * quarter, quarter)
        sems = (head_sem.at[0, part, k], head_relay_sem.at[0, k])
        to = (r, lax.rem(s - 2 * (3 - part) + 1 + turn_up + count, count))
        return send(edge.at[k, rows], relay.at[0, k], sems, to)

    def head_relay_out(k, part):
        rows = pl.ds(part * quarter, quarter)
        sems = (head_relay_sem.at[1, k], head_sem.at[1, part, k])
        return send(relay.at[0, k], main.at[k, rows], sems, (head_rep, lax.rem(head_source + 2, count)))

    def tail_place(rep):
        return (3072, JITTER) if rep == 0 else (1536, EDGE)

    def tail_copy(k, rep, part=None):
        first, rows = tail_place(rep)
        begin = 0
        if part is not None:
            rows //= 4
            begin = part * rows
        at = 0 if part is None else part
        sems = (tail_sem.at[0, at, k], tail_sem.at[1, at, k])
        return send(olds[k].at[pl.ds(begin, rows)], alt.at[k, pl.ds(first + begin, rows)], sems, tail_to)

    def tail_relay_in(k, rep, part):
        rows = tail_place(rep)[1] // 4
        sems = (tail_sem.at[0, part, k], tail_relay_sem.at[0, k])
        to = (r, lax.rem(s + 2 * part - turn_down + count, count))
        return send(olds[k].at[pl.ds(part * rows, rows)], relay.at[1, k, pl.ds(0, rows)], sems, to)

    def tail_relay_out(k, rep, part):
        first, rows = tail_place(rep)
        rows //= 4
        sems = (tail_relay_sem.at[1, k], tail_sem.at[1, part, k])
        to = (tail_rep, lax.rem(tail_source + count - 1, count))
        return send(relay.at[1, k, pl.ds(0, rows)], alt.at[k, pl.ds(first + part * rows, rows)], sems, to)

    piece = PACK // CHUNKS

    def grad_copy(c, rep):
        if rep == 1:
            rows = pl.ds(pl.multiple_of(c * size, 16), size)
            src, dst = grads.at[0, rows], theirs.at[rows]
        else:
            src = pack.at[pl.ds(pl.multiple_of(c * piece, 16), piece)]
            dst = packed.at[pl.ds(pl.multiple_of(core * PACK + c * piece, 16), piece)]
        return send(src, dst, (grad_send.at[c], grad_recv.at[c]), other)

    def pass_copy(c):
        rows = packed.at[pl.ds(pl.multiple_of(core * PACK + c * piece, 16), piece)]
        return send(rows, rows, (pass_sem.at[0, c], pass_sem.at[1, c]), die_to)

    def grad_rows(first, rows):
        return grads.at[0, pl.ds(half + first, rows)]

    def master_rows(first, rows):
        return res.at[0, pl.ds(first, rows)]

    def near_copy(at, source):
        if at == 0:
            return pltpu.make_async_copy(source(0, PACK), near_rows, pack_sem.at[0])
        rows = half - PACK
        return send(source(PACK, rows), near_rows.at[pl.ds(0, rows)], (pack_sem.at[1], pack_sem.at[2]), die_to)

    def far_copy(at, source):
        if at == 1:
            return pltpu.make_async_copy(source(0, half), far_rows.at[pl.ds(half - PACK, half)], pack_sem.at[0])
        return send(source(0, PACK), far_rows.at[pl.ds(half, PACK)], (pack_sem.at[1], pack_sem.at[2]), die_to)

    def pack_rows(at):
        row = core * PACK + at + lax.broadcasted_iota(jnp.int32, (SUB, 128), 0)
        far = far_rows[pl.ds(half - first_rows + at, SUB), :]
        return jnp.where(row < first_rows, near_rows[pl.ds(pl.multiple_of(at, SUB), SUB), :], far)

    def short_copy(c):
        src = short_pack.at[pl.ds(pl.multiple_of(c * piece, 16), piece)]
        dst = short_packed.at[pl.ds(pl.multiple_of(core * PACK + c * piece, 16), piece)]
        return send(src, dst, (wts_send.at[c], wts_recv.at[c]), other)

    def short_place(c, at):
        return pl.ds(pl.multiple_of(at * PACK + c * piece, 16), piece)

    def short_pass(c, at):
        rows = short_place(c, at)
        return send(short_packed.at[rows], out_q.at[rows], (pass_sem.at[0, c], pass_sem.at[1, c]), die_to)

    def short_keep(c):
        rows = short_place(c, core)
        return pltpu.make_async_copy(short_packed.at[rows], out_q.at[rows], short_sem.at[c])

    def start_grads(first, last):
        for rep in (0, 1):

            @pl.when(r == rep)
            def _():
                @pl.loop(first, last)
                def _(c):
                    grad_copy(c, rep).start()

    def wts_copy(c):
        first = pl.multiple_of(c * size, 16)
        return pltpu.make_async_remote_copy(
            wts.at[pl.ds(first, size)],
            out_w.at[pl.ds(pl.multiple_of(r * half + first, 16), size)],
            wts_send.at[c],
            wts_recv.at[c],
            device_id=other,
            device_id_type=MESH,
        )

    def wts_arrival(c):
        first = pl.multiple_of(c * size, 16)
        return pltpu.make_async_remote_copy(
            wts.at[pl.ds(first, size)],
            out_w.at[pl.ds(pl.multiple_of((1 - r) * half + first, 16), size)],
            wts_send.at[c],
            wts_recv.at[c],
            device_id=other,
            device_id_type=MESH,
        )

    def own_copy(c):
        first = pl.multiple_of(c * size, 16)
        return pltpu.make_async_copy(
            wts.at[pl.ds(first, size)],
            out_w.at[pl.ds(pl.multiple_of(r * half + first, 16), size)],
            own_sem.at[c],
        )

    def res_copy(k, c):
        first = pl.multiple_of(c * size, 16)
        return pltpu.make_async_copy(
            res.at[k, pl.ds(first, size)], outs[k].at[pl.ds(first, size)], res_sem.at[k, c]
        )

    @pl.when(sends_head)
    def _():
        for k in range(3):
            load_stage(k).start()

    @pl.when((r == 0) & even)
    def _():
        near_copy(0, grad_rows).start()

    @pl.when((r == 0) & odd)
    def _():
        far_copy(1, grad_rows).start()


    pl.semaphore_signal(barrier, inc=1, device_id=die_to, device_id_type=MESH)

    @pl.when(gets_head & (x > 0))
    def _():
        pl.semaphore_signal(barrier, inc=1, device_id=head_from, device_id_type=MESH)

    @pl.when(head_unwraps)
    def _():
        for part in range(4):
            at = lax.rem(head_relays + 2 * part + count, count)
            pl.semaphore_signal(barrier, inc=1, device_id=(down_rep, at), device_id_type=MESH)

    @pl.when(gets_tail & (x < 3))
    def _():
        pl.semaphore_signal(barrier, inc=1, device_id=tail_from, device_id_type=MESH)

    @pl.when(tail_unwraps)
    def _():
        for part in range(4):
            at = lax.rem(tail_relays + 2 * part + count, count)
            pl.semaphore_signal(barrier, inc=1, device_id=(up_rep, at), device_id_type=MESH)

    @pl.when(relays_head)
    def _():
        pl.semaphore_signal(barrier, inc=1, device_id=(r, lax.rem(head_source + count, count)), device_id_type=MESH)

    @pl.when(relays_tail)
    def _():
        pl.semaphore_signal(barrier, inc=1, device_id=(r, lax.rem(tail_source, count)), device_id_type=MESH)

    targets = 2
    for cond, more in (
        (sends_head, 1),
        (head_wraps, 3),
        (sends_tail, 1),
        (tail_wraps, 3),
        (relays_head, 1),
        (relays_tail, 1),
    ):
        targets = targets + more * cond.astype(jnp.int32)
    pl.semaphore_wait(barrier, targets)

    early = EARLY

    @pl.when(r == 1)
    def _():
        @pl.loop(0, early)
        def _(c):
            grad_copy(c, 1).start()

    @pl.when((r == 0) & even)
    def _():
        near_copy(1, grad_rows).start()

    @pl.when((r == 0) & odd)
    def _():
        far_copy(0, grad_rows).start()

    for rep in (0, 1):

        @pl.when(tail_wraps & (down_rep == rep))
        def _():
            for part in (1, 2, 3):
                for k in range(3):
                    tail_relay_in(k, rep, part).start()

            @pl.when(z_lo == 0)
            def _():
                for k in range(3):
                    tail_relay_in(k, rep, 0).start()

            @pl.when(z_lo > 0)
            def _():
                for k in range(3):
                    tail_copy(k, rep, 0).start()

    for copy in offsets:
        copy.wait()

    pair = s - core
    first_rows = jnp.clip(new_off[pair + 1] - new_off[pair] - half, 0, half)

    @pl.when((r == 0) & even)
    def _():
        near_copy(0, grad_rows).wait()
        far_copy(0, grad_rows).wait_recv()

    @pl.when((r == 0) & odd)
    def _():
        far_copy(1, grad_rows).wait()
        near_copy(1, grad_rows).wait_recv()

    @pl.when(r == 0)
    def _():
        @pl.loop(0, PACK // SUB)
        def _(j):
            pack[pl.ds(pl.multiple_of(j * SUB, SUB), SUB), :] = pack_rows(j * SUB)

    prompt = jnp.where(odd & (z_lo == 3), PROMPT, CHUNKS)

    @pl.when(r == 0)
    def _():
        @pl.loop(0, prompt)
        def _(c):
            grad_copy(c, 0).start()

    @pl.when(sends_head)
    def _():
        begin = within(old_off[o + 1] - old_off[o] - (old_cap - stage_m.shape[0]) - EDGE)
        for k in range(3):
            load_stage(k).wait()

            @pl.loop(0, EDGE // SUB)
            def _(j):
                edge[k, pl.ds(pl.multiple_of(j * SUB, SUB), SUB), :] = stages[k][pl.ds(begin + j * SUB, SUB), :]

            @pl.when(x < 3)
            def _():
                head_copy(k).start()

            @pl.when(x == 3)
            def _():
                for part in range(4):
                    head_relay_in(k, part).start()

    for rep in (0, 1):

        @pl.when(sends_tail & (down_rep == rep) & (x > 0))
        def _():
            for k in range(3):
                tail_copy(k, rep).start()

    for rep in (0, 1):

        @pl.when(even & (r == rep))
        def _():
            for k in range(3):
                die_copy(k, rep).start()

    for rep in (0, 1):

        @pl.when(even & (r == rep))
        def _():
            for k in range(3):
                load_own(k, rep).start()

    my_grads.start()

    for part in range(4):

        @pl.when(relays_head & (x == part))
        def _():
            for k in range(3):
                head_relay_in(k, part).wait_recv()
                head_relay_out(k, part).start()

    for rep in (0, 1):
        for part in range(4):

            @pl.when(relays_tail & (tail_rep == rep) & (x == part))
            def _():
                for k in range(3):
                    tail_relay_in(k, rep, part).wait_recv()
                    tail_relay_out(k, rep, part).start()

    @pl.when(r == 0)
    def _():
        @pl.loop(prompt, CHUNKS)
        def _(c):
            grad_copy(c, 0).start()

    passes = jnp.where(even, CHUNKS, (half - PACK) // piece)
    arrivals = jnp.where(odd, CHUNKS, (half - PACK) // piece)

    @pl.when(r == 1)
    def _():
        @pl.loop(0, CHUNKS)
        def _(c):
            grad_copy(c, 0).wait_recv()

            @pl.when(c == 0)
            def _():
                @pl.loop(early, CHUNKS)
                def _(d):
                    grad_copy(d, 1).start()

            @pl.when(c < passes)
            def _():
                pass_copy(c).start()

    for rep in (0, 1):

        @pl.when(even & (r == rep))
        def _():
            for k in range(3):
                load_own(k, rep).wait()

        @pl.when(odd & (r == rep))
        def _():
            for k in range(3):
                die_copy(k, rep).wait_recv()

    @pl.when(gets_head & (x > 0))
    def _():
        for k in range(3):
            head_copy(k).wait_recv()

    @pl.when(head_unwraps)
    def _():
        for part in range(4):
            for k in range(3):
                head_copy(k, part).wait_recv()

    for rep in (0, 1):

        @pl.when(gets_tail & (r == rep) & (x < 3))
        def _():
            for k in range(3):
                tail_copy(k, rep).wait_recv()

        @pl.when(tail_unwraps & (r == rep))
        def _():
            for part in range(4):
                for k in range(3):
                    tail_copy(k, rep, part).wait_recv()

    my_grads.wait()

    start = within(new_off[s] - old_off[o] + EDGE - 2 * EDGE * core)
    edge_start = within(new_off[s] - old_off[o + 1] + 2 * half)
    split = jnp.where(even, new_off[s + 1], old_off[o + 1])
    flat = new_off[s] + r * half
    stop = new_off[s + 1]

    def update(c, their_rows):
        @pl.loop(0, size // SUB)
        def _(j):
            at = c * size + j * SUB
            rows = pl.ds(pl.multiple_of(at, SUB), SUB)
            row = flat + at + lax.broadcasted_iota(jnp.int32, (SUB, 128), 0)
            near = row < split
            keep = row < stop
            master, first, second = [
                jnp.where(near, main[k, pl.ds(start + at, SUB), :], alt[k, pl.ds(edge_start + at, SUB), :])
                for k in range(3)
            ]
            total = mine[rows, :] + their_rows(at)
            first_n = 0.9 * first + 0.1 * total
            second_n = 0.95 * second + 0.05 * total * total
            first_hat = first_n / (1.0 - 0.9**STEP)
            second_hat = second_n / (1.0 - 0.95**STEP)
            master_n = master - 0.02 * (first_hat / (jnp.sqrt(second_hat) + 1e-08) + 0.1 * master)
            master_n = jnp.where(keep, master_n, 0.0)
            res[0, rows, :] = master_n
            res[1, rows, :] = jnp.where(keep, first_n, 0.0)
            res[2, rows, :] = jnp.where(keep, second_n, 0.0)
            wts[rows, :] = master_n.astype(jnp.bfloat16)

        own_copy(c).start()
        for k in range(3):
            res_copy(k, c).start()

    @pl.when(r == 0)
    def _():
        @pl.loop(0, CHUNKS)
        def _(c):
            grad_copy(c, 1).wait_recv()
            update(c, lambda at: theirs[pl.ds(pl.multiple_of(at, SUB), SUB), :])
            wts_copy(c).start()

        @pl.loop(0, CHUNKS)
        def _(c):
            short_copy(c).wait_recv()
            short_keep(c).start()

            @pl.when(c < passes)
            def _():
                short_pass(c, core).start()


    @pl.when(r == 1)
    def _():
        @pl.loop(0, arrivals)
        def _(c):
            there = packed.at[pl.ds(pl.multiple_of((1 - core) * PACK + c * piece, 16), piece)]
            send(there, there, (pass_sem.at[0, c], pass_sem.at[1, c]), die_to).wait_recv()

        @pl.loop(0, CHUNKS)
        def _(c):
            update(c, lambda at: packed[pl.ds(core * first_rows + at, SUB), :])

            @pl.when((c == (PACK - 1) // size) & even)
            def _():
                near_copy(0, master_rows).start()

            @pl.when((c == (PACK - 1) // size) & odd)
            def _():
                far_copy(0, master_rows).start()

        @pl.when(even)
        def _():
            near_copy(1, master_rows).start()
            near_copy(0, master_rows).wait()
            far_copy(0, master_rows).wait_recv()

        @pl.when(odd)
        def _():
            far_copy(1, master_rows).start()
            far_copy(1, master_rows).wait()
            near_copy(1, master_rows).wait_recv()

        @pl.loop(0, CHUNKS)
        def _(c):
            @pl.loop(0, piece // SUB)
            def _(j):
                at = c * piece + j * SUB
                short_pack[pl.ds(pl.multiple_of(at, SUB), SUB), :] = pack_rows(at).astype(jnp.bfloat16)

            short_copy(c).start()


    for rep in (0, 1):

        @pl.when(even & (r == rep))
        def _():
            for k in range(3):
                die_copy(k, rep).wait_send()

    @pl.when(sends_head & (x < 3))
    def _():
        for k in range(3):
            head_copy(k).wait_send()

    @pl.when(head_wraps)
    def _():
        for part in range(4):
            for k in range(3):
                head_copy(k, part).wait_send()

    @pl.when(relays_head)
    def _():
        for k in range(3):
            head_relay_out(k, 0).wait_send()

    for rep in (0, 1):

        @pl.when(sends_tail & (down_rep == rep) & (x > 0))
        def _():
            for k in range(3):
                tail_copy(k, rep).wait_send()

        @pl.when(tail_wraps & (down_rep == rep))
        def _():
            for part in range(4):
                for k in range(3):
                    tail_copy(k, rep, part).wait_send()

        @pl.when(relays_tail & (tail_rep == rep))
        def _():
            for k in range(3):
                tail_relay_out(k, rep, 0).wait_send()

    @pl.when(even)
    def _():
        near_copy(1, grad_rows).wait_send()

    @pl.when(odd)
    def _():
        far_copy(0, grad_rows).wait_send()

    for rep in (0, 1):

        @pl.when(r == rep)
        def _():
            @pl.loop(0, CHUNKS)
            def _(c):
                grad_copy(c, rep).wait_send()
                own_copy(c).wait()
                for k in range(3):
                    res_copy(k, c).wait()

    @pl.when(r == 0)
    def _():
        @pl.loop(0, CHUNKS)
        def _(c):
            wts_copy(c).wait_send()
            short_keep(c).wait()

        @pl.loop(0, passes)
        def _(c):
            short_pass(c, core).wait_send()

        @pl.loop(0, arrivals)
        def _(c):
            short_pass(c, 1 - core).wait_recv()

    @pl.when(r == 1)
    def _():
        @pl.loop(0, passes)
        def _(c):
            pass_copy(c).wait_send()

        @pl.loop(0, CHUNKS)
        def _(c):
            short_copy(c).wait_send()
            wts_arrival(c).wait_recv()


def finish(
    off_in, in_m, in_f, in_s, in_w, in_q, out_m, out_f, out_s, out_w, off, vm, vf, vs, vw, vq, wide, in_sem, out_sem
):
    r = lax.axis_index("rep")
    s = lax.axis_index("shard")
    core = s % 2
    half = vm.shape[0]
    top, low = pl.ds(0, half), pl.ds(half, half)
    load_off = pltpu.make_async_copy(off_in, off, in_sem.at[0])
    load_q = pltpu.make_async_copy(in_q, vq, in_sem.at[1])
    pairs = [(in_m, vm, out_m), (in_f, vf, out_f), (in_s, vs, out_s), (in_w.at[top], vw.at[top], out_w.at[top])]
    loads = [pltpu.make_async_copy(src, hold, in_sem.at[2 + i]) for i, (src, hold, _) in enumerate(pairs)]
    stores = [pltpu.make_async_copy(hold, dst, out_sem.at[i]) for i, (_, hold, dst) in enumerate(pairs)]
    load_low = pltpu.make_async_copy(in_w.at[low], vw.at[low], in_sem.at[1])
    store_low = pltpu.make_async_copy(vw.at[low], out_w.at[low], out_sem.at[4])
    load_off.start()

    @pl.when(r == 0)
    def _():
        load_q.start()

    @pl.when(r == 1)
    def _():
        load_low.start()

    for load in loads:
        load.start()
    for load, store in zip(loads, stores):
        load.wait()
        store.start()
    load_off.wait()

    @pl.when(r == 0)
    def _():
        pair = s - core
        first_rows = jnp.clip(off[pair + 1] - off[pair] - half, 0, half)
        live = off[s + 1] - off[s] - half
        load_q.wait()

        @pl.loop(0, vq.shape[0] // SUB)
        def _(j):
            rows = pl.ds(pl.multiple_of(j * SUB, SUB), SUB)
            wide[rows, :] = vq[rows, :].astype(jnp.float32)

        @pl.loop(0, half // SUB)
        def _(j):
            row = j * SUB + lax.broadcasted_iota(jnp.int32, (SUB, 128), 0)
            mine = jnp.where(row < live, wide[pl.ds(core * first_rows + j * SUB, SUB), :], 0.0)
            vw[pl.ds(pl.multiple_of(half + j * SUB, SUB), SUB), :] = mine.astype(jnp.bfloat16)

    @pl.when(r == 1)
    def _():
        load_low.wait()

    store_low.start()
    for store in stores:
        store.wait()
    store_low.wait()


def local(old_master, old_first, old_second, grad_parts, old_offsets, new_offsets):
    new_cap, lanes = grad_parts.shape[1:]
    half = new_cap // 2
    hbm = pl.BlockSpec(memory_space=pltpu.HBM)
    free = pl.BlockSpec(memory_space=pl.ANY)
    state = jax.ShapeDtypeStruct((half, lanes), jnp.float32)
    dma = pltpu.SemaphoreType.DMA
    shapes = (state, state, state, jax.ShapeDtypeStruct((new_cap, lanes), jnp.bfloat16))
    short = jax.ShapeDtypeStruct((2 * PACK, lanes), jnp.bfloat16)
    results = pl.pallas_call(
        kernel,
        out_shape=shapes + (short,),
        in_specs=[hbm] * 6,
        out_specs=(free,) * 5,
        scratch_shapes=[
            pltpu.SMEM(old_offsets.shape, jnp.int32),
            pltpu.SMEM(new_offsets.shape, jnp.int32),
            pltpu.VMEM((3, WINDOW, lanes), jnp.float32),
            pltpu.VMEM((3, WINDOW, lanes), jnp.float32),
            pltpu.VMEM((2, 3, EDGE // 4, lanes), jnp.float32),
            pltpu.VMEM((3 * EDGE, lanes), jnp.float32),
            pltpu.VMEM((3 * EDGE, lanes), jnp.float32),
            pltpu.VMEM((3 * EDGE, lanes), jnp.float32),
            pltpu.VMEM((3, EDGE, lanes), jnp.float32),
            pltpu.VMEM((half, lanes), jnp.float32),
            pltpu.VMEM((half, lanes), jnp.float32),
            pltpu.VMEM((PACK, lanes), jnp.float32),
            pltpu.VMEM((half + PACK, lanes), jnp.float32),
            pltpu.VMEM((PACK, lanes), jnp.float32),
            pltpu.VMEM((2 * half, lanes), jnp.float32),
            pltpu.VMEM((PACK, lanes), jnp.bfloat16),
            pltpu.VMEM((2 * PACK, lanes), jnp.bfloat16),
            pltpu.VMEM((3, half, lanes), jnp.float32),
            pltpu.VMEM((half, lanes), jnp.bfloat16),
            dma((2,)),
            dma((3,)),
            dma,
            dma((3,)),
            dma((2, 3)),
            dma((2, 4, 3)),
            dma((2, 4, 3)),
            dma((2, 3)),
            dma((2, 3)),
            dma((3,)),
            dma((2, CHUNKS)),
            dma((CHUNKS,)),
            dma((CHUNKS,)),
            dma((CHUNKS,)),
            dma((CHUNKS,)),
            dma((3, CHUNKS)),
            dma((CHUNKS,)),
            dma((CHUNKS,)),
        ],
        compiler_params=pltpu.CompilerParams(
            collective_id=0, has_side_effects=True, vmem_limit_bytes=60 * 1024 * 1024
        ),
        name="move_and_update",
    )(old_offsets, new_offsets, old_master, old_first, old_second, grad_parts)
    master, first, second, weights = pl.pallas_call(
        finish,
        out_shape=shapes,
        in_specs=[hbm] * 6,
        out_specs=(hbm,) * 4,
        scratch_shapes=[pltpu.SMEM(new_offsets.shape, jnp.int32)]
        + [pltpu.VMEM(shape.shape, shape.dtype) for shape in shapes + (short,)]
        + [pltpu.VMEM((new_cap, lanes), jnp.float32), dma((6,)), dma((5,))],
        compiler_params=pltpu.CompilerParams(vmem_limit_bytes=60 * 1024 * 1024),
        name="finish",
    )(new_offsets, *results)
    return (master[None, None], first[None, None], second[None, None], weights)


def solution(mesh):
    in_specs = (
        P("shard", None),
        P("shard", None),
        P("shard", None),
        P("rep", "shard", None),
        P(),
        P(),
    )
    out_specs = (
        P("shard", "rep", None, None),
        P("shard", "rep", None, None),
        P("shard", "rep", None, None),
        P("shard", None),
    )
    return jax.shard_map(local, mesh=mesh, in_specs=in_specs, out_specs=out_specs, check_vma=False)
```

```python
import functools

import jax
import jax.numpy as jnp
from jax import lax
from jax.experimental import pallas as pl
from jax.experimental.pallas import tpu as pltpu
from jax.sharding import PartitionSpec as P

STEP = 10
MESH = pl.DeviceIdType.MESH
JITTER = 512
EDGE = 2 * JITTER
PACK = 1024
WINDOW = 3584
CHUNKS = 8
SUB = 64
EARLY = 5
PROMPT = 5


def within(start):
    return jnp.clip(start, 0, 2 * EDGE)


def kernel(
    old_off_in,
    new_off_in,
    old_m,
    old_f,
    old_s,
    grads,
    out_m,
    out_f,
    out_s,
    out_w,
    out_q,
    old_off,
    new_off,
    main,
    alt,
    relay,
    stage_m,
    stage_f,
    stage_s,
    edge,
    mine,
    theirs,
    near_rows,
    far_rows,
    pack,
    packed,
    short_pack,
    short_packed,
    res,
    wts,
    off_sem,
    in_sem,
    mine_sem,
    stage_sem,
    die_sem,
    head_sem,
    tail_sem,
    head_relay_sem,
    tail_relay_sem,
    pack_sem,
    pass_sem,
    grad_send,
    grad_recv,
    wts_send,
    wts_recv,
    res_sem,
    own_sem,
    short_sem,
):
    olds = (old_m, old_f, old_s)
    outs = (out_m, out_f, out_s)
    stages = (stage_m, stage_f, stage_s)
    old_cap = old_m.shape[0]
    half = mine.shape[0]
    size = half // CHUNKS
    r = lax.axis_index("rep")
    s = lax.axis_index("shard")
    owners = lax.axis_size("shard") // 2
    o = s // 2
    core = s % 2
    even = core == 0
    odd = core == 1
    other = (1 - r, s)

    x = o % 4

    up_rep = r
    down_rep = r
    sends_head = even & (up_rep == 0) & (o < owners - 1)
    gets_head = even & (r == 0) & (o > 0)
    sends_tail = even & (o > 0)
    gets_tail = odd & (o < owners - 1)
    count = 2 * owners
    head_to = (up_rep, lax.rem(s + 2, count))
    head_from = (down_rep, lax.rem(s + count - 2, count))
    tail_to = (down_rep, lax.rem(s + count - 1, count))
    tail_from = (up_rep, lax.rem(s + 1, count))
    die_to = (r, s + 1 - 2 * core)

    z_lo = (o // 4) % 4
    turn_up = jnp.where(z_lo == 3, 32, 0)
    turn_down = jnp.where(z_lo == 0, 32, 0)
    head_wraps = sends_head & (x == 3)
    head_unwraps = gets_head & (x == 0)
    tail_wraps = sends_tail & (x == 0)
    tail_unwraps = gets_tail & (x == 3)
    head_source = s - 1 + 2 * (3 - x) - turn_up
    head_rep = r
    relays_head = odd & (head_rep == 0) & (head_source >= 0)
    tail_source = s - 2 * x + turn_down
    tail_rep = r
    relays_tail = even & (tail_source < count) & ((x > 0) | (z_lo == 0))
    head_relays = s + jnp.where(z_lo == 0, 24, -8) + 1
    tail_relays = s + jnp.where(z_lo == 3, -24, 8) - 7

    offsets = (
        pltpu.make_async_copy(old_off_in, old_off, off_sem.at[0]),
        pltpu.make_async_copy(new_off_in, new_off, off_sem.at[1]),
    )
    for copy in offsets:
        copy.start()
    my_grads = pltpu.make_async_copy(grads.at[0, pl.ds(r * half, half)], mine, mine_sem)

    def load_own(k, rep):
        if rep == 0:
            return pltpu.make_async_copy(
                olds[k].at[pl.ds(0, WINDOW - EDGE)], main.at[k, pl.ds(EDGE, WINDOW - EDGE)], in_sem.at[k]
            )
        return pltpu.make_async_copy(olds[k].at[pl.ds(JITTER, WINDOW)], main.at[k], in_sem.at[k])

    def load_stage(k):
        rows = stage_m.shape[0]
        return pltpu.make_async_copy(olds[k].at[pl.ds(old_cap - rows, rows)], stages[k], stage_sem.at[k])

    def die_copy(k, rep):
        first = 1024 if rep == 0 else 2560
        rows = min(WINDOW, old_cap - first)
        return pltpu.make_async_remote_copy(
            olds[k].at[pl.ds(first, rows)],
            main.at[k, pl.ds(0, rows)],
            die_sem.at[0, k],
            die_sem.at[1, k],
            device_id=die_to,
            device_id_type=MESH,
        )

    def send(src, dst, sems, to):
        return pltpu.make_async_remote_copy(src, dst, sems[0], sems[1], device_id=to, device_id_type=MESH)

    quarter = EDGE // 4

    def head_copy(k, part=None):
        rows = pl.ds(0, EDGE) if part is None else pl.ds(part * quarter, quarter)
        at = 0 if part is None else part
        sems = (head_sem.at[0, at, k], head_sem.at[1, at, k])
        return send(edge.at[k, rows], main.at[k, rows], sems, head_to)

    def head_relay_in(k, part):
        rows = pl.ds(part * quarter, quarter)
        sems = (head_sem.at[0, part, k], head_relay_sem.at[0, k])
        to = (r, lax.rem(s - 2 * (3 - part) + 1 + turn_up + count, count))
        return send(edge.at[k, rows], relay.at[0, k], sems, to)

    def head_relay_out(k, part):
        rows = pl.ds(part * quarter, quarter)
        sems = (head_relay_sem.at[1, k], head_sem.at[1, part, k])
        return send(relay.at[0, k], main.at[k, rows], sems, (head_rep, lax.rem(head_source + 2, count)))

    def tail_place(rep):
        return (3072, JITTER) if rep == 0 else (1536, EDGE)

    def tail_copy(k, rep, part=None):
        first, rows = tail_place(rep)
        begin = 0
        if part is not None:
            rows //= 4
            begin = part * rows
        at = 0 if part is None else part
        sems = (tail_sem.at[0, at, k], tail_sem.at[1, at, k])
        return send(olds[k].at[pl.ds(begin, rows)], alt.at[k, pl.ds(first + begin, rows)], sems, tail_to)

    def tail_relay_in(k, rep, part):
        rows = tail_place(rep)[1] // 4
        sems = (tail_sem.at[0, part, k], tail_relay_sem.at[0, k])
        to = (r, lax.rem(s + 2 * part - turn_down + count, count))
        return send(olds[k].at[pl.ds(part * rows, rows)], relay.at[1, k, pl.ds(0, rows)], sems, to)

    def tail_relay_out(k, rep, part):
        first, rows = tail_place(rep)
        rows //= 4
        sems = (tail_relay_sem.at[1, k], tail_sem.at[1, part, k])
        to = (tail_rep, lax.rem(tail_source + count - 1, count))
        return send(relay.at[1, k, pl.ds(0, rows)], alt.at[k, pl.ds(first + part * rows, rows)], sems, to)

    piece = PACK // CHUNKS

    def grad_copy(c, rep):
        if rep == 1:
            rows = pl.ds(pl.multiple_of(c * size, 16), size)
            src, dst = grads.at[0, rows], theirs.at[rows]
        else:
            src = pack.at[pl.ds(pl.multiple_of(c * piece, 16), piece)]
            dst = packed.at[pl.ds(pl.multiple_of(core * PACK + c * piece, 16), piece)]
        return send(src, dst, (grad_send.at[c], grad_recv.at[c]), other)

    def pass_copy(c):
        rows = packed.at[pl.ds(pl.multiple_of(core * PACK + c * piece, 16), piece)]
        return send(rows, rows, (pass_sem.at[0, c], pass_sem.at[1, c]), die_to)

    def grad_rows(first, rows):
        return grads.at[0, pl.ds(half + first, rows)]

    def master_rows(first, rows):
        return res.at[0, pl.ds(first, rows)]

    def near_copy(at, source):
        if at == 0:
            return pltpu.make_async_copy(source(0, PACK), near_rows, pack_sem.at[0])
        rows = half - PACK
        return send(source(PACK, rows), near_rows.at[pl.ds(0, rows)], (pack_sem.at[1], pack_sem.at[2]), die_to)

    def far_copy(at, source):
        if at == 1:
            return pltpu.make_async_copy(source(0, half), far_rows.at[pl.ds(half - PACK, half)], pack_sem.at[0])
        return send(source(0, PACK), far_rows.at[pl.ds(half, PACK)], (pack_sem.at[1], pack_sem.at[2]), die_to)

    def pack_rows(at):
        row = core * PACK + at + lax.broadcasted_iota(jnp.int32, (SUB, 128), 0)
        far = far_rows[pl.ds(half - first_rows + at, SUB), :]
        return jnp.where(row < first_rows, near_rows[pl.ds(pl.multiple_of(at, SUB), SUB), :], far)

    def short_copy(c):
        src = short_pack.at[pl.ds(pl.multiple_of(c * piece, 16), piece)]
        dst = short_packed.at[pl.ds(pl.multiple_of(core * PACK + c * piece, 16), piece)]
        return send(src, dst, (wts_send.at[c], wts_recv.at[c]), other)

    def short_place(c, at):
        return pl.ds(pl.multiple_of(at * PACK + c * piece, 16), piece)

    def short_pass(c, at):
        rows = short_place(c, at)
        return send(short_packed.at[rows], out_q.at[rows], (pass_sem.at[0, c], pass_sem.at[1, c]), die_to)

    def short_keep(c):
        rows = short_place(c, core)
        return pltpu.make_async_copy(short_packed.at[rows], out_q.at[rows], short_sem.at[c])

    def start_grads(first, last):
        for rep in (0, 1):

            @pl.when(r == rep)
            def _():
                @pl.loop(first, last)
                def _(c):
                    grad_copy(c, rep).start()

    def wts_copy(c):
        first = pl.multiple_of(c * size, 16)
        return pltpu.make_async_remote_copy(
            wts.at[pl.ds(first, size)],
            out_w.at[pl.ds(pl.multiple_of(r * half + first, 16), size)],
            wts_send.at[c],
            wts_recv.at[c],
            device_id=other,
            device_id_type=MESH,
        )

    def wts_arrival(c):
        first = pl.multiple_of(c * size, 16)
        return pltpu.make_async_remote_copy(
            wts.at[pl.ds(first, size)],
            out_w.at[pl.ds(pl.multiple_of((1 - r) * half + first, 16), size)],
            wts_send.at[c],
            wts_recv.at[c],
            device_id=other,
            device_id_type=MESH,
        )

    def own_copy(c):
        first = pl.multiple_of(c * size, 16)
        return pltpu.make_async_copy(
            wts.at[pl.ds(first, size)],
            out_w.at[pl.ds(pl.multiple_of(r * half + first, 16), size)],
            own_sem.at[c],
        )

    def res_copy(k, c):
        first = pl.multiple_of(c * size, 16)
        return pltpu.make_async_copy(
            res.at[k, pl.ds(first, size)], outs[k].at[pl.ds(first, size)], res_sem.at[k, c]
        )

    @pl.when(sends_head)
    def _():
        for k in range(3):
            load_stage(k).start()

    @pl.when((r == 0) & even)
    def _():
        near_copy(0, grad_rows).start()

    @pl.when((r == 0) & odd)
    def _():
        far_copy(1, grad_rows).start()

    barrier = pltpu.get_barrier_semaphore()
    pl.semaphore_signal(barrier, inc=1, device_id=other, device_id_type=MESH)

    pl.semaphore_signal(barrier, inc=1, device_id=die_to, device_id_type=MESH)

    @pl.when(gets_head & (x > 0))
    def _():
        pl.semaphore_signal(barrier, inc=1, device_id=head_from, device_id_type=MESH)

    @pl.when(head_unwraps)
    def _():
        for part in range(4):
            at = lax.rem(head_relays + 2 * part + count, count)
            pl.semaphore_signal(barrier, inc=1, device_id=(down_rep, at), device_id_type=MESH)

    @pl.when(gets_tail & (x < 3))
    def _():
        pl.semaphore_signal(barrier, inc=1, device_id=tail_from, device_id_type=MESH)

    @pl.when(tail_unwraps)
    def _():
        for part in range(4):
            at = lax.rem(tail_relays + 2 * part + count, count)
            pl.semaphore_signal(barrier, inc=1, device_id=(up_rep, at), device_id_type=MESH)

    @pl.when(relays_head)
    def _():
        pl.semaphore_signal(barrier, inc=1, device_id=(r, lax.rem(head_source + count, count)), device_id_type=MESH)

    @pl.when(relays_tail)
    def _():
        pl.semaphore_signal(barrier, inc=1, device_id=(r, lax.rem(tail_source, count)), device_id_type=MESH)

    targets = 2
    for cond, more in (
        (sends_head, 1),
        (head_wraps, 3),
        (sends_tail, 1),
        (tail_wraps, 3),
        (relays_head, 1),
        (relays_tail, 1),
    ):
        targets = targets + more * cond.astype(jnp.int32)
    pl.semaphore_wait(barrier, targets)

    early = EARLY

    @pl.when(r == 1)
    def _():
        @pl.loop(0, early)
        def _(c):
            grad_copy(c, 1).start()

    @pl.when((r == 0) & even)
    def _():
        near_copy(1, grad_rows).start()

    @pl.when((r == 0) & odd)
    def _():
        far_copy(0, grad_rows).start()

    for rep in (0, 1):

        @pl.when(tail_wraps & (down_rep == rep))
        def _():
            for part in (1, 2, 3):
                for k in range(3):
                    tail_relay_in(k, rep, part).start()

            @pl.when(z_lo == 0)
            def _():
                for k in range(3):
                    tail_relay_in(k, rep, 0).start()

            @pl.when(z_lo > 0)
            def _():
                for k in range(3):
                    tail_copy(k, rep, 0).start()

    for copy in offsets:
        copy.wait()

    pair = s - core
    first_rows = jnp.clip(new_off[pair + 1] - new_off[pair] - half, 0, half)

    @pl.when((r == 0) & even)
    def _():
        near_copy(0, grad_rows).wait()
        far_copy(0, grad_rows).wait_recv()

    @pl.when((r == 0) & odd)
    def _():
        far_copy(1, grad_rows).wait()
        near_copy(1, grad_rows).wait_recv()

    @pl.when(r == 0)
    def _():
        @pl.loop(0, PACK // SUB)
        def _(j):
            pack[pl.ds(pl.multiple_of(j * SUB, SUB), SUB), :] = pack_rows(j * SUB)

    prompt = jnp.where(odd & (z_lo == 3), PROMPT, CHUNKS)

    @pl.when(r == 0)
    def _():
        @pl.loop(0, prompt)
        def _(c):
            grad_copy(c, 0).start()

    @pl.when(sends_head)
    def _():
        begin = within(old_off[o + 1] - old_off[o] - (old_cap - stage_m.shape[0]) - EDGE)
        for k in range(3):
            load_stage(k).wait()

            @pl.loop(0, EDGE // SUB)
            def _(j):
                edge[k, pl.ds(pl.multiple_of(j * SUB, SUB), SUB), :] = stages[k][pl.ds(begin + j * SUB, SUB), :]

            @pl.when(x < 3)
            def _():
                head_copy(k).start()

            @pl.when(x == 3)
            def _():
                for part in range(4):
                    head_relay_in(k, part).start()

    for rep in (0, 1):

        @pl.when(sends_tail & (down_rep == rep) & (x > 0))
        def _():
            for k in range(3):
                tail_copy(k, rep).start()

    for rep in (0, 1):

        @pl.when(even & (r == rep))
        def _():
            for k in range(3):
                die_copy(k, rep).start()

    for rep in (0, 1):

        @pl.when(even & (r == rep))
        def _():
            for k in range(3):
                load_own(k, rep).start()

    my_grads.start()

    for part in range(4):

        @pl.when(relays_head & (x == part))
        def _():
            for k in range(3):
                head_relay_in(k, part).wait_recv()
                head_relay_out(k, part).start()

    for rep in (0, 1):
        for part in range(4):

            @pl.when(relays_tail & (tail_rep == rep) & (x == part))
            def _():
                for k in range(3):
                    tail_relay_in(k, rep, part).wait_recv()
                    tail_relay_out(k, rep, part).start()

    @pl.when(r == 0)
    def _():
        @pl.loop(prompt, CHUNKS)
        def _(c):
            grad_copy(c, 0).start()

    passes = jnp.where(even, CHUNKS, (half - PACK) // piece)
    arrivals = jnp.where(odd, CHUNKS, (half - PACK) // piece)

    @pl.when(r == 1)
    def _():
        @pl.loop(0, CHUNKS)
        def _(c):
            grad_copy(c, 0).wait_recv()

            @pl.when(c == 1)
            def _():
                @pl.loop(early, CHUNKS)
                def _(d):
                    grad_copy(d, 1).start()

            @pl.when(c < passes)
            def _():
                pass_copy(c).start()

    for rep in (0, 1):

        @pl.when(even & (r == rep))
        def _():
            for k in range(3):
                load_own(k, rep).wait()

        @pl.when(odd & (r == rep))
        def _():
            for k in range(3):
                die_copy(k, rep).wait_recv()

    @pl.when(gets_head & (x > 0))
    def _():
        for k in range(3):
            head_copy(k).wait_recv()

    @pl.when(head_unwraps)
    def _():
        for part in range(4):
            for k in range(3):
                head_copy(k, part).wait_recv()

    for rep in (0, 1):

        @pl.when(gets_tail & (r == rep) & (x < 3))
        def _():
            for k in range(3):
                tail_copy(k, rep).wait_recv()

        @pl.when(tail_unwraps & (r == rep))
        def _():
            for part in range(4):
                for k in range(3):
                    tail_copy(k, rep, part).wait_recv()

    my_grads.wait()

    start = within(new_off[s] - old_off[o] + EDGE - 2 * EDGE * core)
    edge_start = within(new_off[s] - old_off[o + 1] + 2 * half)
    split = jnp.where(even, new_off[s + 1], old_off[o + 1])
    flat = new_off[s] + r * half
    stop = new_off[s + 1]

    def update(c, their_rows):
        @pl.loop(0, size // SUB)
        def _(j):
            at = c * size + j * SUB
            rows = pl.ds(pl.multiple_of(at, SUB), SUB)
            row = flat + at + lax.broadcasted_iota(jnp.int32, (SUB, 128), 0)
            near = row < split
            keep = row < stop
            master, first, second = [
                jnp.where(near, main[k, pl.ds(start + at, SUB), :], alt[k, pl.ds(edge_start + at, SUB), :])
                for k in range(3)
            ]
            total = mine[rows, :] + their_rows(at)
            first_n = 0.9 * first + 0.1 * total
            second_n = 0.95 * second + 0.05 * total * total
            first_hat = first_n / (1.0 - 0.9**STEP)
            second_hat = second_n / (1.0 - 0.95**STEP)
            master_n = master - 0.02 * (first_hat / (jnp.sqrt(second_hat) + 1e-08) + 0.1 * master)
            master_n = jnp.where(keep, master_n, 0.0)
            res[0, rows, :] = master_n
            res[1, rows, :] = jnp.where(keep, first_n, 0.0)
            res[2, rows, :] = jnp.where(keep, second_n, 0.0)
            wts[rows, :] = master_n.astype(jnp.bfloat16)

        own_copy(c).start()
        for k in range(3):
            res_copy(k, c).start()

    @pl.when(r == 0)
    def _():
        @pl.loop(0, CHUNKS)
        def _(c):
            grad_copy(c, 1).wait_recv()
            update(c, lambda at: theirs[pl.ds(pl.multiple_of(at, SUB), SUB), :])
            wts_copy(c).start()

        @pl.loop(0, CHUNKS)
        def _(c):
            short_copy(c).wait_recv()
            short_keep(c).start()

            @pl.when(c < passes)
            def _():
                short_pass(c, core).start()


    @pl.when(r == 1)
    def _():
        @pl.loop(0, arrivals)
        def _(c):
            there = packed.at[pl.ds(pl.multiple_of((1 - core) * PACK + c * piece, 16), piece)]
            send(there, there, (pass_sem.at[0, c], pass_sem.at[1, c]), die_to).wait_recv()

        @pl.loop(0, CHUNKS)
        def _(c):
            update(c, lambda at: packed[pl.ds(core * first_rows + at, SUB), :])

            @pl.when((c == (PACK - 1) // size) & even)
            def _():
                near_copy(0, master_rows).start()

            @pl.when((c == (PACK - 1) // size) & odd)
            def _():
                far_copy(0, master_rows).start()

        @pl.when(even)
        def _():
            near_copy(1, master_rows).start()
            near_copy(0, master_rows).wait()
            far_copy(0, master_rows).wait_recv()

        @pl.when(odd)
        def _():
            far_copy(1, master_rows).start()
            far_copy(1, master_rows).wait()
            near_copy(1, master_rows).wait_recv()

        @pl.loop(0, CHUNKS)
        def _(c):
            @pl.loop(0, piece // SUB)
            def _(j):
                at = c * piece + j * SUB
                short_pack[pl.ds(pl.multiple_of(at, SUB), SUB), :] = pack_rows(at).astype(jnp.bfloat16)

            short_copy(c).start()


    for rep in (0, 1):

        @pl.when(even & (r == rep))
        def _():
            for k in range(3):
                die_copy(k, rep).wait_send()

    @pl.when(sends_head & (x < 3))
    def _():
        for k in range(3):
            head_copy(k).wait_send()

    @pl.when(head_wraps)
    def _():
        for part in range(4):
            for k in range(3):
                head_copy(k, part).wait_send()

    @pl.when(relays_head)
    def _():
        for k in range(3):
            head_relay_out(k, 0).wait_send()

    for rep in (0, 1):

        @pl.when(sends_tail & (down_rep == rep) & (x > 0))
        def _():
            for k in range(3):
                tail_copy(k, rep).wait_send()

        @pl.when(tail_wraps & (down_rep == rep))
        def _():
            for part in range(4):
                for k in range(3):
                    tail_copy(k, rep, part).wait_send()

        @pl.when(relays_tail & (tail_rep == rep))
        def _():
            for k in range(3):
                tail_relay_out(k, rep, 0).wait_send()

    @pl.when(even)
    def _():
        near_copy(1, grad_rows).wait_send()

    @pl.when(odd)
    def _():
        far_copy(0, grad_rows).wait_send()

    for rep in (0, 1):

        @pl.when(r == rep)
        def _():
            @pl.loop(0, CHUNKS)
            def _(c):
                grad_copy(c, rep).wait_send()
                own_copy(c).wait()
                for k in range(3):
                    res_copy(k, c).wait()

    @pl.when(r == 0)
    def _():
        @pl.loop(0, CHUNKS)
        def _(c):
            wts_copy(c).wait_send()
            short_keep(c).wait()

        @pl.loop(0, passes)
        def _(c):
            short_pass(c, core).wait_send()

        @pl.loop(0, arrivals)
        def _(c):
            short_pass(c, 1 - core).wait_recv()

    @pl.when(r == 1)
    def _():
        @pl.loop(0, passes)
        def _(c):
            pass_copy(c).wait_send()

        @pl.loop(0, CHUNKS)
        def _(c):
            short_copy(c).wait_send()
            wts_arrival(c).wait_recv()


def finish(
    off_in, in_m, in_f, in_s, in_w, in_q, out_m, out_f, out_s, out_w, off, vm, vf, vs, vw, vq, wide, in_sem, out_sem
):
    r = lax.axis_index("rep")
    s = lax.axis_index("shard")
    core = s % 2
    half = vm.shape[0]
    top, low = pl.ds(0, half), pl.ds(half, half)
    load_off = pltpu.make_async_copy(off_in, off, in_sem.at[0])
    load_q = pltpu.make_async_copy(in_q, vq, in_sem.at[1])
    pairs = [(in_m, vm, out_m), (in_f, vf, out_f), (in_s, vs, out_s), (in_w.at[top], vw.at[top], out_w.at[top])]
    loads = [pltpu.make_async_copy(src, hold, in_sem.at[2 + i]) for i, (src, hold, _) in enumerate(pairs)]
    stores = [pltpu.make_async_copy(hold, dst, out_sem.at[i]) for i, (_, hold, dst) in enumerate(pairs)]
    load_low = pltpu.make_async_copy(in_w.at[low], vw.at[low], in_sem.at[1])
    store_low = pltpu.make_async_copy(vw.at[low], out_w.at[low], out_sem.at[4])
    load_off.start()

    @pl.when(r == 0)
    def _():
        load_q.start()

    @pl.when(r == 1)
    def _():
        load_low.start()

    for load in loads:
        load.start()
    for load, store in zip(loads, stores):
        load.wait()
        store.start()
    load_off.wait()

    @pl.when(r == 0)
    def _():
        pair = s - core
        first_rows = jnp.clip(off[pair + 1] - off[pair] - half, 0, half)
        live = off[s + 1] - off[s] - half
        load_q.wait()

        @pl.loop(0, vq.shape[0] // SUB)
        def _(j):
            rows = pl.ds(pl.multiple_of(j * SUB, SUB), SUB)
            wide[rows, :] = vq[rows, :].astype(jnp.float32)

        @pl.loop(0, half // SUB)
        def _(j):
            row = j * SUB + lax.broadcasted_iota(jnp.int32, (SUB, 128), 0)
            mine = jnp.where(row < live, wide[pl.ds(core * first_rows + j * SUB, SUB), :], 0.0)
            vw[pl.ds(pl.multiple_of(half + j * SUB, SUB), SUB), :] = mine.astype(jnp.bfloat16)

    @pl.when(r == 1)
    def _():
        load_low.wait()

    store_low.start()
    for store in stores:
        store.wait()
    store_low.wait()


def local(old_master, old_first, old_second, grad_parts, old_offsets, new_offsets):
    new_cap, lanes = grad_parts.shape[1:]
    half = new_cap // 2
    hbm = pl.BlockSpec(memory_space=pltpu.HBM)
    free = pl.BlockSpec(memory_space=pl.ANY)
    state = jax.ShapeDtypeStruct((half, lanes), jnp.float32)
    dma = pltpu.SemaphoreType.DMA
    shapes = (state, state, state, jax.ShapeDtypeStruct((new_cap, lanes), jnp.bfloat16))
    short = jax.ShapeDtypeStruct((2 * PACK, lanes), jnp.bfloat16)
    results = pl.pallas_call(
        kernel,
        out_shape=shapes + (short,),
        in_specs=[hbm] * 6,
        out_specs=(free,) * 5,
        scratch_shapes=[
            pltpu.SMEM(old_offsets.shape, jnp.int32),
            pltpu.SMEM(new_offsets.shape, jnp.int32),
            pltpu.VMEM((3, WINDOW, lanes), jnp.float32),
            pltpu.VMEM((3, WINDOW, lanes), jnp.float32),
            pltpu.VMEM((2, 3, EDGE // 4, lanes), jnp.float32),
            pltpu.VMEM((3 * EDGE, lanes), jnp.float32),
            pltpu.VMEM((3 * EDGE, lanes), jnp.float32),
            pltpu.VMEM((3 * EDGE, lanes), jnp.float32),
            pltpu.VMEM((3, EDGE, lanes), jnp.float32),
            pltpu.VMEM((half, lanes), jnp.float32),
            pltpu.VMEM((half, lanes), jnp.float32),
            pltpu.VMEM((PACK, lanes), jnp.float32),
            pltpu.VMEM((half + PACK, lanes), jnp.float32),
            pltpu.VMEM((PACK, lanes), jnp.float32),
            pltpu.VMEM((2 * half, lanes), jnp.float32),
            pltpu.VMEM((PACK, lanes), jnp.bfloat16),
            pltpu.VMEM((2 * PACK, lanes), jnp.bfloat16),
            pltpu.VMEM((3, half, lanes), jnp.float32),
            pltpu.VMEM((half, lanes), jnp.bfloat16),
            dma((2,)),
            dma((3,)),
            dma,
            dma((3,)),
            dma((2, 3)),
            dma((2, 4, 3)),
            dma((2, 4, 3)),
            dma((2, 3)),
            dma((2, 3)),
            dma((3,)),
            dma((2, CHUNKS)),
            dma((CHUNKS,)),
            dma((CHUNKS,)),
            dma((CHUNKS,)),
            dma((CHUNKS,)),
            dma((3, CHUNKS)),
            dma((CHUNKS,)),
            dma((CHUNKS,)),
        ],
        compiler_params=pltpu.CompilerParams(
            collective_id=0, has_side_effects=True, vmem_limit_bytes=60 * 1024 * 1024
        ),
        name="move_and_update",
    )(old_offsets, new_offsets, old_master, old_first, old_second, grad_parts)
    master, first, second, weights = pl.pallas_call(
        finish,
        out_shape=shapes,
        in_specs=[hbm] * 6,
        out_specs=(hbm,) * 4,
        scratch_shapes=[pltpu.SMEM(new_offsets.shape, jnp.int32)]
        + [pltpu.VMEM(shape.shape, shape.dtype) for shape in shapes + (short,)]
        + [pltpu.VMEM((new_cap, lanes), jnp.float32), dma((6,)), dma((5,))],
        compiler_params=pltpu.CompilerParams(vmem_limit_bytes=60 * 1024 * 1024),
        name="finish",
    )(new_offsets, *results)
    return (master[None, None], first[None, None], second[None, None], weights)


def solution(mesh):
    in_specs = (
        P("shard", None),
        P("shard", None),
        P("shard", None),
        P("rep", "shard", None),
        P(),
        P(),
    )
    out_specs = (
        P("shard", "rep", None, None),
        P("shard", "rep", None, None),
        P("shard", "rep", None, None),
        P("shard", None),
    )
    return jax.shard_map(local, mesh=mesh, in_specs=in_specs, out_specs=out_specs, check_vma=False)
```
